32 devices in a mesh: dp: 8 (over z, x), ctx: 4 (over y, core).
Axes of the slice: x: 2, y: 2, z: 4, core: 2. Of those that a mesh axis runs over, the one named last changes fastest.
Arguments:
- tokens: bfloat16 [16, 1024, 1088], P('dp', 'ctx'), may hold values from -6 to 6
- positions: int32 [16, 1024], P('dp'), may hold values from 0 to 1023, as said below
- w_qkv: bfloat16 [3551232], P(('dp', 'ctx')), may hold values from -0.1875 to 0.1875
- w_out: bfloat16 [1183744], P(('dp', 'ctx')), may hold values from -0.75 to 0.75
- w_up: bfloat16 [4734976], P(('dp', 'ctx')), may hold values from -0.1875 to 0.1875
- w_down: bfloat16 [4734976], P(('dp', 'ctx')), may hold values from -0.09375 to 0.09375
- small_params: bfloat16 [13056], P(('dp', 'ctx')), may hold values from -1.2 to 1.6, as said below
- cotangent: bfloat16 [16, 1024, 1088], P('dp', 'ctx'), may hold values from -6 to 6
Outputs:
- result: bfloat16 [16, 1024, 1088], P('dp', 'ctx')
- grad_tokens: bfloat16 [16, 1024, 1088], P('dp', 'ctx')
- grad_qkv: float32 [3551232], P(('dp', 'ctx'))
- grad_out: float32 [1183744], P(('dp', 'ctx'))
- grad_up: float32 [4734976], P(('dp', 'ctx'))
- grad_down: float32 [4734976], P(('dp', 'ctx'))
- grad_small: float32 [13056], P(('dp', 'ctx'))
The draws below stay inside these ranges and needn't reach their ends.
Inputs may be any that keep to these rules, and one draw needn't show every extreme that they name: Each row is a permutation of 0 to 1023. Spans are runs of 128 positions; slot block c (slots c * 2 * 128 onward) holds, in rising order, span j and then span 2 * 4 - 1 - j, with j differing between blocks and sequences. `small_params`: gains near one and biases of either sign, in the layout of the argument.
All inputs are finite; a program needn't handle non-finite values.
Results may differ from the reference program's by a relative error of at most 0.013.
Values may be sent and summed in bfloat16 or wider, within the bound.
No kernel may reach another device: no remote copies, remote signals or barrier semaphores. Data moves between devices by JAX's collectives and lax.ppermute only.
A program may use at most 256 MiB of HBM per device.

```python
import jax
import jax.numpy as jnp
from jax import lax

D = 1088
HEADS = 17
HEAD_DIM = 64
FF = 4352
SEQ_LEN = 1024
SPAN = 128
NSEQ = 16


def draw_positions(key, part):
    key = jax.random.fold_in(key, 11)
    pair_count = SEQ_LEN // (2 * SPAN)
    row_keys = jax.random.split(key, NSEQ)
    ordering = jax.vmap(lambda row_key: jax.random.permutation(row_key, pair_count))(row_keys).astype(jnp.int32)
    offsets = jnp.arange(SPAN, dtype=jnp.int32)
    lower_half = ordering[:, :, None] * SPAN + offsets
    upper_half = (2 * pair_count - 1 - ordering)[:, :, None] * SPAN + offsets
    return jnp.concatenate([lower_half, upper_half], axis=2).reshape(NSEQ, SEQ_LEN).astype(jnp.int32)


def draw_small_params(key, part):
    key = jax.random.fold_in(key, 23)
    entry_count = 8 * D + FF
    normal_key, level_key = jax.random.split(key)
    gaussian = jax.random.normal(normal_key, (entry_count,), jnp.float32)
    levels = jax.random.uniform(level_key, (entry_count,), jnp.float32)
    places = jnp.arange(entry_count)
    is_gain = (places < D) | (places >= 5 * D) & (places < 6 * D)
    gain_values = 0.5 + levels
    biases = jnp.clip(0.3 * gaussian, -1.2, 1.2)
    return jnp.where(is_gain, gain_values, biases).astype(jnp.bfloat16)


def steps_of(own_key, extent, pieces, low, largest):
    def one(dim, parts):
        draws = jax.random.uniform(jax.random.fold_in(jax.random.fold_in(own_key, 6), dim), (parts,), jnp.float32, low / len(pieces), largest / len(pieces))
        return jnp.repeat(jnp.exp(draws), extent[dim] // parts).reshape((-1,) + (1,) * (len(extent) - dim - 1))

    factor_of = one(*pieces[0])
    for cut in pieces[1:]:
        factor_of = factor_of * one(*cut)
    return factor_of


def normal_values(key, shape, scale, bound, cuts=(), held_as=jnp.bfloat16):
    gain = steps_of(key, shape, cuts, -0.22, 0.18) if cuts else 1.0
    result = jax.random.normal(key, shape, jnp.float32) * scale * gain
    return jnp.minimum(jnp.maximum(result, -bound), bound).astype(held_as)


def setup_inputs(seed: int = 0) -> dict:
    streams_of = jax.random.split(jax.random.key(seed), 9)
    tokens = normal_values(streams_of[0], (NSEQ, SEQ_LEN, D), 1.0, 6.0, ((0, 8), (1, 4)))
    positions = draw_positions(jax.random.fold_in(streams_of[8], 71), 0)
    w_qkv = normal_values(streams_of[2], (3 * D * D,), D ** -0.5, 0.1875, ((0, 32),))
    w_out = normal_values(streams_of[3], (D * D,), (D // 16) ** -0.5, 0.75, ((0, 32),))
    w_up = normal_values(streams_of[4], (D * FF,), D ** -0.5, 0.1875, ((0, 32),))
    w_down = normal_values(streams_of[5], (FF * D,), FF ** -0.5, 0.09375, ((0, 32),))
    small_params = draw_small_params(jax.random.fold_in(streams_of[8], 71), 0)
    cotangent = normal_values(streams_of[7], (NSEQ, SEQ_LEN, D), 1.0, 6.0, ((0, 8), (1, 4)))
    return {"tokens": tokens, "positions": positions, "w_qkv": w_qkv, "w_out": w_out, "w_up": w_up, "w_down": w_down, "small_params": small_params, "cotangent": cotangent}


@jax.custom_vjp
def low(v):
    return lax.optimization_barrier(v.astype(jnp.bfloat16)).astype(jnp.float32)

@jax.custom_vjp
def low_back(v):
    return v

def low_keep(v):
    return (low(v), None)

def low_pass(kept, grad):
    return (grad,)

def back_keep(v):
    return (v, None)

def back_low(kept, grad):
    return (low(grad),)
low.defvjp(low_keep, low_pass)
low_back.defvjp(back_keep, back_low)

def normalize(values):
    center = values - lax.optimization_barrier(jnp.mean(values, axis=-1, keepdims=True))
    return center * lax.rsqrt(lax.optimization_barrier(jnp.mean(center * center, axis=-1, keepdims=True)) + 1e-05)

def reference(tokens, positions, w_qkv, w_out, w_up, w_down, small_params, cotangent):
    precise = lax.Precision.HIGHEST
    seq_total = tokens.shape[0]
    block_count = seq_total // 4
    factor = HEAD_DIM ** (-0.5)

    def forward(inputs_all, qkv_flat, out_flat, up_flat, down_flat, packed):
        qkv_mat = qkv_flat.reshape(D, 3 * D)
        out_mat = out_flat.reshape(D, D)
        up_mat = up_flat.reshape(D, FF)
        down_mat = down_flat.reshape(FF, D)
        gain_one, bias_one, bias_query, bias_value, bias_out, gain_two, bias_two = [packed[number * D:(number + 1) * D] for number in range(7)]
        up_bias = packed[7 * D:7 * D + FF]
        down_bias = packed[7 * D + FF:]
        qkv_bias = jnp.concatenate([bias_query, jnp.zeros_like(bias_query), bias_value])

        def block_fn(block_input):
            inputs_block, places = block_input
            flat_rows = inputs_block.reshape(-1, D)
            act_one = low(normalize(flat_rows) * gain_one + bias_one)
            qkv_rows = jnp.dot(act_one, qkv_mat, precision=precise) + qkv_bias
            qkv_rows = low_back(low(qkv_rows)).reshape(4, SEQ_LEN, 3, HEADS, HEAD_DIM)
            query = qkv_rows[:, :, 0]
            key_rows = qkv_rows[:, :, 1]
            value_rows = qkv_rows[:, :, 2]
            scores = jnp.einsum('bqhd,bkhd->bhqk', query, key_rows, precision=precise) * factor
            allowed = places[:, None, None, :] <= places[:, None, :, None]
            scores = low_back(jnp.where(allowed, scores, -1e+30))
            expo = jnp.exp(scores - lax.optimization_barrier(jnp.max(scores, axis=-1, keepdims=True)))
            probs = expo / lax.optimization_barrier(jnp.sum(expo, axis=-1, keepdims=True))
            mixed = jnp.einsum('bhqk,bkhd->bqhd', low(probs), value_rows, precision=precise).reshape(-1, D)
            mixed = low_back(low(mixed))
            attn_rows = low_back(jnp.dot(mixed, out_mat, precision=precise) + bias_out)
            resid = flat_rows + attn_rows
            act_two = low(normalize(resid) * gain_two + bias_two)
            pre_act = low_back(jnp.dot(act_two, up_mat, precision=precise) + up_bias)
            gelu_rows = low(jax.nn.gelu(pre_act, approximate=True))
            branch = low_back(jnp.dot(gelu_rows, down_mat, precision=precise) + down_bias)
            return (resid + branch).reshape(inputs_block.shape)
        mapped = lax.map(jax.checkpoint(block_fn), (inputs_all.reshape(block_count, 4, SEQ_LEN, D), positions.reshape(block_count, 4, SEQ_LEN)))
        return mapped.reshape(seq_total, SEQ_LEN, D)
    params = tuple((weight_array.astype(jnp.float32) for weight_array in (w_qkv, w_out, w_up, w_down, small_params)))
    outputs, pull_back = jax.vjp(forward, tokens.astype(jnp.float32), *params)
    gradients = pull_back(cotangent.astype(jnp.float32))
    return (outputs.astype(jnp.bfloat16), gradients[0].astype(jnp.bfloat16), gradients[1], gradients[2], gradients[3], gradients[4], gradients[5])
```

```python
import jax
import jax.numpy as jnp
from jax import lax
from jax.sharding import Mesh, PartitionSpec as P

HEADS = 17
HEAD_DIM = 64
FF = 4352
LANES = 8
SWAP = ((0, 1), (1, 0))
OWNERS = ("dp", "y")


def layer_stats(values):
    center = values - jnp.mean(values, axis=-1, keepdims=True)
    inverse = lax.rsqrt(jnp.mean(center * center, axis=-1, keepdims=True) + 1e-05)
    return (center * inverse, inverse)


def norm_back(upstream, normed, inverse, gain_vector):
    scaled = upstream * gain_vector
    return inverse * (
        scaled
        - jnp.mean(scaled, axis=-1, keepdims=True)
        - normed * jnp.mean(scaled * normed, axis=-1, keepdims=True)
    )


def lead_dot(left_side, right_side):
    return lax.dot_general(
        left_side, right_side, (((0,), (0,)), ((), ())), preferred_element_type=jnp.float32
    )


def tail_dot(left_side, right_side):
    return lax.dot_general(
        left_side, right_side, (((1,), (1,)), ((), ())), preferred_element_type=jnp.float32
    )


def smooth_gate(values):
    return jax.nn.gelu(values, approximate=True)


def pack_small(values, width):
    room = LANES * width - values.shape[-1]
    padded = jnp.pad(values, [(0, 0)] * (values.ndim - 1) + [(0, room)])
    return padded.reshape(values.shape[:-1] + (LANES, width))


def gather_packed(block, core):
    own = lax.all_gather(block, OWNERS, axis=0, tiled=True)
    other = lax.ppermute(own, "core", SWAP)
    even = jnp.where(core == 0, own, other)
    odd = jnp.where(core == 0, other, own)
    shape = (-1, 1, LANES, block.shape[1])
    return jnp.concatenate([even.reshape(shape), odd.reshape(shape)], axis=1)


def scatter_packed(packed, core):
    even, odd = packed[:, 0], packed[:, 1]
    keep = jnp.where(core == 0, even, odd)
    give = jnp.where(core == 0, odd, even)
    got = lax.ppermute(give, "core", SWAP)
    pair = (keep.astype(jnp.float32) + got.astype(jnp.float32)).astype(jnp.bfloat16)
    return lax.psum_scatter(pair, OWNERS, scatter_dimension=0, tiled=True)[0]


def local(tokens, positions, w_qkv, w_out, w_up, w_down, small_params, cotangent):
    seqs_here, local_len, model_width = tokens.shape
    seq_len = positions.shape[1]
    rows = seqs_here * local_len
    factor = HEAD_DIM ** (-0.5)
    y = lax.axis_index("y")
    core = lax.axis_index("core")
    pairs = lax.axis_size("dp") * 2
    small_len = small_params.shape[0]
    small_width = -(-small_len // LANES)
    qkv_width = w_qkv.shape[0] // LANES

    def trade(values):
        mine = lax.dynamic_index_in_dim(values, y, 0, keepdims=False)
        give = lax.dynamic_index_in_dim(values, 1 - y, 0, keepdims=False)
        return jnp.concatenate([mine, lax.ppermute(give, "y", SWAP)], axis=0)

    def trade_back(values):
        mine = values[:local_len]
        got = lax.ppermute(values[local_len:], "y", SWAP)
        first = jnp.where(y == 0, mine, got)
        second = jnp.where(y == 0, got, mine)
        return jnp.stack([first, second])

    first_block = jnp.concatenate(
        [w_qkv.reshape(LANES, qkv_width), pack_small(small_params, small_width)], axis=1
    )
    inputs = trade(tokens)
    qkv_small = gather_packed(first_block, core)
    out_mat = gather_packed(w_out.reshape(LANES, -1), core).reshape(model_width, model_width)
    up_mat = gather_packed(w_up.reshape(LANES, -1), core).reshape(model_width, FF)
    down_mat = gather_packed(w_down.reshape(LANES, -1), core).reshape(FF, model_width)
    grad_rows = trade(cotangent)

    qkv_mat = qkv_small[..., :qkv_width].reshape(model_width, 3 * model_width)
    packed = qkv_small[..., qkv_width:].reshape(2 * pairs, -1)[:, :small_len]
    packed = packed.reshape(-1).astype(jnp.float32)
    pieces = [packed[number * model_width : (number + 1) * model_width] for number in range(7)]
    gain_one, bias_one, bias_query, bias_value, bias_out, gain_two, bias_two = pieces
    up_bias = packed[7 * model_width : 7 * model_width + FF]
    down_bias = packed[7 * model_width + FF :]

    place_row = lax.dynamic_index_in_dim(positions, y, 0, keepdims=False)

    def places_of(core_index):
        near = lax.dynamic_slice_in_dim(place_row, (2 * y + core_index) * local_len, local_len)
        far = lax.dynamic_slice_in_dim(place_row, (2 - 2 * y + core_index) * local_len, local_len)
        return jnp.concatenate([near, far])

    places = places_of(core)
    key_places = jnp.concatenate([places, places_of(1 - core)])
    allowed = (key_places[None, :] <= places[:, None])[None]

    inputs = inputs.astype(jnp.float32)
    normed_one, inverse_one = layer_stats(inputs)
    act_one = (normed_one * gain_one + bias_one).astype(jnp.bfloat16)
    qkv_bias = jnp.concatenate([bias_query, jnp.zeros_like(bias_query), bias_value])
    qkv_rows = (jnp.dot(act_one, qkv_mat, preferred_element_type=jnp.float32) + qkv_bias).astype(
        jnp.bfloat16
    )
    kv_all = jnp.concatenate(
        [qkv_rows[:, model_width:], lax.ppermute(qkv_rows[:, model_width:], "core", SWAP)], axis=0
    )
    query = qkv_rows[:, :model_width].reshape(rows, HEADS, HEAD_DIM)
    keys = kv_all[:, :model_width].reshape(seq_len, HEADS, HEAD_DIM)
    vals = kv_all[:, model_width:].reshape(seq_len, HEADS, HEAD_DIM)

    def masked_scores():
        scores = jnp.einsum("qhd,khd->hqk", query, keys, preferred_element_type=jnp.float32)
        return jnp.where(allowed, scores * factor, -1e30)

    scores = masked_scores()
    top_score = jnp.max(scores, axis=-1, keepdims=True)
    expo = jnp.exp(scores - top_score)
    denom = jnp.sum(expo, axis=-1, keepdims=True)
    probs = expo / denom
    log_total = top_score + jnp.log(denom)
    mixed = jnp.einsum(
        "hqk,khd->qhd", probs.astype(jnp.bfloat16), vals, preferred_element_type=jnp.float32
    )
    mixed = mixed.astype(jnp.bfloat16).reshape(rows, model_width)
    resid = inputs + jnp.dot(mixed, out_mat, preferred_element_type=jnp.float32) + bias_out
    normed_two, inverse_two = layer_stats(resid)
    act_two = (normed_two * gain_two + bias_two).astype(jnp.bfloat16)
    pre_act = jnp.dot(act_two, up_mat, preferred_element_type=jnp.float32) + up_bias
    gelu_rows = smooth_gate(pre_act).astype(jnp.bfloat16)
    outputs = resid + jnp.dot(gelu_rows, down_mat, preferred_element_type=jnp.float32) + down_bias
    result = trade_back(outputs.astype(jnp.bfloat16))

    def send_sum(grad, extra=None):
        grad = grad.astype(jnp.bfloat16).reshape(pairs, 2, LANES, -1)
        if extra is not None:
            grad = jnp.concatenate([grad, extra], axis=-1)
        return scatter_packed(grad, core)

    grad_float = grad_rows.astype(jnp.float32)
    sum_down = send_sum(lead_dot(gelu_rows, grad_rows))
    down_bias_term = jnp.sum(grad_float, axis=0)
    grad_gelu = tail_dot(grad_rows, down_mat)
    gelu_pull = jax.vjp(smooth_gate, pre_act)[1]
    grad_pre = gelu_pull(grad_gelu)[0].astype(jnp.bfloat16)
    sum_up = send_sum(lead_dot(act_two, grad_pre))
    up_bias_term = jnp.sum(grad_pre.astype(jnp.float32), axis=0)
    grad_act_two = tail_dot(grad_pre, up_mat)
    gain_two_term = jnp.sum(grad_act_two * normed_two, axis=0)
    bias_two_term = jnp.sum(grad_act_two, axis=0)
    grad_resid = grad_float + norm_back(grad_act_two, normed_two, inverse_two, gain_two)
    grad_attn = grad_resid.astype(jnp.bfloat16)
    sum_out = send_sum(lead_dot(mixed, grad_attn))
    bias_out_term = jnp.sum(grad_attn.astype(jnp.float32), axis=0)
    grad_mixed = tail_dot(grad_attn, out_mat).astype(jnp.bfloat16)
    grad_mixed = grad_mixed.reshape(rows, HEADS, HEAD_DIM)
    probs_again = jnp.exp(masked_scores() - log_total)
    grad_probs = jnp.einsum("qhd,khd->hqk", grad_mixed, vals, preferred_element_type=jnp.float32)
    grad_scores = probs_again * (
        grad_probs - jnp.sum(grad_probs * probs_again, axis=-1, keepdims=True)
    )
    grad_scores = grad_scores.astype(jnp.bfloat16)
    grad_query = (
        jnp.einsum("hqk,khd->qhd", grad_scores, keys, preferred_element_type=jnp.float32) * factor
    )
    key_terms = (
        jnp.einsum("hqk,qhd->khd", grad_scores, query, preferred_element_type=jnp.float32) * factor
    )
    value_terms = jnp.einsum(
        "hqk,qhd->khd",
        probs_again.astype(jnp.bfloat16),
        grad_mixed,
        preferred_element_type=jnp.float32,
    )
    kv_terms = jnp.concatenate(
        [key_terms.reshape(seq_len, model_width), value_terms.reshape(seq_len, model_width)], axis=1
    )
    kv_got = lax.ppermute(kv_terms[rows:].astype(jnp.bfloat16), "core", SWAP)
    grad_kv = kv_terms[:rows] + kv_got.astype(jnp.float32)
    grad_qkv_rows = jnp.concatenate(
        [grad_query.reshape(rows, model_width), grad_kv], axis=1
    ).astype(jnp.bfloat16)
    qkv_sums = jnp.sum(grad_qkv_rows.astype(jnp.float32), axis=0)
    grad_act_one = tail_dot(grad_qkv_rows, qkv_mat)
    gain_one_term = jnp.sum(grad_act_one * normed_one, axis=0)
    bias_one_term = jnp.sum(grad_act_one, axis=0)
    small_grad = jnp.concatenate(
        [
            gain_one_term,
            bias_one_term,
            qkv_sums[:model_width],
            qkv_sums[2 * model_width :],
            bias_out_term,
            gain_two_term,
            bias_two_term,
            up_bias_term,
            down_bias_term,
        ]
    ).astype(jnp.bfloat16)
    small_grad = pack_small(small_grad.reshape(pairs, 2, small_len), small_width)
    sum_qkv = send_sum(lead_dot(act_one, grad_qkv_rows), small_grad)
    grad_input = grad_resid + norm_back(grad_act_one, normed_one, inverse_one, gain_one)
    grad_tokens = trade_back(grad_input.astype(jnp.bfloat16))
    grad_qkv = sum_qkv[:, :qkv_width].astype(jnp.float32).reshape(-1)
    grad_small = sum_qkv[:, qkv_width:].astype(jnp.float32).reshape(-1)[:small_len]
    grad_out, grad_up, grad_down = [
        piece.astype(jnp.float32).reshape(-1) for piece in (sum_out, sum_up, sum_down)
    ]
    return (result, grad_tokens, grad_qkv, grad_out, grad_up, grad_down, grad_small)


def solution(mesh):
    groups, owners = mesh.shape["dp"], mesh.shape["ctx"]
    fine = Mesh(mesh.devices.reshape(groups, owners // 2, 2), ("dp", "y", "core"))
    rows = P("dp", ("y", "core"), None)
    flat = P(("dp", "y", "core"))
    return jax.shard_map(
        local,
        mesh=fine,
        in_specs=(rows, P("dp", None), flat, flat, flat, flat, flat, rows),
        out_specs=(rows, rows, flat, flat, flat, flat, flat),
        check_vma=False,
    )
```

```python
import jax
import jax.numpy as jnp
from jax import lax
from jax.experimental import pallas as pl
from jax.experimental.pallas import tpu as pltpu
from jax.sharding import Mesh, PartitionSpec as P

HEADS = 17
HEAD_DIM = 64
FF = 4352
LANES = 8
SWAP = ((0, 1), (1, 0))
OWNERS = ("dp", "y")


def layer_stats(values):
    center = values - jnp.mean(values, axis=-1, keepdims=True)
    inverse = lax.rsqrt(jnp.mean(center * center, axis=-1, keepdims=True) + 1e-05)
    return (center * inverse, inverse)


def norm_back(upstream, normed, inverse, gain_vector):
    scaled = upstream * gain_vector
    return inverse * (
        scaled
        - jnp.mean(scaled, axis=-1, keepdims=True)
        - normed * jnp.mean(scaled * normed, axis=-1, keepdims=True)
    )


def lead_dot(left_side, right_side):
    return lax.dot_general(
        left_side, right_side, (((0,), (0,)), ((), ())), preferred_element_type=jnp.float32
    )


def tail_dot(left_side, right_side):
    return lax.dot_general(
        left_side, right_side, (((1,), (1,)), ((), ())), preferred_element_type=jnp.float32
    )


def smooth_gate(values):
    return jax.nn.gelu(values, approximate=True)


def pack_small(values, width):
    room = LANES * width - values.shape[-1]
    padded = jnp.pad(values, [(0, 0)] * (values.ndim - 1) + [(0, room)])
    return padded.reshape(values.shape[:-1] + (LANES, width))


def gather_packed(block, core):
    own = lax.all_gather(block, OWNERS, axis=0, tiled=True)
    other = lax.ppermute(own, "core", SWAP)
    even = jnp.where(core == 0, own, other)
    odd = jnp.where(core == 0, other, own)
    shape = (-1, 1, LANES, block.shape[1])
    return jnp.concatenate([even.reshape(shape), odd.reshape(shape)], axis=1)


def scatter_packed(packed, core):
    even, odd = packed[:, 0], packed[:, 1]
    keep = jnp.where(core == 0, even, odd)
    give = jnp.where(core == 0, odd, even)
    got = lax.ppermute(give, "core", SWAP)
    pair = (keep.astype(jnp.float32) + got.astype(jnp.float32)).astype(jnp.bfloat16)
    return lax.psum_scatter(pair, OWNERS, scatter_dimension=0, tiled=True)[0]


def dot_rows(left, right):
    return lax.dot_general(
        left, right, (((1,), (0,)), ((), ())), preferred_element_type=jnp.float32
    )


def bias_of(key_places, query_places):
    return jnp.where(key_places <= query_places, 0.0, -1e30).astype(jnp.float32)


def per_pair(one_pair):
    wide = 2 * HEAD_DIM
    full = HEADS // 2

    def step(number, carry):
        one_pair(pl.ds(pl.multiple_of(number * wide, wide), wide), 2 * number, 2)
        return carry

    lax.fori_loop(0, full, step, 0)
    if HEADS % 2:
        one_pair(pl.ds(full * wide, HEAD_DIM), 2 * full, 1)


def only_head(values, number, heads):
    if heads == 1:
        return values
    lane = lax.broadcasted_iota(jnp.int32, values.shape, 1)
    inside = lane < HEAD_DIM if number == 0 else lane >= HEAD_DIM
    return jnp.where(inside, values, jnp.zeros_like(values))


def join_heads(parts):
    if len(parts) == 1:
        return parts[0]
    lane = lax.broadcasted_iota(jnp.int32, parts[0].shape, 1)
    return jnp.where(lane < HEAD_DIM, parts[0], parts[1])


def attend_kernel(
    q_ref, own_ref, other_ref, query_ref, key_ref, mixed_ref, log_ref, low_bias, up_bias
):
    half = q_ref.shape[0] // 2
    low_bias[...] = bias_of(key_ref[: 2 * half], query_ref[:, :half])
    up_bias[...] = bias_of(key_ref[2 * half :], query_ref[:, half:])

    def one_pair(lanes, first, heads):
        q = q_ref[:, lanes] * jnp.asarray(HEAD_DIM**-0.5, jnp.bfloat16)
        k_low = jnp.concatenate([own_ref[0, :half, lanes], other_ref[0, :half, lanes]], axis=0)
        k_up = jnp.concatenate([own_ref[0, half:, lanes], other_ref[0, half:, lanes]], axis=0)
        v_low = jnp.concatenate([own_ref[1, :half, lanes], other_ref[1, :half, lanes]], axis=0).T
        v_up = jnp.concatenate([own_ref[1, half:, lanes], other_ref[1, half:, lanes]], axis=0).T
        low_parts, up_parts = [], []
        for number in range(heads):
            rows = slice(number * HEAD_DIM, (number + 1) * HEAD_DIM)
            q_head = only_head(q, number, heads)
            s = tail_dot(k_low, q_head[:half]) + low_bias[...]
            top = jnp.max(s, axis=0, keepdims=True)
            e = jnp.exp(s - top)
            total = jnp.sum(e, axis=0, keepdims=True)
            mixed = dot_rows(v_low[rows], e.astype(jnp.bfloat16)) / total
            low_parts.append(mixed)
            log_ref[pl.ds(first + number, 1), :half] = top + jnp.log(total)
            s_low = tail_dot(k_low, q_head[half:])
            s_up = tail_dot(k_up, q_head[half:]) + up_bias[...]
            top = jnp.maximum(
                jnp.max(s_low, axis=0, keepdims=True), jnp.max(s_up, axis=0, keepdims=True)
            )
            e_low = jnp.exp(s_low - top)
            e_up = jnp.exp(s_up - top)
            total = jnp.sum(e_low, axis=0, keepdims=True) + jnp.sum(e_up, axis=0, keepdims=True)
            mixed = dot_rows(v_low[rows], e_low.astype(jnp.bfloat16))
            mixed = mixed + dot_rows(v_up[rows], e_up.astype(jnp.bfloat16))
            up_parts.append(mixed / total)
            log_ref[pl.ds(first + number, 1), half:] = top + jnp.log(total)
        mixed_ref[:half, lanes] = jnp.concatenate(low_parts, axis=0).T.astype(jnp.bfloat16)
        mixed_ref[half:, lanes] = jnp.concatenate(up_parts, axis=0).T.astype(jnp.bfloat16)

    per_pair(one_pair)


def attend_back_kernel(
    q_ref,
    own_ref,
    other_ref,
    query_ref,
    key_ref,
    mixed_ref,
    log_ref,
    grad_ref,
    dq_ref,
    own_out,
    other_out,
    low_bias,
    up_bias,
):
    half = q_ref.shape[0] // 2
    factor = HEAD_DIM**-0.5
    low_bias[...] = bias_of(key_ref[: 2 * half], query_ref[:, :half])
    up_bias[...] = bias_of(key_ref[2 * half :], query_ref[:, half:])

    def one_pair(lanes, first, heads):
        q = q_ref[:, lanes] * jnp.asarray(factor, jnp.bfloat16)
        grad = grad_ref[:, lanes]
        product = (grad.astype(jnp.float32) * mixed_ref[:, lanes].astype(jnp.float32)).T
        q_heads = [only_head(q, number, heads) for number in range(heads)]
        grad_heads = [only_head(grad, number, heads) for number in range(heads)]
        deltas = [
            jnp.sum(product[number * HEAD_DIM : (number + 1) * HEAD_DIM], axis=0, keepdims=True)
            for number in range(heads)
        ]
        logs = [log_ref[pl.ds(first + number, 1), :] for number in range(heads)]
        dq_low = [None] * heads
        dq_up = [None] * heads
        for source, out, place in ((own_ref, own_out, 0), (other_ref, other_out, 1)):
            bias_rows = slice(place * half, (place + 1) * half)
            for upper in (False, True):
                rows = slice(half, None) if upper else slice(0, half)
                k = source[0, rows, lanes]
                v = source[1, rows, lanes]
                k_turned = k.T
                dk_parts, dv_parts = [], []
                for number in range(heads):
                    head_rows = slice(number * HEAD_DIM, (number + 1) * HEAD_DIM)
                    first_query = half if upper else 0
                    q_head = q_heads[number][first_query:]
                    grad_head = grad_heads[number][first_query:]
                    s = tail_dot(k, q_head)
                    if upper:
                        s = s + up_bias[bias_rows]
                    else:
                        s = jnp.concatenate([s[:, :half] + low_bias[bias_rows], s[:, half:]], axis=1)
                    p = jnp.exp(s - logs[number][:, first_query:])
                    dp = tail_dot(v, grad_head)
                    ds = (p * (dp - deltas[number][:, first_query:])).astype(jnp.bfloat16)
                    dv_parts.append(dot_rows(p.astype(jnp.bfloat16), grad[first_query:]))
                    dk_parts.append(dot_rows(ds, q[first_query:]))
                    turned = dot_rows(k_turned[head_rows], ds)
                    low = None if upper else turned[:, :half]
                    up = turned if upper else turned[:, half:]
                    if low is not None:
                        dq_low[number] = low if dq_low[number] is None else dq_low[number] + low
                    dq_up[number] = up if dq_up[number] is None else dq_up[number] + up
                out[0, rows, lanes] = join_heads(dk_parts).astype(jnp.bfloat16)
                out[1, rows, lanes] = join_heads(dv_parts).astype(jnp.bfloat16)
        dq_ref[:half, lanes] = (jnp.concatenate(dq_low, axis=0).T * factor).astype(jnp.bfloat16)
        dq_ref[half:, lanes] = (jnp.concatenate(dq_up, axis=0).T * factor).astype(jnp.bfloat16)

    per_pair(one_pair)


def kernel_call(body, outs, half, cost):
    return pl.pallas_call(
        body,
        out_shape=outs,
        scratch_shapes=[pltpu.VMEM((2 * half, half), jnp.float32)] * 2,
        compiler_params=pltpu.CompilerParams(vmem_limit_bytes=48 * 1024 * 1024),
        cost_estimate=pl.CostEstimate(flops=cost, bytes_accessed=12 << 20, transcendentals=cost // 256),
    )


def attend(query, own, other, query_places, key_places):
    rows, width = query.shape
    outs = (
        jax.ShapeDtypeStruct((rows, width), jnp.bfloat16),
        jax.ShapeDtypeStruct((HEADS, rows), jnp.float32),
    )
    call = kernel_call(attend_kernel, outs, rows // 2, 8 << 30)
    return call(query, own, other, query_places, key_places)


def attend_back(query, own, other, query_places, key_places, mixed, logs, grad):
    rows, width = query.shape
    outs = (
        jax.ShapeDtypeStruct((rows, width), jnp.bfloat16),
        jax.ShapeDtypeStruct(own.shape, jnp.bfloat16),
        jax.ShapeDtypeStruct(own.shape, jnp.bfloat16),
    )
    call = kernel_call(attend_back_kernel, outs, rows // 2, 24 << 30)
    return call(query, own, other, query_places, key_places, mixed, logs, grad)


ALL = ("dp", "y", "core")


def round_low(values):
    return values.astype(jnp.bfloat16)


def one_hot_columns(targets, width):
    line = lax.broadcasted_iota(jnp.int32, (width, targets.shape[0]), 0)
    return (line == targets[None, :]).astype(jnp.bfloat16)


def swap_with(values, axis, bit):
    count = lax.axis_size(axis)
    return lax.ppermute(values, axis, [(here, here ^ (1 << bit)) for here in range(count)])


def near_owners(order, dp_bits, each):
    owner = (lax.axis_index("dp") * 2 + lax.axis_index("y")) * 2 + lax.axis_index("core")
    bits = dp_bits + 2
    column = jnp.arange(each << bits, dtype=jnp.int32)
    place, inner = column // each, column % each
    far = jnp.zeros_like(place)
    for number, (axis, bit) in enumerate(order):
        weight = {"core": 0, "y": 1, "dp": 2 + bit}[axis]
        far = far + (((place >> (bits - 1 - number)) & 1) << weight)
    return (owner ^ far) * each + inner


def halve_first(left, right, order):
    half = left.shape[1] // 2
    give = round_low(lead_dot(left[:, half:], right))
    got = swap_with(give, *order[0])
    return round_low(lead_dot(left[:, :half], right) + got.astype(jnp.float32))


def halve(values, axis, bit):
    half = values.shape[0] // 2
    got = swap_with(values[half:], axis, bit)
    return round_low(values[:half].astype(jnp.float32) + got.astype(jnp.float32))


def local(tokens, positions, w_qkv, w_out, w_up, w_down, small_params, cotangent):
    seqs_here, local_len, model_width = tokens.shape
    span = local_len // 2
    rows = seqs_here * local_len
    half = rows // 2
    y = lax.axis_index("y")
    core = lax.axis_index("core")
    groups = lax.axis_size("dp")
    owners = groups * 4
    small_len = small_params.shape[0]
    whole_rows = model_width % owners == 0
    each = model_width // owners
    dp_bits = groups.bit_length() - 1

    def trade(values):
        mine = lax.dynamic_index_in_dim(values, y, 0, keepdims=False)
        give = lax.dynamic_index_in_dim(values, 1 - y, 0, keepdims=False)
        got = lax.ppermute(give, "y", SWAP)
        return jnp.concatenate([mine[:span], got[:span], mine[span:], got[span:]], axis=0)

    def trade_back(values):
        mine = jnp.concatenate([values[:span], values[half : half + span]], axis=0)
        give = jnp.concatenate([values[span:half], values[half + span :]], axis=0)
        got = lax.ppermute(give, "y", SWAP)
        first = jnp.where(y == 0, mine, got)
        second = jnp.where(y == 0, got, mine)
        return jnp.stack([first, second])

    inputs = trade(tokens)
    if whole_rows:
        blocks = jnp.concatenate(
            [w_qkv.reshape(each, 3 * model_width), w_out.reshape(each, model_width)], axis=1
        )
        room = -(each + 1) % 8
        held = each + 1 + room
        extra = jnp.pad(small_params.reshape(1, -1), [(0, room), (0, FF - small_len)])
        extra = extra.reshape(1 + room, FF)
        blocks = jnp.concatenate([blocks, extra], axis=0)
        up_block = jnp.pad(w_up.reshape(each, FF), [(0, held - each), (0, 0)])
        blocks = lax.all_gather(blocks, ALL, axis=0, tiled=True)
        up_mat = lax.all_gather(up_block, ALL, axis=0, tiled=True)
        down_mat = lax.all_gather(w_down.reshape(-1, model_width), ALL, axis=0, tiled=True)
        qkv_mat = blocks[:, : 3 * model_width]
        out_mat = blocks[:, 3 * model_width :]
        packed = blocks.reshape(owners, held, FF)[:, each, :small_len].reshape(-1)
        column = jnp.arange(owners * held, dtype=jnp.int32)
        inside = column % held
        spread = jnp.where(inside < each, column // held * each + inside, -1)
        spread = one_hot_columns(spread, model_width)

        def widen(values):
            return round_low(dot_rows(values, spread))

        def narrow(values):
            return tail_dot(round_low(values), spread)

    else:
        small_width = -(-small_len // LANES)
        qkv_width = w_qkv.shape[0] // LANES
        blocks = jnp.concatenate(
            [w_qkv.reshape(LANES, qkv_width), pack_small(small_params, small_width)], axis=1
        )
        blocks = gather_packed(blocks, core)
        qkv_mat = blocks[..., :qkv_width].reshape(model_width, 3 * model_width)
        packed = blocks[..., qkv_width:].reshape(owners, -1)[:, :small_len].reshape(-1)
        out_mat = gather_packed(w_out.reshape(LANES, -1), core).reshape(model_width, model_width)
        up_mat = gather_packed(w_up.reshape(LANES, -1), core).reshape(model_width, FF)
        down_mat = gather_packed(w_down.reshape(LANES, -1), core).reshape(FF, model_width)

        def widen(values):
            return values

        def narrow(values):
            return values

    grad_rows = trade(cotangent)
    packed = packed.astype(jnp.float32)
    pieces = [packed[number * model_width : (number + 1) * model_width] for number in range(7)]
    gain_one, bias_one, bias_query, bias_value, bias_out, gain_two, bias_two = pieces
    up_bias = packed[7 * model_width : 7 * model_width + FF]
    down_bias = packed[7 * model_width + FF :]

    place_row = lax.dynamic_index_in_dim(positions, y, 0, keepdims=False)

    def places_of(core_index):
        near = lax.dynamic_slice_in_dim(place_row, (2 * y + core_index) * local_len, local_len)
        far = lax.dynamic_slice_in_dim(place_row, (2 - 2 * y + core_index) * local_len, local_len)
        return jnp.concatenate([near[:span], far[:span]]), jnp.concatenate([near[span:], far[span:]])

    own_low, own_up = places_of(core)
    other_low, other_up = places_of(1 - core)
    query_places = jnp.concatenate([own_low, own_up])[None, :]
    key_places = jnp.concatenate([own_low, other_low, own_up, other_up])[:, None]

    inputs = inputs.astype(jnp.float32)
    normed_one, inverse_one = layer_stats(inputs)
    act_one = round_low(normed_one * gain_one + bias_one)
    qkv_bias = jnp.concatenate([bias_query, jnp.zeros_like(bias_query), bias_value])
    qkv_rows = round_low(dot_rows(widen(act_one), qkv_mat) + qkv_bias)
    query = qkv_rows[:, :model_width]
    own_kv = jnp.stack([qkv_rows[:, model_width : 2 * model_width], qkv_rows[:, 2 * model_width :]])
    other_kv = lax.ppermute(own_kv, "core", SWAP)
    mixed, logs = attend(query, own_kv, other_kv, query_places, key_places)
    resid = inputs + dot_rows(widen(mixed), out_mat) + bias_out
    normed_two, inverse_two = layer_stats(resid)
    act_two = round_low(normed_two * gain_two + bias_two)
    pre_act = dot_rows(widen(act_two), up_mat) + up_bias
    gelu_rows = round_low(smooth_gate(pre_act))
    outputs = resid + dot_rows(gelu_rows, down_mat) + down_bias
    result = trade_back(round_low(outputs))

    if whole_rows:
        steps = [("dp", bit) for bit in range(dp_bits)]
        order_a = [("core", 0), steps[0], ("y", 0)] + steps[1:]
        order_b = [("core", 0), ("y", 0), steps[0]] + steps[1:]
        turn_a = one_hot_columns(near_owners(order_a, dp_bits, each), model_width)
        turn_b = one_hot_columns(near_owners(order_b, dp_bits, each), model_width)

        def send_sum(left, right, extra=None):
            cut = (right.shape[1] // 256) * 128
            left_a = round_low(dot_rows(left, turn_a))
            left_b = round_low(dot_rows(left, turn_b))
            part_a = halve_first(left_a, right[:, :cut], order_a)
            part_b = halve_first(left_b, right[:, cut:], order_b)
            if extra is not None:
                extra = extra.reshape(model_width, -1)
                extra = round_low(lead_dot(turn_b, extra))
                part_b = jnp.concatenate([part_b, halve(extra, *order_b[0])], axis=1)
            for step_a, step_b in zip(order_a[1:3], order_b[1:3]):
                part_a, part_b = halve(part_a, *step_a), halve(part_b, *step_b)
            part = jnp.concatenate([part_a, part_b], axis=1)
            for step in order_a[3:]:
                part = halve(part, *step)
            return part

    else:

        def send_sum(left, right, extra=None):
            grad = round_low(lead_dot(left, right)).reshape(groups * 2, 2, LANES, -1)
            if extra is not None:
                extra = extra.reshape(groups * 2, 2, small_len)
                grad = jnp.concatenate([grad, pack_small(extra, small_width)], axis=-1)
            return scatter_packed(grad, core)

    grad_float = grad_rows.astype(jnp.float32)
    sum_down = round_low(lead_dot(gelu_rows, grad_rows)).reshape(owners, -1, model_width)
    sum_down = lax.psum_scatter(sum_down, ALL, scatter_dimension=0, tiled=True)
    down_bias_term = jnp.sum(grad_float, axis=0)
    grad_gelu = tail_dot(grad_rows, down_mat)
    gelu_pull = jax.vjp(smooth_gate, pre_act)[1]
    grad_pre = round_low(gelu_pull(grad_gelu)[0])
    sum_up = send_sum(act_two, grad_pre)
    up_bias_term = jnp.sum(grad_pre.astype(jnp.float32), axis=0)
    grad_act_two = narrow(tail_dot(grad_pre, up_mat))
    gain_two_term = jnp.sum(grad_act_two * normed_two, axis=0)
    bias_two_term = jnp.sum(grad_act_two, axis=0)
    grad_resid = grad_float + norm_back(grad_act_two, normed_two, inverse_two, gain_two)
    grad_attn = round_low(grad_resid)
    sum_out = send_sum(mixed, grad_attn)
    bias_out_term = jnp.sum(grad_attn.astype(jnp.float32), axis=0)
    grad_mixed = round_low(narrow(tail_dot(grad_attn, out_mat)))
    grad_query, grad_own, grad_other = attend_back(
        query, own_kv, other_kv, query_places, key_places, mixed, logs, grad_mixed
    )
    grad_got = lax.ppermute(grad_other, "core", SWAP)
    grad_kv = round_low(grad_own.astype(jnp.float32) + grad_got.astype(jnp.float32))
    grad_qkv_rows = jnp.concatenate([grad_query, grad_kv[0], grad_kv[1]], axis=1)
    qkv_sums = jnp.sum(grad_qkv_rows.astype(jnp.float32), axis=0)
    grad_act_one = narrow(tail_dot(grad_qkv_rows, qkv_mat))
    gain_one_term = jnp.sum(grad_act_one * normed_one, axis=0)
    bias_one_term = jnp.sum(grad_act_one, axis=0)
    small_grad = jnp.concatenate(
        [
            gain_one_term,
            bias_one_term,
            qkv_sums[:model_width],
            qkv_sums[2 * model_width :],
            bias_out_term,
            gain_two_term,
            bias_two_term,
            up_bias_term,
            down_bias_term,
        ]
    )
    sum_qkv = send_sum(act_one, grad_qkv_rows, round_low(small_grad))
    grad_input = grad_resid + norm_back(grad_act_one, normed_one, inverse_one, gain_one)
    grad_tokens = trade_back(round_low(grad_input))
    main = w_qkv.shape[0] // sum_qkv.shape[0]
    grad_qkv = sum_qkv[:, :main].astype(jnp.float32).reshape(-1)
    grad_small = sum_qkv[:, main:].astype(jnp.float32).reshape(-1)[:small_len]
    grad_out, grad_up, grad_down = [
        piece.astype(jnp.float32).reshape(-1) for piece in (sum_out, sum_up, sum_down)
    ]
    return (result, grad_tokens, grad_qkv, grad_out, grad_up, grad_down, grad_small)


def solution(mesh):
    groups, owners = mesh.shape["dp"], mesh.shape["ctx"]
    fine = Mesh(mesh.devices.reshape(groups, owners // 2, 2), ("dp", "y", "core"))
    rows = P("dp", ("y", "core"), None)
    flat = P(("dp", "y", "core"))
    return jax.shard_map(
        local,
        mesh=fine,
        in_specs=(rows, P("dp", None), flat, flat, flat, flat, flat, rows),
        out_specs=(rows, rows, flat, flat, flat, flat, flat),
        check_vma=False,
    )
```

```python
import jax
import jax.numpy as jnp
from jax import lax
from jax.experimental import pallas as pl
from jax.experimental.pallas import tpu as pltpu
from jax.sharding import Mesh, PartitionSpec as P

HEADS = 17
HEAD_DIM = 64
FF = 4352
LANES = 8
KV_WIDE = 1152
SWAP = ((0, 1), (1, 0))
OWNERS = ("dp", "y")


def layer_stats(values):
    center = values - jnp.mean(values, axis=-1, keepdims=True)
    inverse = lax.rsqrt(jnp.mean(center * center, axis=-1, keepdims=True) + 1e-05)
    return (center * inverse, inverse)


def norm_back(upstream, normed, inverse, gain_vector):
    scaled = upstream * gain_vector
    return inverse * (
        scaled
        - jnp.mean(scaled, axis=-1, keepdims=True)
        - normed * jnp.mean(scaled * normed, axis=-1, keepdims=True)
    )


def lead_dot(left_side, right_side):
    return lax.dot_general(
        left_side, right_side, (((0,), (0,)), ((), ())), preferred_element_type=jnp.float32
    )


def tail_dot(left_side, right_side):
    return lax.dot_general(
        left_side, right_side, (((1,), (1,)), ((), ())), preferred_element_type=jnp.float32
    )


def gate_and_slope(values):
    rate = (2.0 / jnp.pi) ** 0.5
    square = values * values
    bend = jnp.tanh(rate * values * (1.0 + 0.044715 * square))
    share = 0.5 * (1.0 + bend)
    slope = share + 0.5 * values * (1.0 - bend * bend) * rate * (1.0 + 0.134145 * square)
    return values * share, slope


def pack_small(values, width):
    room = LANES * width - values.shape[-1]
    padded = jnp.pad(values, [(0, 0)] * (values.ndim - 1) + [(0, room)])
    return padded.reshape(values.shape[:-1] + (LANES, width))


def gather_packed(block, core):
    own = lax.all_gather(block, OWNERS, axis=0, tiled=True)
    other = lax.ppermute(own, "core", SWAP)
    even = jnp.where(core == 0, own, other)
    odd = jnp.where(core == 0, other, own)
    shape = (-1, 1, LANES, block.shape[1])
    return jnp.concatenate([even.reshape(shape), odd.reshape(shape)], axis=1)


def scatter_packed(packed, core):
    even, odd = packed[:, 0], packed[:, 1]
    keep = jnp.where(core == 0, even, odd)
    give = jnp.where(core == 0, odd, even)
    got = lax.ppermute(give, "core", SWAP)
    pair = (keep.astype(jnp.float32) + got.astype(jnp.float32)).astype(jnp.bfloat16)
    return lax.psum_scatter(pair, OWNERS, scatter_dimension=0, tiled=True)[0]


def dot_rows(left, right):
    return lax.dot_general(
        left, right, (((1,), (0,)), ((), ())), preferred_element_type=jnp.float32
    )


def bias_of(key_places, query_places):
    return jnp.where(key_places <= query_places, 0.0, -1e30).astype(jnp.float32)


def per_pair(one_pair):
    wide = 2 * HEAD_DIM
    full = HEADS // 2

    def step(number, carry):
        start = pl.multiple_of(number * wide, wide)
        one_pair(pl.ds(start, wide), pl.ds(KV_WIDE + start, wide), 2 * number, 2)
        return carry

    lax.fori_loop(0, full, step, 0)
    if HEADS % 2:
        start = full * wide
        one_pair(pl.ds(start, HEAD_DIM), pl.ds(KV_WIDE + start, HEAD_DIM), 2 * full, 1)


def only_head(values, number, heads):
    if heads == 1:
        return values
    lane = lax.broadcasted_iota(jnp.int32, values.shape, 1)
    inside = lane < HEAD_DIM if number == 0 else lane >= HEAD_DIM
    return jnp.where(inside, values, jnp.zeros_like(values))


def join_heads(parts):
    if len(parts) == 1:
        return parts[0]
    lane = lax.broadcasted_iota(jnp.int32, parts[0].shape, 1)
    return jnp.where(lane < HEAD_DIM, parts[0], parts[1])


def attend_kernel(
    q_ref, own_ref, other_ref, query_ref, key_ref, mixed_ref, log_ref, low_bias, up_bias
):
    half = q_ref.shape[0] // 2
    low_bias[...] = bias_of(key_ref[: 2 * half], query_ref[:, :half])
    up_bias[...] = bias_of(key_ref[2 * half :], query_ref[:, half:])

    def one_pair(lanes, vlanes, first, heads):
        q = q_ref[:, lanes] * jnp.asarray(HEAD_DIM**-0.5, jnp.bfloat16)
        k_low = jnp.concatenate([own_ref[:half, lanes], other_ref[:half, lanes]], axis=0)
        k_up = jnp.concatenate([own_ref[half:, lanes], other_ref[half:, lanes]], axis=0)
        v_low = jnp.concatenate([own_ref[:half, vlanes], other_ref[:half, vlanes]], axis=0).T
        v_up = jnp.concatenate([own_ref[half:, vlanes], other_ref[half:, vlanes]], axis=0).T
        low_parts, up_parts = [], []
        for number in range(heads):
            rows = slice(number * HEAD_DIM, (number + 1) * HEAD_DIM)
            q_head = only_head(q, number, heads)
            s = tail_dot(k_low, q_head[:half]) + low_bias[...]
            top = jnp.max(s, axis=0, keepdims=True)
            e = jnp.exp(s - top)
            total = jnp.sum(e, axis=0, keepdims=True)
            mixed = dot_rows(v_low[rows], e.astype(jnp.bfloat16)) / total
            low_parts.append(mixed)
            log_ref[pl.ds(first + number, 1), :half] = top + jnp.log(total)
            s_low = tail_dot(k_low, q_head[half:])
            s_up = tail_dot(k_up, q_head[half:]) + up_bias[...]
            top = jnp.maximum(
                jnp.max(s_low, axis=0, keepdims=True), jnp.max(s_up, axis=0, keepdims=True)
            )
            e_low = jnp.exp(s_low - top)
            e_up = jnp.exp(s_up - top)
            total = jnp.sum(e_low, axis=0, keepdims=True) + jnp.sum(e_up, axis=0, keepdims=True)
            mixed = dot_rows(v_low[rows], e_low.astype(jnp.bfloat16))
            mixed = mixed + dot_rows(v_up[rows], e_up.astype(jnp.bfloat16))
            up_parts.append(mixed / total)
            log_ref[pl.ds(first + number, 1), half:] = top + jnp.log(total)
        mixed_ref[:half, lanes] = jnp.concatenate(low_parts, axis=0).T.astype(jnp.bfloat16)
        mixed_ref[half:, lanes] = jnp.concatenate(up_parts, axis=0).T.astype(jnp.bfloat16)

    per_pair(one_pair)


def attend_back_kernel(
    q_ref,
    own_ref,
    other_ref,
    query_ref,
    key_ref,
    mixed_ref,
    log_ref,
    grad_ref,
    dq_ref,
    own_out,
    other_out,
    low_bias,
    up_bias,
):
    half = q_ref.shape[0] // 2
    factor = HEAD_DIM**-0.5
    low_bias[...] = bias_of(key_ref[: 2 * half], query_ref[:, :half])
    up_bias[...] = bias_of(key_ref[2 * half :], query_ref[:, half:])

    def one_pair(lanes, vlanes, first, heads):
        q = q_ref[:, lanes] * jnp.asarray(factor, jnp.bfloat16)
        grad = grad_ref[:, lanes]
        product = (grad.astype(jnp.float32) * mixed_ref[:, lanes].astype(jnp.float32)).T
        q_heads = [only_head(q, number, heads) for number in range(heads)]
        grad_heads = [only_head(grad, number, heads) for number in range(heads)]
        deltas = [
            jnp.sum(product[number * HEAD_DIM : (number + 1) * HEAD_DIM], axis=0, keepdims=True)
            for number in range(heads)
        ]
        logs = [log_ref[pl.ds(first + number, 1), :] for number in range(heads)]
        dq_low = [None] * heads
        dq_up = [None] * heads
        for source, out, place in ((own_ref, own_out, 0), (other_ref, other_out, 1)):
            bias_rows = slice(place * half, (place + 1) * half)
            for upper in (False, True):
                rows = slice(half, None) if upper else slice(0, half)
                k = source[rows, lanes]
                v = source[rows, vlanes]
                k_turned = k.T
                dk_parts, dv_parts = [], []
                for number in range(heads):
                    head_rows = slice(number * HEAD_DIM, (number + 1) * HEAD_DIM)
                    first_query = half if upper else 0
                    q_head = q_heads[number][first_query:]
                    grad_head = grad_heads[number][first_query:]
                    s = tail_dot(k, q_head)
                    if upper:
                        s = s + up_bias[bias_rows]
                    else:
                        s = jnp.concatenate([s[:, :half] + low_bias[bias_rows], s[:, half:]], axis=1)
                    p = jnp.exp(s - logs[number][:, first_query:])
                    dp = tail_dot(v, grad_head)
                    ds = (p * (dp - deltas[number][:, first_query:])).astype(jnp.bfloat16)
                    dv_parts.append(dot_rows(p.astype(jnp.bfloat16), grad[first_query:]))
                    dk_parts.append(dot_rows(ds, q[first_query:]))
                    turned = dot_rows(k_turned[head_rows], ds)
                    low = None if upper else turned[:, :half]
                    up = turned if upper else turned[:, half:]
                    if low is not None:
                        dq_low[number] = low if dq_low[number] is None else dq_low[number] + low
                    dq_up[number] = up if dq_up[number] is None else dq_up[number] + up
                out[rows, lanes] = join_heads(dk_parts).astype(jnp.bfloat16)
                out[rows, vlanes] = join_heads(dv_parts).astype(jnp.bfloat16)
        dq_ref[:half, lanes] = (jnp.concatenate(dq_low, axis=0).T * factor).astype(jnp.bfloat16)
        dq_ref[half:, lanes] = (jnp.concatenate(dq_up, axis=0).T * factor).astype(jnp.bfloat16)

    per_pair(one_pair)


def kernel_call(body, outs, half, cost):
    return pl.pallas_call(
        body,
        out_shape=outs,
        scratch_shapes=[pltpu.VMEM((2 * half, half), jnp.float32)] * 2,
        compiler_params=pltpu.CompilerParams(vmem_limit_bytes=48 * 1024 * 1024),
        cost_estimate=pl.CostEstimate(flops=cost, bytes_accessed=12 << 20, transcendentals=cost // 256),
    )


def outer_kernel(left_ref, right_ref, out_ref):
    out_ref[...] = lead_dot(left_ref[...], right_ref[...]).astype(out_ref.dtype)


def outer(left, right):
    rows, count = left.shape
    width = right.shape[1]
    step = 256
    return pl.pallas_call(
        outer_kernel,
        grid=(count // step,),
        in_specs=[
            pl.BlockSpec((rows, step), lambda i: (0, i)),
            pl.BlockSpec((rows, width), lambda i: (0, 0)),
        ],
        out_specs=pl.BlockSpec((step, width), lambda i: (i, 0)),
        out_shape=jax.ShapeDtypeStruct((count, width), jnp.bfloat16),
        compiler_params=pltpu.CompilerParams(vmem_limit_bytes=32 * 1024 * 1024),
        cost_estimate=pl.CostEstimate(
            flops=2 * rows * count * width, bytes_accessed=16 << 20, transcendentals=0
        ),
    )(left, right)


def attend(query, own, other, query_places, key_places):
    rows, width = query.shape
    outs = (
        jax.ShapeDtypeStruct((rows, width), jnp.bfloat16),
        jax.ShapeDtypeStruct((HEADS, rows), jnp.float32),
    )
    call = kernel_call(attend_kernel, outs, rows // 2, 8 << 30)
    return call(query, own, other, query_places, key_places)


def attend_back(query, own, other, query_places, key_places, mixed, logs, grad):
    rows, width = query.shape
    outs = (
        jax.ShapeDtypeStruct((rows, width), jnp.bfloat16),
        jax.ShapeDtypeStruct(own.shape, jnp.bfloat16),
        jax.ShapeDtypeStruct(own.shape, jnp.bfloat16),
    )
    call = kernel_call(attend_back_kernel, outs, rows // 2, 24 << 30)
    return call(query, own, other, query_places, key_places, mixed, logs, grad)


ALL = ("dp", "y", "core")


def round_low(values):
    return values.astype(jnp.bfloat16)


def one_hot_columns(targets, width):
    line = lax.broadcasted_iota(jnp.int32, (width, targets.shape[0]), 0)
    return (line == targets[None, :]).astype(jnp.bfloat16)


def swap_with(values, axis, bit):
    count = lax.axis_size(axis)
    return lax.ppermute(values, axis, [(here, here ^ (1 << bit)) for here in range(count)])


def near_owners(order, dp_bits, each):
    owner = (lax.axis_index("dp") * 2 + lax.axis_index("y")) * 2 + lax.axis_index("core")
    bits = dp_bits + 2
    column = jnp.arange(each << bits, dtype=jnp.int32)
    place, inner = column // each, column % each
    far = jnp.zeros_like(place)
    for number, (axis, bit) in enumerate(order):
        weight = {"core": 0, "y": 1, "dp": 2 + bit}[axis]
        far = far + (((place >> (bits - 1 - number)) & 1) << weight)
    return (owner ^ far) * each + inner


def give_first(left, right, order):
    half = left.shape[1] // 2
    return swap_with(round_low(lead_dot(left[:, half:], right)), *order[0])


def keep_first(left, right, got):
    half = left.shape[1] // 2
    return round_low(lead_dot(left[:, :half], right) + got.astype(jnp.float32))


def double(values, axis, bit):
    return jnp.concatenate([values, swap_with(values, axis, bit)], axis=0)


tie = lax.optimization_barrier


def halve(values, axis, bit):
    half = values.shape[0] // 2
    got = swap_with(values[half:], axis, bit)
    return round_low(values[:half].astype(jnp.float32) + got.astype(jnp.float32))


def local(tokens, positions, w_qkv, w_out, w_up, w_down, small_params, cotangent):
    seqs_here, local_len, model_width = tokens.shape
    span = local_len // 2
    rows = seqs_here * local_len
    half = rows // 2
    y = lax.axis_index("y")
    core = lax.axis_index("core")
    groups = lax.axis_size("dp")
    owners = groups * 4
    small_len = small_params.shape[0]
    whole_rows = model_width % owners == 0
    each = model_width // owners
    dp_bits = groups.bit_length() - 1

    def trade(values):
        mine = lax.dynamic_index_in_dim(values, y, 0, keepdims=False)
        give = lax.dynamic_index_in_dim(values, 1 - y, 0, keepdims=False)
        got = lax.ppermute(give, "y", SWAP)
        return jnp.concatenate([mine[:span], got[:span], mine[span:], got[span:]], axis=0)

    def trade_back(values):
        mine = jnp.concatenate([values[:span], values[half : half + span]], axis=0)
        give = jnp.concatenate([values[span:half], values[half + span :]], axis=0)
        got = lax.ppermute(give, "y", SWAP)
        first = jnp.where(y == 0, mine, got)
        second = jnp.where(y == 0, got, mine)
        return jnp.stack([first, second])

    inputs = trade(tokens)
    grad_rows = trade(cotangent)
    if whole_rows:
        steps = [("dp", bit) for bit in range(dp_bits)]
        order_a = [("core", 0), steps[0], ("y", 0)] + steps[1:]
        order_b = [("core", 0), ("y", 0), steps[0]] + steps[1:]
        turn_a = one_hot_columns(near_owners(order_a, dp_bits, each), model_width)
        turn_b = one_hot_columns(near_owners(order_b, dp_bits, each), model_width)
        blocks = jnp.concatenate(
            [w_qkv.reshape(each, 3 * model_width), w_out.reshape(each, model_width)], axis=1
        )
        room = -(each + 1) % 8
        held = each + 1 + room
        extra = jnp.pad(small_params.reshape(1, -1), [(0, room), (0, FF - small_len)])
        extra = extra.reshape(1 + room, FF)
        blocks = jnp.concatenate([blocks, extra], axis=0)
        blocks = lax.all_gather(blocks, ALL, axis=0, tiled=True)
        down_mat = lax.all_gather(w_down.reshape(-1, model_width), ALL, axis=0, tiled=True)
        up_part = w_up.reshape(each, FF)
        for step in order_a[:2:-1]:
            up_part = double(up_part, *step)
        up_cut = FF // 2
        up_a = double(up_part[:, :up_cut], *order_a[2])
        up_b = double(up_part[:, up_cut:], *order_b[2])
        up_a = double(up_a, *order_a[1])
        up_b = double(up_b, *order_b[1])
        blocks, up_a, up_b = tie((blocks, up_a, up_b))
        qkv_mat = blocks[:, : 3 * model_width]
        out_mat = blocks[:, 3 * model_width :]
        packed = blocks.reshape(owners, held, FF)[:, each, :small_len].reshape(-1)
        column = jnp.arange(owners * held, dtype=jnp.int32)
        inside = column % held
        spread = jnp.where(inside < each, column // held * each + inside, -1)
        spread = one_hot_columns(spread, model_width)

        def widen(values):
            return round_low(dot_rows(values, spread))

        def narrow(values):
            return tail_dot(round_low(values), spread)

        def turned(values):
            return round_low(dot_rows(values, turn_a)), round_low(dot_rows(values, turn_b))

    else:
        small_width = -(-small_len // LANES)
        qkv_width = w_qkv.shape[0] // LANES
        blocks = jnp.concatenate(
            [w_qkv.reshape(LANES, qkv_width), pack_small(small_params, small_width)], axis=1
        )
        blocks = gather_packed(blocks, core)
        qkv_mat = blocks[..., :qkv_width].reshape(model_width, 3 * model_width)
        packed = blocks[..., qkv_width:].reshape(owners, -1)[:, :small_len].reshape(-1)
        out_mat = gather_packed(w_out.reshape(LANES, -1), core).reshape(model_width, model_width)
        up_mat = gather_packed(w_up.reshape(LANES, -1), core).reshape(model_width, FF)
        down_mat = gather_packed(w_down.reshape(LANES, -1), core).reshape(FF, model_width)

        def widen(values):
            return values

        def narrow(values):
            return values

        def send_sum(left, right, extra=None):
            grad = round_low(lead_dot(left, right)).reshape(groups * 2, 2, LANES, -1)
            if extra is not None:
                extra = extra.reshape(groups * 2, 2, small_len)
                grad = jnp.concatenate([grad, pack_small(extra, small_width)], axis=-1)
            return scatter_packed(grad, core)

    packed = packed.astype(jnp.float32)
    pieces = [packed[number * model_width : (number + 1) * model_width] for number in range(7)]
    gain_one, bias_one, bias_query, bias_value, bias_out, gain_two, bias_two = pieces
    up_bias = packed[7 * model_width : 7 * model_width + FF]
    down_bias = packed[7 * model_width + FF :]

    place_row = lax.dynamic_index_in_dim(positions, y, 0, keepdims=False)

    def places_of(core_index):
        near = lax.dynamic_slice_in_dim(place_row, (2 * y + core_index) * local_len, local_len)
        far = lax.dynamic_slice_in_dim(place_row, (2 - 2 * y + core_index) * local_len, local_len)
        return jnp.concatenate([near[:span], far[:span]]), jnp.concatenate([near[span:], far[span:]])

    own_low, own_up = places_of(core)
    other_low, other_up = places_of(1 - core)
    query_places = jnp.concatenate([own_low, own_up])[None, :]
    key_places = jnp.concatenate([own_low, other_low, own_up, other_up])[:, None]

    inputs = inputs.astype(jnp.float32)
    normed_one, inverse_one = layer_stats(inputs)
    act_one = round_low(normed_one * gain_one + bias_one)
    qkv_bias = jnp.concatenate([bias_query, jnp.zeros_like(bias_query), bias_value])
    qkv_rows = round_low(dot_rows(widen(act_one), qkv_mat) + qkv_bias)
    query = qkv_rows[:, :model_width]
    spare = jnp.zeros((rows, KV_WIDE - model_width), jnp.bfloat16)
    own_kv = jnp.concatenate(
        [qkv_rows[:, model_width : 2 * model_width], spare, qkv_rows[:, 2 * model_width :], spare],
        axis=1,
    )
    other_kv = lax.ppermute(own_kv, "core", SWAP)
    mixed, logs = attend(query, own_kv, other_kv, query_places, key_places)
    if whole_rows:
        up_a = double(up_a, *order_a[0])
        up_b = double(up_b, *order_b[0])
        mixed, up_a, up_b = tie((mixed, up_a, up_b))
    resid = inputs + dot_rows(widen(mixed), out_mat) + bias_out
    normed_two, inverse_two = layer_stats(resid)
    act_two = round_low(normed_two * gain_two + bias_two)
    if whole_rows:
        two_a, two_b = turned(act_two)
        gelu_a, slope_a = gate_and_slope(dot_rows(two_a, up_a) + up_bias[:up_cut])
        gelu_b, slope_b = gate_and_slope(dot_rows(two_b, up_b) + up_bias[up_cut:])
        slopes = [round_low(slope_a), round_low(slope_b)]
        gelu_rows = jnp.concatenate([round_low(gelu_a), round_low(gelu_b)], axis=1)
    else:
        gelu_rows, slope = gate_and_slope(dot_rows(act_two, up_mat) + up_bias)
        slopes = [round_low(slope)]
        gelu_rows = round_low(gelu_rows)
    sum_down = outer(gelu_rows, grad_rows)
    gelu_rows, sum_down, slopes = tie((gelu_rows, sum_down, slopes))
    sum_down = sum_down.reshape(owners, -1, model_width)
    sum_down = lax.psum_scatter(sum_down, ALL, scatter_dimension=0, tiled=True)
    outputs = resid + dot_rows(gelu_rows, down_mat) + down_bias
    result = trade_back(round_low(outputs))

    grad_float = grad_rows.astype(jnp.float32)
    down_bias_term = jnp.sum(grad_float, axis=0)
    wide = FF // len(slopes)
    grad_pre = [
        round_low(
            tail_dot(grad_rows, down_mat[number * wide : (number + 1) * wide])
            * slope.astype(jnp.float32)
        )
        for number, slope in enumerate(slopes)
    ]
    up_bias_term = jnp.concatenate(
        [jnp.sum(part.astype(jnp.float32), axis=0) for part in grad_pre]
    )
    if whole_rows:
        pre_a, pre_b = grad_pre
        got_a = give_first(two_a, pre_a, order_a)
        got_b = give_first(two_b, pre_b, order_b)
        back_a, back_b = tail_dot(pre_a, up_a), tail_dot(pre_b, up_b)
        back_a, back_b, got_a, got_b = tie((back_a, back_b, got_a, got_b))
        sum_a = keep_first(two_a, pre_a, got_a)
        sum_b = keep_first(two_b, pre_b, got_b)
        back_a, back_b, sum_a, sum_b = tie((back_a, back_b, sum_a, sum_b))
        grad_act_two = tail_dot(round_low(back_a), turn_a) + tail_dot(round_low(back_b), turn_b)
    else:
        sum_up = send_sum(act_two, grad_pre[0])
        grad_act_two = tail_dot(grad_pre[0], up_mat)
    gain_two_term = jnp.sum(grad_act_two * normed_two, axis=0)
    bias_two_term = jnp.sum(grad_act_two, axis=0)
    grad_resid = grad_float + norm_back(grad_act_two, normed_two, inverse_two, gain_two)
    grad_attn = round_low(grad_resid)
    bias_out_term = jnp.sum(grad_attn.astype(jnp.float32), axis=0)
    if whole_rows:
        out_cut = (model_width // 256) * 128
        mixed_a, mixed_b = turned(mixed)
        out_got_a = give_first(mixed_a, grad_attn[:, :out_cut], order_a)
        out_got_b = give_first(mixed_b, grad_attn[:, out_cut:], order_b)
    else:
        sum_out = send_sum(mixed, grad_attn)
    grad_mixed = round_low(narrow(tail_dot(grad_attn, out_mat)))
    if whole_rows:
        out_a = keep_first(mixed_a, grad_attn[:, :out_cut], out_got_a)
        out_b = keep_first(mixed_b, grad_attn[:, out_cut:], out_got_b)
        grad_mixed, out_a, out_b = tie((grad_mixed, out_a, out_b))
    grad_query, grad_own, grad_other = attend_back(
        query, own_kv, other_kv, query_places, key_places, mixed, logs, grad_mixed
    )
    if whole_rows:
        sum_a, sum_b = halve(sum_a, *order_a[1]), halve(sum_b, *order_b[1])
        out_a, out_b = halve(out_a, *order_a[1]), halve(out_b, *order_b[1])
        grad_other, sum_a, sum_b, out_a, out_b = tie((grad_other, sum_a, sum_b, out_a, out_b))
        one_a, one_b = turned(act_one)
    grad_got = lax.ppermute(grad_other, "core", SWAP)
    grad_kv = round_low(grad_own.astype(jnp.float32) + grad_got.astype(jnp.float32))
    grad_qkv_rows = jnp.concatenate(
        [grad_query, grad_kv[:, :model_width], grad_kv[:, KV_WIDE : KV_WIDE + model_width]], axis=1
    )
    qkv_sums = jnp.sum(grad_qkv_rows.astype(jnp.float32), axis=0)
    if whole_rows:
        qkv_cut = (3 * model_width // 256) * 128
        rows_a, rows_b = grad_qkv_rows[:, :qkv_cut], grad_qkv_rows[:, qkv_cut:]
        qkv_got_a = give_first(one_a, rows_a, order_a)
        qkv_got_b = give_first(one_b, rows_b, order_b)
    grad_act_one = narrow(tail_dot(grad_qkv_rows, qkv_mat))
    if whole_rows:
        sum_a, sum_b = halve(sum_a, *order_a[2]), halve(sum_b, *order_b[2])
        out_a, out_b = halve(out_a, *order_a[2]), halve(out_b, *order_b[2])
        rest = jnp.concatenate([sum_a, sum_b, out_a, out_b], axis=1)
        qkv_a = keep_first(one_a, rows_a, qkv_got_a)
        qkv_b = keep_first(one_b, rows_b, qkv_got_b)
        rest, qkv_a, qkv_b, grad_act_one = tie((rest, qkv_a, qkv_b, grad_act_one))
    gain_one_term = jnp.sum(grad_act_one * normed_one, axis=0)
    bias_one_term = jnp.sum(grad_act_one, axis=0)
    small_grad = jnp.concatenate(
        [
            gain_one_term,
            bias_one_term,
            qkv_sums[:model_width],
            qkv_sums[2 * model_width :],
            bias_out_term,
            gain_two_term,
            bias_two_term,
            up_bias_term,
            down_bias_term,
        ]
    )
    small_grad = round_low(small_grad)
    grad_input = grad_resid + norm_back(grad_act_one, normed_one, inverse_one, gain_one)
    grad_input = round_low(grad_input)
    if whole_rows:
        small_rows = round_low(lead_dot(turn_a, small_grad.reshape(model_width, -1)))
        small_rows = halve(small_rows, *order_a[0])
        qkv_a, qkv_b = halve(qkv_a, *order_a[1]), halve(qkv_b, *order_b[1])
        rest = halve(rest, *order_a[3])
        grad_input, qkv_a, qkv_b, rest, small_rows = tie(
            (grad_input, qkv_a, qkv_b, rest, small_rows)
        )
        qkv_a, qkv_b = halve(qkv_a, *order_a[2]), halve(qkv_b, *order_b[2])
        small_rows = halve(halve(small_rows, *order_a[1]), *order_a[2])
        for step in order_a[4:]:
            rest = halve(rest, *step)
        qkv_a, qkv_b, rest, small_rows = tie((qkv_a, qkv_b, rest, small_rows))
        sum_qkv = jnp.concatenate([qkv_a, qkv_b, small_rows], axis=1)
        for step in order_a[3:]:
            sum_qkv = halve(sum_qkv, *step)
        sum_up, sum_out = rest[:, :FF], rest[:, FF:]
    else:
        sum_qkv = send_sum(act_one, grad_qkv_rows, small_grad)
    grad_tokens = trade_back(grad_input)
    main = w_qkv.shape[0] // sum_qkv.shape[0]
    grad_qkv = sum_qkv[:, :main].astype(jnp.float32).reshape(-1)
    grad_small = sum_qkv[:, main:].astype(jnp.float32).reshape(-1)[:small_len]
    grad_out, grad_up, grad_down = [
        piece.astype(jnp.float32).reshape(-1) for piece in (sum_out, sum_up, sum_down)
    ]
    return (result, grad_tokens, grad_qkv, grad_out, grad_up, grad_down, grad_small)


def solution(mesh):
    groups, owners = mesh.shape["dp"], mesh.shape["ctx"]
    fine = Mesh(mesh.devices.reshape(groups, owners // 2, 2), ("dp", "y", "core"))
    rows = P("dp", ("y", "core"), None)
    flat = P(("dp", "y", "core"))
    return jax.shard_map(
        local,
        mesh=fine,
        in_specs=(rows, P("dp", None), flat, flat, flat, flat, flat, rows),
        out_specs=(rows, rows, flat, flat, flat, flat, flat),
        check_vma=False,
    )
```

```python
import jax
import jax.numpy as jnp
from jax import lax
from jax.experimental import pallas as pl
from jax.experimental.pallas import tpu as pltpu
from jax.sharding import Mesh, PartitionSpec as P

HEADS = 17
HEAD_DIM = 64
FF = 4352
LANES = 8
WIDE = 1152
SWAP = ((0, 1), (1, 0))
OWNERS = ("dp", "y")


def layer_stats(values):
    center = values - jnp.mean(values, axis=-1, keepdims=True)
    inverse = lax.rsqrt(jnp.mean(center * center, axis=-1, keepdims=True) + 1e-05)
    return (center * inverse, inverse)


def norm_back(upstream, normed, inverse, gain_vector):
    scaled = upstream * gain_vector
    return inverse * (
        scaled
        - jnp.mean(scaled, axis=-1, keepdims=True)
        - normed * jnp.mean(scaled * normed, axis=-1, keepdims=True)
    )


def lead_dot(left_side, right_side):
    return lax.dot_general(
        left_side, right_side, (((0,), (0,)), ((), ())), preferred_element_type=jnp.float32
    )


def tail_dot(left_side, right_side):
    return lax.dot_general(
        left_side, right_side, (((1,), (1,)), ((), ())), preferred_element_type=jnp.float32
    )


def gate_and_slope(values):
    rate = (2.0 / jnp.pi) ** 0.5
    square = values * values
    bend = jnp.tanh(rate * values * (1.0 + 0.044715 * square))
    share = 0.5 * (1.0 + bend)
    slope = share + 0.5 * values * (1.0 - bend * bend) * rate * (1.0 + 0.134145 * square)
    return values * share, slope


def pack_small(values, width):
    room = LANES * width - values.shape[-1]
    padded = jnp.pad(values, [(0, 0)] * (values.ndim - 1) + [(0, room)])
    return padded.reshape(values.shape[:-1] + (LANES, width))


def gather_packed(block, core):
    own = lax.all_gather(block, OWNERS, axis=0, tiled=True)
    other = lax.ppermute(own, "core", SWAP)
    even = jnp.where(core == 0, own, other)
    odd = jnp.where(core == 0, other, own)
    shape = (-1, 1, LANES, block.shape[1])
    return jnp.concatenate([even.reshape(shape), odd.reshape(shape)], axis=1)


def scatter_packed(packed, core):
    even, odd = packed[:, 0], packed[:, 1]
    keep = jnp.where(core == 0, even, odd)
    give = jnp.where(core == 0, odd, even)
    got = lax.ppermute(give, "core", SWAP)
    pair = (keep.astype(jnp.float32) + got.astype(jnp.float32)).astype(jnp.bfloat16)
    return lax.psum_scatter(pair, OWNERS, scatter_dimension=0, tiled=True)[0]


def dot_rows(left, right):
    return lax.dot_general(
        left, right, (((1,), (0,)), ((), ())), preferred_element_type=jnp.float32
    )


def bias_of(key_places, query_places):
    return jnp.where(key_places <= query_places, 0.0, -1e30).astype(jnp.float32)


def per_pair(one_pair):
    pair = 2 * HEAD_DIM
    full = HEADS // 2

    def step(number, carry):
        one_pair(pl.multiple_of(number * pair, pair), 2 * number, 2)
        return carry

    lax.fori_loop(0, full, step, 0)
    if HEADS % 2:
        one_pair(full * pair, 2 * full, 1)


def lanes_at(start, block):
    return pl.ds(block * WIDE + start, 2 * HEAD_DIM)


def stand(parts):
    if len(parts) == 1:
        parts = parts + [jnp.zeros_like(parts[0])]
    return jnp.concatenate(parts, axis=0).T


def only_head(values, number, heads):
    if heads == 1:
        return values
    lane = lax.broadcasted_iota(jnp.int32, values.shape, 1)
    inside = lane < HEAD_DIM if number == 0 else lane >= HEAD_DIM
    return jnp.where(inside, values, jnp.zeros_like(values))


def join_heads(parts):
    if len(parts) == 1:
        return parts[0]
    lane = lax.broadcasted_iota(jnp.int32, parts[0].shape, 1)
    return jnp.where(lane < HEAD_DIM, parts[0], parts[1])


def attend_kernel(
    own_ref, other_ref, query_ref, key_ref, mixed_ref, log_ref, low_bias, up_bias
):
    half = own_ref.shape[0] // 2
    low_bias[...] = bias_of(key_ref[: 2 * half], query_ref[:, :half])
    up_bias[...] = bias_of(key_ref[2 * half :], query_ref[:, half:])

    def one_pair(start, first, heads):
        q = own_ref[:, lanes_at(start, 0)] * jnp.asarray(HEAD_DIM**-0.5, jnp.bfloat16)
        k_own, v_own = own_ref[:, lanes_at(start, 1)], own_ref[:, lanes_at(start, 2)]
        k_other, v_other = other_ref[:, lanes_at(start, 0)], other_ref[:, lanes_at(start, 1)]
        k_low = jnp.concatenate([k_own[:half], k_other[:half]], axis=0)
        k_up = jnp.concatenate([k_own[half:], k_other[half:]], axis=0)
        v_low = jnp.concatenate([v_own[:half], v_other[:half]], axis=0).T
        v_up = jnp.concatenate([v_own[half:], v_other[half:]], axis=0).T
        low_parts, up_parts = [], []
        for number in range(heads):
            rows = slice(number * HEAD_DIM, (number + 1) * HEAD_DIM)
            q_head = only_head(q, number, heads)
            s = tail_dot(k_low, q_head[:half]) + low_bias[...]
            top = jnp.max(s, axis=0, keepdims=True)
            e = jnp.exp(s - top)
            total = jnp.sum(e, axis=0, keepdims=True)
            mixed = dot_rows(v_low[rows], e.astype(jnp.bfloat16)) / total
            low_parts.append(mixed)
            log_ref[pl.ds(first + number, 1), :half] = top + jnp.log(total)
            s_low = tail_dot(k_low, q_head[half:])
            s_up = tail_dot(k_up, q_head[half:]) + up_bias[...]
            top = jnp.maximum(
                jnp.max(s_low, axis=0, keepdims=True), jnp.max(s_up, axis=0, keepdims=True)
            )
            e_low = jnp.exp(s_low - top)
            e_up = jnp.exp(s_up - top)
            total = jnp.sum(e_low, axis=0, keepdims=True) + jnp.sum(e_up, axis=0, keepdims=True)
            mixed = dot_rows(v_low[rows], e_low.astype(jnp.bfloat16))
            mixed = mixed + dot_rows(v_up[rows], e_up.astype(jnp.bfloat16))
            up_parts.append(mixed / total)
            log_ref[pl.ds(first + number, 1), half:] = top + jnp.log(total)
        mixed_ref[:half, lanes_at(start, 0)] = stand(low_parts).astype(jnp.bfloat16)
        mixed_ref[half:, lanes_at(start, 0)] = stand(up_parts).astype(jnp.bfloat16)

    per_pair(one_pair)


def attend_back_kernel(
    own_ref,
    other_ref,
    query_ref,
    key_ref,
    mixed_ref,
    log_ref,
    grad_ref,
    own_out,
    other_out,
    low_bias,
    up_bias,
):
    half = own_ref.shape[0] // 2
    factor = HEAD_DIM**-0.5
    low_bias[...] = bias_of(key_ref[: 2 * half], query_ref[:, :half])
    up_bias[...] = bias_of(key_ref[2 * half :], query_ref[:, half:])

    def one_pair(start, first, heads):
        lanes = lanes_at(start, 0)
        q = own_ref[:, lanes] * jnp.asarray(factor, jnp.bfloat16)
        grad = grad_ref[:, lanes]
        product = (grad.astype(jnp.float32) * mixed_ref[:, lanes].astype(jnp.float32)).T
        q_heads = [only_head(q, number, heads) for number in range(heads)]
        grad_heads = [only_head(grad, number, heads) for number in range(heads)]
        deltas = [
            jnp.sum(product[number * HEAD_DIM : (number + 1) * HEAD_DIM], axis=0, keepdims=True)
            for number in range(heads)
        ]
        logs = [log_ref[pl.ds(first + number, 1), :] for number in range(heads)]
        dq_low = [None] * heads
        dq_up = [None] * heads
        for source, out, place, block in (
            (own_ref, own_out, 0, 1),
            (other_ref, other_out, 1, 0),
        ):
            klanes, vlanes = lanes_at(start, block), lanes_at(start, block + 1)
            bias_rows = slice(place * half, (place + 1) * half)
            for upper in (False, True):
                rows = slice(half, None) if upper else slice(0, half)
                k = source[rows, klanes]
                v = source[rows, vlanes]
                k_turned = k.T
                dk_parts, dv_parts = [], []
                for number in range(heads):
                    head_rows = slice(number * HEAD_DIM, (number + 1) * HEAD_DIM)
                    first_query = half if upper else 0
                    q_head = q_heads[number][first_query:]
                    grad_head = grad_heads[number][first_query:]
                    s = tail_dot(k, q_head)
                    if upper:
                        s = s + up_bias[bias_rows]
                    else:
                        s = jnp.concatenate([s[:, :half] + low_bias[bias_rows], s[:, half:]], axis=1)
                    p = jnp.exp(s - logs[number][:, first_query:])
                    dp = tail_dot(v, grad_head)
                    ds = (p * (dp - deltas[number][:, first_query:])).astype(jnp.bfloat16)
                    dv_parts.append(dot_rows(p.astype(jnp.bfloat16), grad[first_query:]))
                    dk_parts.append(dot_rows(ds, q[first_query:]))
                    turned = dot_rows(k_turned[head_rows], ds)
                    low = None if upper else turned[:, :half]
                    up = turned if upper else turned[:, half:]
                    if low is not None:
                        dq_low[number] = low if dq_low[number] is None else dq_low[number] + low
                    dq_up[number] = up if dq_up[number] is None else dq_up[number] + up
                out[rows, klanes] = join_heads(dk_parts).astype(jnp.bfloat16)
                out[rows, vlanes] = join_heads(dv_parts).astype(jnp.bfloat16)
        own_out[:half, lanes] = (stand(dq_low) * factor).astype(jnp.bfloat16)
        own_out[half:, lanes] = (stand(dq_up) * factor).astype(jnp.bfloat16)

    per_pair(one_pair)


def add_kernel(own_ref, got_ref, out_ref):
    total = own_ref[...].astype(jnp.float32) + got_ref[...].astype(jnp.float32)
    out_ref[...] = total.astype(out_ref.dtype)


def add_received(own, got):
    rows = own.shape[0]
    block = (rows, WIDE)
    return pl.pallas_call(
        add_kernel,
        grid=(2,),
        in_specs=[
            pl.BlockSpec(block, lambda i: (0, i + 1)),
            pl.BlockSpec(block, lambda i: (0, i)),
        ],
        out_specs=pl.BlockSpec(block, lambda i: (0, i + 1)),
        out_shape=jax.ShapeDtypeStruct(own.shape, own.dtype),
        input_output_aliases={0: 0},
        compiler_params=pltpu.CompilerParams(vmem_limit_bytes=32 * 1024 * 1024),
        cost_estimate=pl.CostEstimate(flops=1 << 20, bytes_accessed=7 << 20, transcendentals=0),
    )(own, got)


def kernel_call(body, outs, half, cost):
    return pl.pallas_call(
        body,
        out_shape=outs,
        scratch_shapes=[pltpu.VMEM((2 * half, half), jnp.float32)] * 2,
        compiler_params=pltpu.CompilerParams(vmem_limit_bytes=48 * 1024 * 1024),
        cost_estimate=pl.CostEstimate(flops=cost, bytes_accessed=12 << 20, transcendentals=cost // 256),
    )


def outer_kernel(left_ref, right_ref, out_ref):
    out_ref[...] = lead_dot(left_ref[...], right_ref[...]).astype(out_ref.dtype)


def outer(left, right):
    rows, count = left.shape
    width = right.shape[1]
    step = 256
    return pl.pallas_call(
        outer_kernel,
        grid=(count // step,),
        in_specs=[
            pl.BlockSpec((rows, step), lambda i: (0, i)),
            pl.BlockSpec((rows, width), lambda i: (0, 0)),
        ],
        out_specs=pl.BlockSpec((step, width), lambda i: (i, 0)),
        out_shape=jax.ShapeDtypeStruct((count, width), jnp.bfloat16),
        compiler_params=pltpu.CompilerParams(vmem_limit_bytes=32 * 1024 * 1024),
        cost_estimate=pl.CostEstimate(
            flops=2 * rows * count * width, bytes_accessed=16 << 20, transcendentals=0
        ),
    )(left, right)


def attend(own, other, query_places, key_places):
    rows = own.shape[0]
    outs = (
        jax.ShapeDtypeStruct((rows, WIDE), jnp.bfloat16),
        jax.ShapeDtypeStruct((HEADS, rows), jnp.float32),
    )
    call = kernel_call(attend_kernel, outs, rows // 2, 1 << 30)
    return call(own, other, query_places, key_places)


def attend_back(own, other, query_places, key_places, mixed, logs, grad):
    outs = (
        jax.ShapeDtypeStruct(own.shape, jnp.bfloat16),
        jax.ShapeDtypeStruct(other.shape, jnp.bfloat16),
    )
    call = kernel_call(attend_back_kernel, outs, own.shape[0] // 2, 1 << 30)
    return call(own, other, query_places, key_places, mixed, logs, grad)


ALL = ("dp", "y", "core")


def round_low(values):
    return values.astype(jnp.bfloat16)


def one_hot_columns(targets, width):
    line = lax.broadcasted_iota(jnp.int32, (width, targets.shape[0]), 0)
    return (line == targets[None, :]).astype(jnp.bfloat16)


def swap_with(values, axis, bit):
    count = lax.axis_size(axis)
    return lax.ppermute(values, axis, [(here, here ^ (1 << bit)) for here in range(count)])


def near_owners(order, dp_bits, each):
    owner = (lax.axis_index("dp") * 2 + lax.axis_index("y")) * 2 + lax.axis_index("core")
    bits = dp_bits + 2
    column = jnp.arange(each << bits, dtype=jnp.int32)
    place, inner = column // each, column % each
    far = jnp.zeros_like(place)
    for number, (axis, bit) in enumerate(order):
        weight = {"core": 0, "y": 1, "dp": 2 + bit}[axis]
        far = far + (((place >> (bits - 1 - number)) & 1) << weight)
    return (owner ^ far) * each + inner


def give_first(left, right, order):
    half = left.shape[1] // 2
    return swap_with(round_low(lead_dot(left[:, half:], right)), *order[0])


def keep_first(left, right, got):
    half = left.shape[1] // 2
    kept = round_low(lead_dot(left[:, :half], right))
    return round_low(kept.astype(jnp.float32) + got.astype(jnp.float32))


def double(values, axis, bit):
    return jnp.concatenate([values, swap_with(values, axis, bit)], axis=0)


tie = lax.optimization_barrier


def halve(values, axis, bit):
    half = values.shape[0] // 2
    got = swap_with(values[half:], axis, bit)
    return round_low(values[:half].astype(jnp.float32) + got.astype(jnp.float32))


def spread_blocks(values, width):
    spare = jnp.zeros((values.shape[0], WIDE - width), values.dtype)
    parts = []
    for number in range(3):
        parts += [values[:, number * width : (number + 1) * width], spare]
    return jnp.concatenate(parts, axis=1)


def pick_blocks(values, width):
    return jnp.concatenate(
        [values[:, number * WIDE : number * WIDE + width] for number in range(3)], axis=1
    )


def local(tokens, positions, w_qkv, w_out, w_up, w_down, small_params, cotangent):
    seqs_here, local_len, model_width = tokens.shape
    span = local_len // 2
    rows = seqs_here * local_len
    half = rows // 2
    y = lax.axis_index("y")
    core = lax.axis_index("core")
    groups = lax.axis_size("dp")
    owners = groups * 4
    small_len = small_params.shape[0]
    whole_rows = model_width % owners == 0
    each = model_width // owners
    dp_bits = groups.bit_length() - 1

    def trade(values):
        mine = lax.dynamic_index_in_dim(values, y, 0, keepdims=False)
        give = lax.dynamic_index_in_dim(values, 1 - y, 0, keepdims=False)
        got = lax.ppermute(give, "y", SWAP)
        return jnp.concatenate([mine[:span], got[:span], mine[span:], got[span:]], axis=0)

    def trade_back(values):
        mine = jnp.concatenate([values[:span], values[half : half + span]], axis=0)
        give = jnp.concatenate([values[span:half], values[half + span :]], axis=0)
        got = lax.ppermute(give, "y", SWAP)
        first = jnp.where(y == 0, mine, got)
        second = jnp.where(y == 0, got, mine)
        return jnp.stack([first, second])

    place_row = lax.dynamic_index_in_dim(positions, y, 0, keepdims=False)

    def places_of(core_index):
        near = lax.dynamic_slice_in_dim(place_row, (2 * y + core_index) * local_len, local_len)
        far = lax.dynamic_slice_in_dim(place_row, (2 - 2 * y + core_index) * local_len, local_len)
        return jnp.concatenate([near[:span], far[:span]]), jnp.concatenate([near[span:], far[span:]])

    own_low, own_up = places_of(core)
    other_low, other_up = places_of(1 - core)
    query_places = jnp.concatenate([own_low, own_up])[None, :]
    key_places = jnp.concatenate([own_low, other_low, own_up, other_up])[:, None]

    inputs = trade(tokens)
    grad_rows = trade(cotangent)
    if whole_rows:
        steps = [("dp", bit) for bit in range(dp_bits)]
        order_a = [("core", 0), steps[0], ("y", 0)] + steps[1:]
        order_b = [("core", 0), ("y", 0), steps[0]] + steps[1:]
        near_a = near_owners(order_a, dp_bits, each)
        near_b = near_owners(order_b, dp_bits, each)
        turn_a = one_hot_columns(near_a, model_width)
        turn_b = one_hot_columns(near_b, model_width)
        head_a = one_hot_columns(near_a, WIDE)
        head_b = one_hot_columns(near_b, WIDE)
        room = -(each + 1) % 8
        held = each + 1 + room
        column = jnp.arange(owners * held, dtype=jnp.int32)
        inside = column % held
        spread = jnp.where(inside < each, column // held * each + inside, -1)
        head_spread = one_hot_columns(spread, WIDE)
        spread = one_hot_columns(spread, model_width)
        blocks = jnp.concatenate(
            [
                spread_blocks(w_qkv.reshape(each, 3 * model_width), model_width),
                w_out.reshape(each, model_width),
            ],
            axis=1,
        )
        extra = jnp.pad(
            small_params.reshape(1, -1), [(0, room), (0, blocks.shape[1] - small_len)]
        )
        blocks = jnp.concatenate([blocks, extra], axis=0)
        blocks = lax.all_gather(blocks, ALL, axis=0, tiled=True)
        down_mat = lax.all_gather(w_down.reshape(-1, model_width), ALL, axis=0, tiled=True)
        up_part = w_up.reshape(each, FF)
        for step in order_a[:2:-1]:
            up_part = double(up_part, *step)
        up_cut = FF // 2
        blocks, up_part, inputs, grad_rows, query_places, key_places, turn_a, turn_b, spread = tie(
            (
                blocks,
                up_part,
                inputs,
                grad_rows,
                query_places,
                key_places,
                turn_a,
                turn_b,
                spread,
            )
        )
        head_a, head_b, head_spread = tie((head_a, head_b, head_spread))
        up_a, up_b = up_part[:, :up_cut], up_part[:, up_cut:]
        more_a, more_b = swap_with(up_a, *order_a[2]), swap_with(up_b, *order_b[2])
        qkv_mat = blocks[:, : 3 * WIDE]
        out_mat = blocks[:, 3 * WIDE :]
        packed = blocks.reshape(owners, held, -1)[:, each, :small_len].reshape(-1)

        def widen(values):
            return round_low(dot_rows(values, spread))

        def narrow(values):
            return tail_dot(round_low(values), spread)

        def turned(values, first, second):
            return round_low(dot_rows(values, first)), round_low(dot_rows(values, second))

    else:
        small_width = -(-small_len // LANES)
        qkv_width = w_qkv.shape[0] // LANES
        blocks = jnp.concatenate(
            [w_qkv.reshape(LANES, qkv_width), pack_small(small_params, small_width)], axis=1
        )
        blocks = gather_packed(blocks, core)
        qkv_mat = blocks[..., :qkv_width].reshape(model_width, 3 * model_width)
        qkv_mat = spread_blocks(qkv_mat, model_width)
        packed = blocks[..., qkv_width:].reshape(owners, -1)[:, :small_len].reshape(-1)
        out_mat = gather_packed(w_out.reshape(LANES, -1), core).reshape(model_width, model_width)
        up_mat = gather_packed(w_up.reshape(LANES, -1), core).reshape(model_width, FF)
        down_mat = gather_packed(w_down.reshape(LANES, -1), core).reshape(FF, model_width)

        def widen(values):
            return values

        def narrow(values):
            return values

        def send_sum(left, right, extra=None):
            grad = round_low(lead_dot(left, right)).reshape(groups * 2, 2, LANES, -1)
            if extra is not None:
                extra = extra.reshape(groups * 2, 2, small_len)
                grad = jnp.concatenate([grad, pack_small(extra, small_width)], axis=-1)
            return scatter_packed(grad, core)

    packed = packed.astype(jnp.float32)
    pieces = [packed[number * model_width : (number + 1) * model_width] for number in range(7)]
    gain_one, bias_one, bias_query, bias_value, bias_out, gain_two, bias_two = pieces
    up_bias = packed[7 * model_width : 7 * model_width + FF]
    down_bias = packed[7 * model_width + FF :]

    inputs = inputs.astype(jnp.float32)
    normed_one, inverse_one = layer_stats(inputs)
    act_one = round_low(normed_one * gain_one + bias_one)
    qkv_bias = jnp.concatenate([bias_query, jnp.zeros_like(bias_query), bias_value])
    qkv_bias = spread_blocks(qkv_bias[None, :], model_width)
    own = round_low(dot_rows(widen(act_one), qkv_mat) + qkv_bias)
    other = lax.ppermute(own[:, WIDE:], "core", SWAP)
    if whole_rows:
        one_a, one_b = turned(act_one, turn_a, turn_b)
        one_a, one_b, more_a, more_b = tie((one_a, one_b, more_a, more_b))
        up_a = jnp.concatenate([up_a, more_a], axis=0)
        up_b = jnp.concatenate([up_b, more_b], axis=0)
        more_a, more_b = swap_with(up_a, *order_a[1]), swap_with(up_b, *order_b[1])
        other, one_a, one_b, up_a, up_b = tie((other, one_a, one_b, up_a, up_b))
    mixed, logs = attend(own, other, query_places, key_places)
    if whole_rows:
        mixed, more_a, more_b = tie((mixed, more_a, more_b))
        up_a = double(jnp.concatenate([up_a, more_a], axis=0), *order_a[0])
        up_b = double(jnp.concatenate([up_b, more_b], axis=0), *order_b[0])
        spread_mixed = round_low(dot_rows(mixed, head_spread))
    else:
        spread_mixed = mixed[:, :model_width]
    resid = inputs + dot_rows(spread_mixed, out_mat) + bias_out
    normed_two, inverse_two = layer_stats(resid)
    act_two = round_low(normed_two * gain_two + bias_two)
    if whole_rows:
        two_a, two_b = turned(act_two, turn_a, turn_b)
        gelu_a, slope_a = gate_and_slope(dot_rows(two_a, up_a) + up_bias[:up_cut])
        gelu_b, slope_b = gate_and_slope(dot_rows(two_b, up_b) + up_bias[up_cut:])
        slopes = [round_low(slope_a), round_low(slope_b)]
        gelu_rows = jnp.concatenate([round_low(gelu_a), round_low(gelu_b)], axis=1)
    else:
        gelu_rows, slope = gate_and_slope(dot_rows(act_two, up_mat) + up_bias)
        slopes = [round_low(slope)]
        gelu_rows = round_low(gelu_rows)
    sum_down = outer(gelu_rows, grad_rows)
    gelu_rows, sum_down, slopes = tie((gelu_rows, sum_down, slopes))
    sum_down = sum_down.reshape(owners, -1, model_width)
    sum_down = lax.psum_scatter(sum_down, ALL, scatter_dimension=0, tiled=True)

    grad_float = grad_rows.astype(jnp.float32)
    down_bias_term = jnp.sum(grad_float, axis=0)
    wide = FF // len(slopes)
    grad_pre = [
        round_low(
            tail_dot(grad_rows, down_mat[number * wide : (number + 1) * wide])
            * slope.astype(jnp.float32)
        )
        for number, slope in enumerate(slopes)
    ]
    up_bias_term = jnp.concatenate(
        [jnp.sum(part.astype(jnp.float32), axis=0) for part in grad_pre]
    )
    if whole_rows:
        pre_a, pre_b = grad_pre
        got_a = give_first(two_a, pre_a, order_a)
        got_b = give_first(two_b, pre_b, order_b)
        back_a, back_b = tail_dot(pre_a, up_a), tail_dot(pre_b, up_b)
        back_a, back_b, got_a, got_b = tie((back_a, back_b, got_a, got_b))
        sum_a = keep_first(two_a, pre_a, got_a)
        sum_b = keep_first(two_b, pre_b, got_b)
        back_a, back_b, sum_a, sum_b = tie((back_a, back_b, sum_a, sum_b))
        grad_act_two = tail_dot(round_low(back_a), turn_a) + tail_dot(round_low(back_b), turn_b)
    else:
        sum_up = send_sum(act_two, grad_pre[0])
        grad_act_two = tail_dot(grad_pre[0], up_mat)
    gain_two_term = jnp.sum(grad_act_two * normed_two, axis=0)
    bias_two_term = jnp.sum(grad_act_two, axis=0)
    grad_resid = grad_float + norm_back(grad_act_two, normed_two, inverse_two, gain_two)
    grad_attn = round_low(grad_resid)
    bias_out_term = jnp.sum(grad_attn.astype(jnp.float32), axis=0)
    grad_mixed = round_low(tail_dot(grad_attn, out_mat))
    if whole_rows:
        out_cut = (model_width // 256) * 128
        mixed_a, mixed_b = turned(mixed, head_a, head_b)
        out_got_a = give_first(mixed_a, grad_attn[:, :out_cut], order_a)
        out_got_b = give_first(mixed_b, grad_attn[:, out_cut:], order_b)
        grad_mixed = round_low(tail_dot(grad_mixed, head_spread))
        out_a = keep_first(mixed_a, grad_attn[:, :out_cut], out_got_a)
        out_b = keep_first(mixed_b, grad_attn[:, out_cut:], out_got_b)
        sum_a, sum_b = halve(sum_a, *order_a[1]), halve(sum_b, *order_b[1])
        grad_mixed, out_a, out_b, sum_a, sum_b = tie((grad_mixed, out_a, out_b, sum_a, sum_b))
    else:
        sum_out = send_sum(mixed[:, :model_width], grad_attn)
        grad_mixed = jnp.pad(grad_mixed, [(0, 0), (0, WIDE - model_width)])
    grad_own, grad_other = attend_back(
        own, other, query_places, key_places, mixed, logs, grad_mixed
    )
    grad_qkv_rows = add_received(grad_own, lax.ppermute(grad_other, "core", SWAP))
    if whole_rows:
        sum_a, sum_b = halve(sum_a, *order_a[2]), halve(sum_b, *order_b[2])
        out_a, out_b = halve(out_a, *order_a[1]), halve(out_b, *order_b[1])
        grad_qkv_rows, sum_a, sum_b, out_a, out_b = tie(
            (grad_qkv_rows, sum_a, sum_b, out_a, out_b)
        )
        qkv_cut = (3 * WIDE // 256) * 128
        rows_a, rows_b = grad_qkv_rows[:, :qkv_cut], grad_qkv_rows[:, qkv_cut:]
        qkv_got_a = give_first(one_a, rows_a, order_a)
        qkv_got_b = give_first(one_b, rows_b, order_b)
        sum_up = halve(jnp.concatenate([sum_a, sum_b], axis=1), *order_a[3])
        out_a, out_b = halve(out_a, *order_a[2]), halve(out_b, *order_b[2])
        qkv_a = keep_first(one_a, rows_a, qkv_got_a)
        qkv_b = keep_first(one_b, rows_b, qkv_got_b)
        grad_qkv_rows, qkv_a, qkv_b, sum_up, out_a, out_b, gelu_rows = tie(
            (grad_qkv_rows, qkv_a, qkv_b, sum_up, out_a, out_b, gelu_rows)
        )
    grad_act_one = narrow(tail_dot(grad_qkv_rows, qkv_mat))
    qkv_sums = jnp.sum(grad_qkv_rows.astype(jnp.float32), axis=0)
    gain_one_term = jnp.sum(grad_act_one * normed_one, axis=0)
    bias_one_term = jnp.sum(grad_act_one, axis=0)
    small_grad = jnp.concatenate(
        [
            gain_one_term,
            bias_one_term,
            qkv_sums[:model_width],
            qkv_sums[2 * WIDE : 2 * WIDE + model_width],
            bias_out_term,
            gain_two_term,
            bias_two_term,
            up_bias_term,
            down_bias_term,
        ]
    )
    small_grad = round_low(small_grad)
    grad_input = grad_resid + norm_back(grad_act_one, normed_one, inverse_one, gain_one)
    grad_input = round_low(grad_input)
    outputs = round_low(resid + dot_rows(gelu_rows, down_mat) + down_bias)
    if whole_rows:
        small_rows = round_low(lead_dot(turn_a, small_grad.reshape(model_width, -1)))
        small_rows = halve(small_rows, *order_a[0])
        qkv_a, qkv_b = halve(qkv_a, *order_a[1]), halve(qkv_b, *order_b[1])
        sum_up = halve(sum_up, *order_a[4]) if dp_bits > 2 else sum_up
        sum_out = halve(jnp.concatenate([out_a, out_b], axis=1), *order_a[3])
        grad_input, qkv_a, qkv_b, sum_up, sum_out, small_rows = tie(
            (grad_input, qkv_a, qkv_b, sum_up, sum_out, small_rows)
        )
        qkv_a, qkv_b = halve(qkv_a, *order_a[2]), halve(qkv_b, *order_b[2])
        small_rows = halve(halve(small_rows, *order_a[1]), *order_a[2])
        for step in order_a[5:]:
            sum_up = halve(sum_up, *step)
        for step in order_a[4:]:
            sum_out = halve(sum_out, *step)
        qkv_a, qkv_b, sum_up, sum_out, small_rows, outputs, grad_input = tie(
            (qkv_a, qkv_b, sum_up, sum_out, small_rows, outputs, grad_input)
        )
        sum_qkv = jnp.concatenate([qkv_a, qkv_b, small_rows], axis=1)
        for step in order_a[3:]:
            sum_qkv = halve(sum_qkv, *step)
        grad_qkv = pick_blocks(sum_qkv, model_width)
        grad_small = sum_qkv[:, 3 * WIDE :]
    else:
        sum_qkv = send_sum(act_one, pick_blocks(grad_qkv_rows, model_width), small_grad)
        grad_qkv, grad_small = sum_qkv[:, :qkv_width], sum_qkv[:, qkv_width:]
    result = trade_back(outputs)
    grad_tokens = trade_back(grad_input)
    grad_small = grad_small.astype(jnp.float32).reshape(-1)[:small_len]
    grad_qkv, grad_out, grad_up, grad_down = [
        piece.astype(jnp.float32).reshape(-1) for piece in (grad_qkv, sum_out, sum_up, sum_down)
    ]
    return (result, grad_tokens, grad_qkv, grad_out, grad_up, grad_down, grad_small)


def solution(mesh):
    groups, owners = mesh.shape["dp"], mesh.shape["ctx"]
    fine = Mesh(mesh.devices.reshape(groups, owners // 2, 2), ("dp", "y", "core"))
    rows = P("dp", ("y", "core"), None)
    flat = P(("dp", "y", "core"))
    return jax.shard_map(
        local,
        mesh=fine,
        in_specs=(rows, P("dp", None), flat, flat, flat, flat, flat, rows),
        out_specs=(rows, rows, flat, flat, flat, flat, flat),
        check_vma=False,
    )
```

```python
import jax
import jax.numpy as jnp
from jax import lax
from jax.experimental import pallas as pl
from jax.experimental.pallas import tpu as pltpu
from jax.sharding import Mesh, PartitionSpec as P

HEADS = 17
HEAD_DIM = 64
FF = 4352
LANES = 8
WIDE = 1152
SWAP = ((0, 1), (1, 0))
OWNERS = ("dp", "y")


def layer_stats(values):
    center = values - jnp.mean(values, axis=-1, keepdims=True)
    inverse = lax.rsqrt(jnp.mean(center * center, axis=-1, keepdims=True) + 1e-05)
    return (center * inverse, inverse)


def norm_back(upstream, normed, inverse, gain_vector):
    scaled = upstream * gain_vector
    return inverse * (
        scaled
        - jnp.mean(scaled, axis=-1, keepdims=True)
        - normed * jnp.mean(scaled * normed, axis=-1, keepdims=True)
    )


def lead_dot(left_side, right_side):
    return lax.dot_general(
        left_side, right_side, (((0,), (0,)), ((), ())), preferred_element_type=jnp.float32
    )


def tail_dot(left_side, right_side):
    return lax.dot_general(
        left_side, right_side, (((1,), (1,)), ((), ())), preferred_element_type=jnp.float32
    )


def gate_and_slope(values):
    rate = (2.0 / jnp.pi) ** 0.5
    square = values * values
    bend = jnp.tanh(rate * values * (1.0 + 0.044715 * square))
    share = 0.5 * (1.0 + bend)
    slope = share + 0.5 * values * (1.0 - bend * bend) * rate * (1.0 + 0.134145 * square)
    return values * share, slope


def pack_small(values, width):
    room = LANES * width - values.shape[-1]
    padded = jnp.pad(values, [(0, 0)] * (values.ndim - 1) + [(0, room)])
    return padded.reshape(values.shape[:-1] + (LANES, width))


def gather_packed(block, core):
    own = lax.all_gather(block, OWNERS, axis=0, tiled=True)
    other = lax.ppermute(own, "core", SWAP)
    even = jnp.where(core == 0, own, other)
    odd = jnp.where(core == 0, other, own)
    shape = (-1, 1, LANES, block.shape[1])
    return jnp.concatenate([even.reshape(shape), odd.reshape(shape)], axis=1)


def scatter_packed(packed, core):
    even, odd = packed[:, 0], packed[:, 1]
    keep = jnp.where(core == 0, even, odd)
    give = jnp.where(core == 0, odd, even)
    got = lax.ppermute(give, "core", SWAP)
    pair = (keep.astype(jnp.float32) + got.astype(jnp.float32)).astype(jnp.bfloat16)
    return lax.psum_scatter(pair, OWNERS, scatter_dimension=0, tiled=True)[0]


def dot_rows(left, right):
    return lax.dot_general(
        left, right, (((1,), (0,)), ((), ())), preferred_element_type=jnp.float32
    )


def bias_of(key_places, query_places):
    return jnp.where(key_places <= query_places, 0.0, -1e30).astype(jnp.float32)


def per_pair(one_pair):
    pair = 2 * HEAD_DIM
    full = HEADS // 2

    def step(number, carry):
        one_pair(pl.multiple_of(number * pair, pair), 2 * number, 2)
        return carry

    lax.fori_loop(0, full, step, 0)
    if HEADS % 2:
        one_pair(full * pair, 2 * full, 1)


def lanes_at(start, block):
    return pl.ds(block * WIDE + start, 2 * HEAD_DIM)


def stand(parts):
    if len(parts) == 1:
        parts = parts + [jnp.zeros_like(parts[0])]
    return jnp.concatenate(parts, axis=0).T


def only_head(values, number, heads):
    if heads == 1:
        return values
    lane = lax.broadcasted_iota(jnp.int32, values.shape, 1)
    inside = lane < HEAD_DIM if number == 0 else lane >= HEAD_DIM
    return jnp.where(inside, values, jnp.zeros_like(values))


def join_heads(parts):
    if len(parts) == 1:
        return parts[0]
    lane = lax.broadcasted_iota(jnp.int32, parts[0].shape, 1)
    return jnp.where(lane < HEAD_DIM, parts[0], parts[1])


def attend_kernel(
    own_ref, other_ref, query_ref, key_ref, mixed_ref, log_ref, low_bias, up_bias
):
    half = own_ref.shape[0] // 2
    low_bias[...] = bias_of(key_ref[: 2 * half], query_ref[:, :half])
    up_bias[...] = bias_of(key_ref[2 * half :], query_ref[:, half:])

    def one_pair(start, first, heads):
        q = own_ref[:, lanes_at(start, 0)] * jnp.asarray(HEAD_DIM**-0.5, jnp.bfloat16)
        k_own, v_own = own_ref[:, lanes_at(start, 1)], own_ref[:, lanes_at(start, 2)]
        k_other, v_other = other_ref[:, lanes_at(start, 0)], other_ref[:, lanes_at(start, 1)]
        k_low = jnp.concatenate([k_own[:half], k_other[:half]], axis=0)
        k_up = jnp.concatenate([k_own[half:], k_other[half:]], axis=0)
        v_low = jnp.concatenate([v_own[:half], v_other[:half]], axis=0).T
        v_up = jnp.concatenate([v_own[half:], v_other[half:]], axis=0).T
        low_parts, up_parts = [], []
        for number in range(heads):
            rows = slice(number * HEAD_DIM, (number + 1) * HEAD_DIM)
            q_head = only_head(q, number, heads)
            s = tail_dot(k_low, q_head[:half]) + low_bias[...]
            top = jnp.max(s, axis=0, keepdims=True)
            e = jnp.exp(s - top)
            total = jnp.sum(e, axis=0, keepdims=True)
            mixed = dot_rows(v_low[rows], e.astype(jnp.bfloat16)) / total
            low_parts.append(mixed)
            log_ref[pl.ds(first + number, 1), :half] = top + jnp.log(total)
            s_low = tail_dot(k_low, q_head[half:])
            s_up = tail_dot(k_up, q_head[half:]) + up_bias[...]
            top = jnp.maximum(
                jnp.max(s_low, axis=0, keepdims=True), jnp.max(s_up, axis=0, keepdims=True)
            )
            e_low = jnp.exp(s_low - top)
            e_up = jnp.exp(s_up - top)
            total = jnp.sum(e_low, axis=0, keepdims=True) + jnp.sum(e_up, axis=0, keepdims=True)
            mixed = dot_rows(v_low[rows], e_low.astype(jnp.bfloat16))
            mixed = mixed + dot_rows(v_up[rows], e_up.astype(jnp.bfloat16))
            up_parts.append(mixed / total)
            log_ref[pl.ds(first + number, 1), half:] = top + jnp.log(total)
        mixed_ref[:half, lanes_at(start, 0)] = stand(low_parts).astype(jnp.bfloat16)
        mixed_ref[half:, lanes_at(start, 0)] = stand(up_parts).astype(jnp.bfloat16)

    per_pair(one_pair)


def attend_back_kernel(
    own_ref,
    other_ref,
    query_ref,
    key_ref,
    mixed_ref,
    log_ref,
    grad_ref,
    own_out,
    other_out,
    low_bias,
    up_bias,
):
    half = own_ref.shape[0] // 2
    factor = HEAD_DIM**-0.5
    low_bias[...] = bias_of(key_ref[: 2 * half], query_ref[:, :half])
    up_bias[...] = bias_of(key_ref[2 * half :], query_ref[:, half:])

    def one_pair(start, first, heads):
        lanes = lanes_at(start, 0)
        q = own_ref[:, lanes] * jnp.asarray(factor, jnp.bfloat16)
        grad = grad_ref[:, lanes]
        product = (grad.astype(jnp.float32) * mixed_ref[:, lanes].astype(jnp.float32)).T
        q_heads = [only_head(q, number, heads) for number in range(heads)]
        grad_heads = [only_head(grad, number, heads) for number in range(heads)]
        deltas = [
            jnp.sum(product[number * HEAD_DIM : (number + 1) * HEAD_DIM], axis=0, keepdims=True)
            for number in range(heads)
        ]
        logs = [log_ref[pl.ds(first + number, 1), :] for number in range(heads)]
        dq_low = [None] * heads
        dq_up = [None] * heads
        for source, out, place, block in (
            (own_ref, own_out, 0, 1),
            (other_ref, other_out, 1, 0),
        ):
            klanes, vlanes = lanes_at(start, block), lanes_at(start, block + 1)
            bias_rows = slice(place * half, (place + 1) * half)
            for upper in (False, True):
                rows = slice(half, None) if upper else slice(0, half)
                k = source[rows, klanes]
                v = source[rows, vlanes]
                k_turned = k.T
                dk_parts, dv_parts = [], []
                for number in range(heads):
                    head_rows = slice(number * HEAD_DIM, (number + 1) * HEAD_DIM)
                    first_query = half if upper else 0
                    q_head = q_heads[number][first_query:]
                    grad_head = grad_heads[number][first_query:]
                    s = tail_dot(k, q_head)
                    if upper:
                        s = s + up_bias[bias_rows]
                    else:
                        s = jnp.concatenate([s[:, :half] + low_bias[bias_rows], s[:, half:]], axis=1)
                    p = jnp.exp(s - logs[number][:, first_query:])
                    dp = tail_dot(v, grad_head)
                    ds = (p * (dp - deltas[number][:, first_query:])).astype(jnp.bfloat16)
                    dv_parts.append(dot_rows(p.astype(jnp.bfloat16), grad[first_query:]))
                    dk_parts.append(dot_rows(ds, q[first_query:]))
                    turned = dot_rows(k_turned[head_rows], ds)
                    low = None if upper else turned[:, :half]
                    up = turned if upper else turned[:, half:]
                    if low is not None:
                        dq_low[number] = low if dq_low[number] is None else dq_low[number] + low
                    dq_up[number] = up if dq_up[number] is None else dq_up[number] + up
                out[rows, klanes] = join_heads(dk_parts).astype(jnp.bfloat16)
                out[rows, vlanes] = join_heads(dv_parts).astype(jnp.bfloat16)
        own_out[:half, lanes] = (stand(dq_low) * factor).astype(jnp.bfloat16)
        own_out[half:, lanes] = (stand(dq_up) * factor).astype(jnp.bfloat16)

    per_pair(one_pair)


def add_kernel(own_ref, got_ref, out_ref):
    total = own_ref[...].astype(jnp.float32) + got_ref[...].astype(jnp.float32)
    out_ref[...] = total.astype(out_ref.dtype)


def add_received(own, got):
    rows = own.shape[0]
    block = (rows, WIDE)
    return pl.pallas_call(
        add_kernel,
        grid=(2,),
        in_specs=[
            pl.BlockSpec(block, lambda i: (0, i + 1)),
            pl.BlockSpec(block, lambda i: (0, i)),
        ],
        out_specs=pl.BlockSpec(block, lambda i: (0, i + 1)),
        out_shape=jax.ShapeDtypeStruct(own.shape, own.dtype),
        input_output_aliases={0: 0},
        compiler_params=pltpu.CompilerParams(vmem_limit_bytes=32 * 1024 * 1024),
        cost_estimate=pl.CostEstimate(flops=1 << 20, bytes_accessed=7 << 20, transcendentals=0),
    )(own, got)


def kernel_call(body, outs, half, cost):
    return pl.pallas_call(
        body,
        out_shape=outs,
        scratch_shapes=[pltpu.VMEM((2 * half, half), jnp.float32)] * 2,
        compiler_params=pltpu.CompilerParams(vmem_limit_bytes=48 * 1024 * 1024),
        cost_estimate=pl.CostEstimate(flops=cost, bytes_accessed=12 << 20, transcendentals=cost // 256),
    )


def outer_kernel(left_ref, right_ref, out_ref):
    out_ref[...] = lead_dot(left_ref[...], right_ref[...]).astype(out_ref.dtype)


def outer(left, right):
    rows, count = left.shape
    width = right.shape[1]
    step = 256
    return pl.pallas_call(
        outer_kernel,
        grid=(count // step,),
        in_specs=[
            pl.BlockSpec((rows, step), lambda i: (0, i)),
            pl.BlockSpec((rows, width), lambda i: (0, 0)),
        ],
        out_specs=pl.BlockSpec((step, width), lambda i: (i, 0)),
        out_shape=jax.ShapeDtypeStruct((count, width), jnp.bfloat16),
        compiler_params=pltpu.CompilerParams(vmem_limit_bytes=32 * 1024 * 1024),
        cost_estimate=pl.CostEstimate(
            flops=2 * rows * count * width, bytes_accessed=16 << 20, transcendentals=0
        ),
    )(left, right)


def attend(own, other, query_places, key_places):
    rows = own.shape[0]
    outs = (
        jax.ShapeDtypeStruct((rows, WIDE), jnp.bfloat16),
        jax.ShapeDtypeStruct((HEADS, rows), jnp.float32),
    )
    call = kernel_call(attend_kernel, outs, rows // 2, 1 << 30)
    return call(own, other, query_places, key_places)


def attend_back(own, other, query_places, key_places, mixed, logs, grad):
    outs = (
        jax.ShapeDtypeStruct(own.shape, jnp.bfloat16),
        jax.ShapeDtypeStruct(other.shape, jnp.bfloat16),
    )
    call = kernel_call(attend_back_kernel, outs, own.shape[0] // 2, 1 << 30)
    return call(own, other, query_places, key_places, mixed, logs, grad)


ALL = ("dp", "y", "core")


def round_low(values):
    return values.astype(jnp.bfloat16)


def one_hot_columns(targets, width):
    line = lax.broadcasted_iota(jnp.int32, (width, targets.shape[0]), 0)
    return (line == targets[None, :]).astype(jnp.bfloat16)


def swap_with(values, axis, bit):
    count = lax.axis_size(axis)
    return lax.ppermute(values, axis, [(here, here ^ (1 << bit)) for here in range(count)])


def near_owners(order, dp_bits, each):
    owner = (lax.axis_index("dp") * 2 + lax.axis_index("y")) * 2 + lax.axis_index("core")
    bits = dp_bits + 2
    column = jnp.arange(each << bits, dtype=jnp.int32)
    place, inner = column // each, column % each
    far = jnp.zeros_like(place)
    for number, (axis, bit) in enumerate(order):
        weight = {"core": 0, "y": 1, "dp": 2 + bit}[axis]
        far = far + (((place >> (bits - 1 - number)) & 1) << weight)
    return (owner ^ far) * each + inner


def give_first(left, right, order):
    half = left.shape[1] // 2
    return swap_with(round_low(lead_dot(left[:, half:], right)), *order[0])


def keep_first(left, right, got):
    half = left.shape[1] // 2
    kept = round_low(lead_dot(left[:, :half], right))
    return round_low(kept.astype(jnp.float32) + got.astype(jnp.float32))


def double(values, axis, bit):
    return jnp.concatenate([values, swap_with(values, axis, bit)], axis=0)


tie = lax.optimization_barrier


def send_half(values, axis, bit):
    return swap_with(values[values.shape[0] // 2 :], axis, bit)


def add_half(values, got):
    half = values.shape[0] // 2
    return round_low(values[:half].astype(jnp.float32) + got.astype(jnp.float32))


def halve(values, axis, bit):
    return add_half(values, send_half(values, axis, bit))


def spread_blocks(values, width):
    spare = jnp.zeros((values.shape[0], WIDE - width), values.dtype)
    parts = []
    for number in range(3):
        parts += [values[:, number * width : (number + 1) * width], spare]
    return jnp.concatenate(parts, axis=1)


def pick_blocks(values, width):
    return jnp.concatenate(
        [values[:, number * WIDE : number * WIDE + width] for number in range(3)], axis=1
    )


def local(tokens, positions, w_qkv, w_out, w_up, w_down, small_params, cotangent):
    seqs_here, local_len, model_width = tokens.shape
    span = local_len // 2
    rows = seqs_here * local_len
    half = rows // 2
    y = lax.axis_index("y")
    core = lax.axis_index("core")
    groups = lax.axis_size("dp")
    owners = groups * 4
    small_len = small_params.shape[0]
    whole_rows = model_width % owners == 0
    each = model_width // owners
    dp_bits = groups.bit_length() - 1

    def trade(values):
        mine = lax.dynamic_index_in_dim(values, y, 0, keepdims=False)
        give = lax.dynamic_index_in_dim(values, 1 - y, 0, keepdims=False)
        got = lax.ppermute(give, "y", SWAP)
        return jnp.concatenate([mine[:span], got[:span], mine[span:], got[span:]], axis=0)

    def trade_back(values):
        mine = jnp.concatenate([values[:span], values[half : half + span]], axis=0)
        give = jnp.concatenate([values[span:half], values[half + span :]], axis=0)
        got = lax.ppermute(give, "y", SWAP)
        first = jnp.where(y == 0, mine, got)
        second = jnp.where(y == 0, got, mine)
        return jnp.stack([first, second])

    place_row = lax.dynamic_index_in_dim(positions, y, 0, keepdims=False)

    def places_of(core_index):
        near = lax.dynamic_slice_in_dim(place_row, (2 * y + core_index) * local_len, local_len)
        far = lax.dynamic_slice_in_dim(place_row, (2 - 2 * y + core_index) * local_len, local_len)
        return jnp.concatenate([near[:span], far[:span]]), jnp.concatenate([near[span:], far[span:]])

    own_low, own_up = places_of(core)
    other_low, other_up = places_of(1 - core)
    query_places = jnp.concatenate([own_low, own_up])[None, :]
    key_places = jnp.concatenate([own_low, other_low, own_up, other_up])[:, None]

    inputs = trade(tokens)
    grad_rows = trade(cotangent)
    if whole_rows:
        steps = [("dp", bit) for bit in range(dp_bits)]
        order_a = [("core", 0), steps[0], ("y", 0)] + steps[1:]
        order_b = [("core", 0), ("y", 0), steps[0]] + steps[1:]
        near_a = near_owners(order_a, dp_bits, each)
        near_b = near_owners(order_b, dp_bits, each)
        turn_a = one_hot_columns(near_a, model_width)
        turn_b = one_hot_columns(near_b, model_width)
        head_a = one_hot_columns(near_a, WIDE)
        head_b = one_hot_columns(near_b, WIDE)
        room = -(each + 1) % 8
        held = each + 1 + room
        column = jnp.arange(owners * held, dtype=jnp.int32)
        inside = column % held
        spread = jnp.where(inside < each, column // held * each + inside, -1)
        head_spread = one_hot_columns(spread, WIDE)
        spread = one_hot_columns(spread, model_width)
        blocks = jnp.concatenate(
            [
                spread_blocks(w_qkv.reshape(each, 3 * model_width), model_width),
                w_out.reshape(each, model_width),
            ],
            axis=1,
        )
        extra = jnp.pad(
            small_params.reshape(1, -1), [(0, room), (0, blocks.shape[1] - small_len)]
        )
        blocks = jnp.concatenate([blocks, extra], axis=0)
        blocks = lax.all_gather(blocks, ALL, axis=0, tiled=True)
        down_mat = lax.all_gather(w_down.reshape(-1, model_width), ALL, axis=0, tiled=True)
        up_part = w_up.reshape(each, FF)
        for step in order_a[:2:-1]:
            up_part = double(up_part, *step)
        up_cut = FF // 2
        blocks, up_part, inputs, grad_rows, query_places, key_places, turn_a, turn_b, spread = tie(
            (
                blocks,
                up_part,
                inputs,
                grad_rows,
                query_places,
                key_places,
                turn_a,
                turn_b,
                spread,
            )
        )
        head_a, head_b, head_spread = tie((head_a, head_b, head_spread))
        up_a, up_b = up_part[:, :up_cut], up_part[:, up_cut:]
        more_a, more_b = swap_with(up_a, *order_a[2]), swap_with(up_b, *order_b[2])
        qkv_mat = blocks[:, : 3 * WIDE]
        out_mat = blocks[:, 3 * WIDE :]
        packed = blocks.reshape(owners, held, -1)[:, each, :small_len].reshape(-1)

        def widen(values):
            return round_low(dot_rows(values, spread))

        def narrow(values):
            return tail_dot(round_low(values), spread)

        def turned(values, first, second):
            return round_low(dot_rows(values, first)), round_low(dot_rows(values, second))

    else:
        small_width = -(-small_len // LANES)
        qkv_width = w_qkv.shape[0] // LANES
        blocks = jnp.concatenate(
            [w_qkv.reshape(LANES, qkv_width), pack_small(small_params, small_width)], axis=1
        )
        blocks = gather_packed(blocks, core)
        qkv_mat = blocks[..., :qkv_width].reshape(model_width, 3 * model_width)
        qkv_mat = spread_blocks(qkv_mat, model_width)
        packed = blocks[..., qkv_width:].reshape(owners, -1)[:, :small_len].reshape(-1)
        out_mat = gather_packed(w_out.reshape(LANES, -1), core).reshape(model_width, model_width)
        up_mat = gather_packed(w_up.reshape(LANES, -1), core).reshape(model_width, FF)
        down_mat = gather_packed(w_down.reshape(LANES, -1), core).reshape(FF, model_width)

        def widen(values):
            return values

        def narrow(values):
            return values

        def send_sum(left, right, extra=None):
            grad = round_low(lead_dot(left, right)).reshape(groups * 2, 2, LANES, -1)
            if extra is not None:
                extra = extra.reshape(groups * 2, 2, small_len)
                grad = jnp.concatenate([grad, pack_small(extra, small_width)], axis=-1)
            return scatter_packed(grad, core)

    packed = packed.astype(jnp.float32)
    pieces = [packed[number * model_width : (number + 1) * model_width] for number in range(7)]
    gain_one, bias_one, bias_query, bias_value, bias_out, gain_two, bias_two = pieces
    up_bias = packed[7 * model_width : 7 * model_width + FF]
    down_bias = packed[7 * model_width + FF :]

    inputs = inputs.astype(jnp.float32)
    normed_one, inverse_one = layer_stats(inputs)
    act_one = round_low(normed_one * gain_one + bias_one)
    qkv_bias = jnp.concatenate([bias_query, jnp.zeros_like(bias_query), bias_value])
    qkv_bias = spread_blocks(qkv_bias[None, :], model_width)
    own = round_low(dot_rows(widen(act_one), qkv_mat) + qkv_bias)
    other = lax.ppermute(own[:, WIDE:], "core", SWAP)
    if whole_rows:
        one_a, one_b = turned(act_one, turn_a, turn_b)
        one_a, one_b, more_a, more_b = tie((one_a, one_b, more_a, more_b))
        up_a = jnp.concatenate([up_a, more_a], axis=0)
        up_b = jnp.concatenate([up_b, more_b], axis=0)
        more_a, more_b = swap_with(up_a, *order_a[1]), swap_with(up_b, *order_b[1])
        other, one_a, one_b, up_a, up_b = tie((other, one_a, one_b, up_a, up_b))
    mixed, logs = attend(own, other, query_places, key_places)
    if whole_rows:
        mixed, more_a, more_b = tie((mixed, more_a, more_b))
        up_a = double(jnp.concatenate([up_a, more_a], axis=0), *order_a[0])
        up_b = double(jnp.concatenate([up_b, more_b], axis=0), *order_b[0])
        spread_mixed = round_low(dot_rows(mixed, head_spread))
    else:
        spread_mixed = mixed[:, :model_width]
    resid = inputs + dot_rows(spread_mixed, out_mat) + bias_out
    normed_two, inverse_two = layer_stats(resid)
    act_two = round_low(normed_two * gain_two + bias_two)
    if whole_rows:
        two_a, two_b = turned(act_two, turn_a, turn_b)
        gelu_a, slope_a = gate_and_slope(dot_rows(two_a, up_a) + up_bias[:up_cut])
        gelu_b, slope_b = gate_and_slope(dot_rows(two_b, up_b) + up_bias[up_cut:])
        slopes = [round_low(slope_a), round_low(slope_b)]
        gelu_rows = jnp.concatenate([round_low(gelu_a), round_low(gelu_b)], axis=1)
    else:
        gelu_rows, slope = gate_and_slope(dot_rows(act_two, up_mat) + up_bias)
        slopes = [round_low(slope)]
        gelu_rows = round_low(gelu_rows)
    sum_down = outer(gelu_rows, grad_rows)
    gelu_rows, sum_down, slopes = tie((gelu_rows, sum_down, slopes))
    sum_down = sum_down.reshape(owners, -1, model_width)
    sum_down = lax.psum_scatter(sum_down, ALL, scatter_dimension=0, tiled=True)

    grad_float = grad_rows.astype(jnp.float32)
    down_bias_term = jnp.sum(grad_float, axis=0)
    wide = FF // len(slopes)
    grad_pre = [
        round_low(
            tail_dot(grad_rows, down_mat[number * wide : (number + 1) * wide])
            * slope.astype(jnp.float32)
        )
        for number, slope in enumerate(slopes)
    ]
    up_bias_term = jnp.concatenate(
        [jnp.sum(part.astype(jnp.float32), axis=0) for part in grad_pre]
    )
    if whole_rows:
        pre_a, pre_b = grad_pre
        got_a = give_first(two_a, pre_a, order_a)
        got_b = give_first(two_b, pre_b, order_b)
        back_a, back_b = tail_dot(pre_a, up_a), tail_dot(pre_b, up_b)
        back_a, back_b, got_a, got_b = tie((back_a, back_b, got_a, got_b))
        sum_a = keep_first(two_a, pre_a, got_a)
        sum_b = keep_first(two_b, pre_b, got_b)
        back_a, back_b, sum_a, sum_b = tie((back_a, back_b, sum_a, sum_b))
        grad_act_two = tail_dot(round_low(back_a), turn_a) + tail_dot(round_low(back_b), turn_b)
    else:
        sum_up = send_sum(act_two, grad_pre[0])
        grad_act_two = tail_dot(grad_pre[0], up_mat)
    gain_two_term = jnp.sum(grad_act_two * normed_two, axis=0)
    bias_two_term = jnp.sum(grad_act_two, axis=0)
    grad_resid = grad_float + norm_back(grad_act_two, normed_two, inverse_two, gain_two)
    grad_attn = round_low(grad_resid)
    bias_out_term = jnp.sum(grad_attn.astype(jnp.float32), axis=0)
    grad_mixed = round_low(tail_dot(grad_attn, out_mat))
    if whole_rows:
        out_cut = (model_width // 256) * 128
        mixed_a, mixed_b = turned(mixed, head_a, head_b)
        out_got_a = give_first(mixed_a, grad_attn[:, :out_cut], order_a)
        out_got_b = give_first(mixed_b, grad_attn[:, out_cut:], order_b)
        grad_mixed = round_low(tail_dot(grad_mixed, head_spread))
        out_a = keep_first(mixed_a, grad_attn[:, :out_cut], out_got_a)
        out_b = keep_first(mixed_b, grad_attn[:, out_cut:], out_got_b)
        grad_mixed, out_a, out_b = tie((grad_mixed, out_a, out_b))
        got_a, got_b = send_half(sum_a, *order_a[1]), send_half(sum_b, *order_b[1])
        out_got_a, out_got_b = send_half(out_a, *order_a[1]), send_half(out_b, *order_b[1])
    else:
        sum_out = send_sum(mixed[:, :model_width], grad_attn)
        grad_mixed = jnp.pad(grad_mixed, [(0, 0), (0, WIDE - model_width)])
    grad_own, grad_other = attend_back(
        own, other, query_places, key_places, mixed, logs, grad_mixed
    )
    grad_got = lax.ppermute(grad_other, "core", SWAP)
    if whole_rows:
        grad_own, got_a, got_b, out_got_a, out_got_b = tie(
            (grad_own, got_a, got_b, out_got_a, out_got_b)
        )
        sum_a, sum_b = add_half(sum_a, got_a), add_half(sum_b, got_b)
        out_a, out_b = add_half(out_a, out_got_a), add_half(out_b, out_got_b)
        rest_a = jnp.concatenate([sum_a, out_a], axis=1)
        rest_b = jnp.concatenate([sum_b, out_b], axis=1)
        got_a, got_b = send_half(rest_a, *order_a[2]), send_half(rest_b, *order_b[2])
    grad_qkv_rows = add_received(grad_own, grad_got)
    if whole_rows:
        qkv_cut = (3 * WIDE // 256) * 128
        rows_a, rows_b = grad_qkv_rows[:, :qkv_cut], grad_qkv_rows[:, qkv_cut:]
        qkv_got_a = give_first(one_a, rows_a, order_a)
        qkv_got_b = give_first(one_b, rows_b, order_b)
        qkv_a = keep_first(one_a, rows_a, qkv_got_a)
        qkv_b = keep_first(one_b, rows_b, qkv_got_b)
        grad_qkv_rows, qkv_a, qkv_b, got_a, got_b, gelu_rows, sum_down = tie(
            (grad_qkv_rows, qkv_a, qkv_b, got_a, got_b, gelu_rows, sum_down)
        )
        rest = jnp.concatenate([add_half(rest_a, got_a), add_half(rest_b, got_b)], axis=1)
        qkv_got_a = send_half(qkv_a, *order_a[1])
        qkv_got_b = send_half(qkv_b, *order_b[1])
        rest_got = send_half(rest, *order_a[3])
    grad_act_one = tail_dot(grad_qkv_rows, qkv_mat)
    if whole_rows:
        grad_act_one, qkv_got_a, qkv_got_b, rest_got = tie(
            (grad_act_one, qkv_got_a, qkv_got_b, rest_got)
        )
        qkv_a, qkv_b = add_half(qkv_a, qkv_got_a), add_half(qkv_b, qkv_got_b)
        qkv_got_a = send_half(qkv_a, *order_a[2])
        qkv_got_b = send_half(qkv_b, *order_b[2])
        rest = add_half(rest, rest_got)
        rest_got = send_half(rest, *order_a[4])
    grad_act_one = narrow(grad_act_one)
    qkv_sums = jnp.sum(grad_qkv_rows.astype(jnp.float32), axis=0)
    gain_one_term = jnp.sum(grad_act_one * normed_one, axis=0)
    bias_one_term = jnp.sum(grad_act_one, axis=0)
    small_grad = jnp.concatenate(
        [
            gain_one_term,
            bias_one_term,
            qkv_sums[:model_width],
            qkv_sums[2 * WIDE : 2 * WIDE + model_width],
            bias_out_term,
            gain_two_term,
            bias_two_term,
            up_bias_term,
            down_bias_term,
        ]
    )
    small_grad = round_low(small_grad)
    grad_input = grad_resid + norm_back(grad_act_one, normed_one, inverse_one, gain_one)
    grad_input = round_low(grad_input)
    outputs = round_low(resid + dot_rows(gelu_rows, down_mat) + down_bias)
    if whole_rows:
        small_rows = round_low(lead_dot(turn_a, small_grad.reshape(model_width, -1)))
        grad_input, outputs, qkv_got_a, qkv_got_b, rest_got = tie(
            (grad_input, outputs, qkv_got_a, qkv_got_b, rest_got)
        )
        qkv_a, qkv_b = add_half(qkv_a, qkv_got_a), add_half(qkv_b, qkv_got_b)
        sum_qkv = jnp.concatenate([qkv_a, qkv_b], axis=1)
        sum_qkv = halve(sum_qkv, *order_a[3])
        rest = add_half(rest, rest_got)
        for step in order_a[5:]:
            rest = halve(rest, *step)
        for step in order_a[:4]:
            small_rows = halve(small_rows, *step)
        sum_qkv = jnp.concatenate([sum_qkv, small_rows], axis=1)
        for step in order_a[4:]:
            sum_qkv = halve(sum_qkv, *step)
        sides = [up_cut, up_cut + out_cut, FF + out_cut]
        sum_up = jnp.concatenate([rest[:, : sides[0]], rest[:, sides[1] : sides[2]]], axis=1)
        sum_out = jnp.concatenate([rest[:, sides[0] : sides[1]], rest[:, sides[2] :]], axis=1)
        grad_qkv = pick_blocks(sum_qkv, model_width)
        grad_small = sum_qkv[:, 3 * WIDE :]
    else:
        sum_qkv = send_sum(act_one, pick_blocks(grad_qkv_rows, model_width), small_grad)
        grad_qkv, grad_small = sum_qkv[:, :qkv_width], sum_qkv[:, qkv_width:]
    result = trade_back(outputs)
    grad_tokens = trade_back(grad_input)
    grad_small = grad_small.astype(jnp.float32).reshape(-1)[:small_len]
    grad_qkv, grad_out, grad_up, grad_down = [
        piece.astype(jnp.float32).reshape(-1) for piece in (grad_qkv, sum_out, sum_up, sum_down)
    ]
    return (result, grad_tokens, grad_qkv, grad_out, grad_up, grad_down, grad_small)


def solution(mesh):
    groups, owners = mesh.shape["dp"], mesh.shape["ctx"]
    fine = Mesh(mesh.devices.reshape(groups, owners // 2, 2), ("dp", "y", "core"))
    rows = P("dp", ("y", "core"), None)
    flat = P(("dp", "y", "core"))
    return jax.shard_map(
        local,
        mesh=fine,
        in_specs=(rows, P("dp", None), flat, flat, flat, flat, flat, rows),
        out_specs=(rows, rows, flat, flat, flat, flat, flat),
        check_vma=False,
    )
```

```python
import jax
import jax.numpy as jnp
from jax import lax
from jax.experimental import pallas as pl
from jax.experimental.pallas import tpu as pltpu
from jax.sharding import Mesh, PartitionSpec as P

HEADS = 17
HEAD_DIM = 64
FF = 4352
LANES = 8
WIDE = 1152
SWAP = ((0, 1), (1, 0))
OWNERS = ("dp", "y")


def layer_stats(values):
    center = values - jnp.mean(values, axis=-1, keepdims=True)
    inverse = lax.rsqrt(jnp.mean(center * center, axis=-1, keepdims=True) + 1e-05)
    return (center * inverse, inverse)


def norm_back(upstream, normed, inverse, gain_vector):
    scaled = upstream * gain_vector
    return inverse * (
        scaled
        - jnp.mean(scaled, axis=-1, keepdims=True)
        - normed * jnp.mean(scaled * normed, axis=-1, keepdims=True)
    )


def lead_dot(left_side, right_side):
    return lax.dot_general(
        left_side, right_side, (((0,), (0,)), ((), ())), preferred_element_type=jnp.float32
    )


def tail_dot(left_side, right_side):
    return lax.dot_general(
        left_side, right_side, (((1,), (1,)), ((), ())), preferred_element_type=jnp.float32
    )


def gate_and_slope(values):
    rate = (2.0 / jnp.pi) ** 0.5
    square = values * values
    bend = jnp.tanh(rate * values * (1.0 + 0.044715 * square))
    share = 0.5 * (1.0 + bend)
    slope = share + 0.5 * values * (1.0 - bend * bend) * rate * (1.0 + 0.134145 * square)
    return values * share, slope


def pack_small(values, width):
    room = LANES * width - values.shape[-1]
    padded = jnp.pad(values, [(0, 0)] * (values.ndim - 1) + [(0, room)])
    return padded.reshape(values.shape[:-1] + (LANES, width))


def gather_packed(block, core):
    own = lax.all_gather(block, OWNERS, axis=0, tiled=True)
    other = lax.ppermute(own, "core", SWAP)
    even = jnp.where(core == 0, own, other)
    odd = jnp.where(core == 0, other, own)
    shape = (-1, 1, LANES, block.shape[1])
    return jnp.concatenate([even.reshape(shape), odd.reshape(shape)], axis=1)


def scatter_packed(packed, core):
    even, odd = packed[:, 0], packed[:, 1]
    keep = jnp.where(core == 0, even, odd)
    give = jnp.where(core == 0, odd, even)
    got = lax.ppermute(give, "core", SWAP)
    pair = (keep.astype(jnp.float32) + got.astype(jnp.float32)).astype(jnp.bfloat16)
    return lax.psum_scatter(pair, OWNERS, scatter_dimension=0, tiled=True)[0]


def dot_rows(left, right):
    return lax.dot_general(
        left, right, (((1,), (0,)), ((), ())), preferred_element_type=jnp.float32
    )


def bias_of(key_places, query_places):
    return jnp.where(key_places <= query_places, 0.0, -1e30).astype(jnp.float32)


def per_pair(one_pair):
    pair = 2 * HEAD_DIM
    full = HEADS // 2

    def step(number, carry):
        one_pair(pl.multiple_of(number * pair, pair), 2 * number, 2)
        return carry

    lax.fori_loop(0, full, step, 0)
    if HEADS % 2:
        one_pair(full * pair, 2 * full, 1)


def lanes_at(start, block):
    return pl.ds(block * WIDE + start, 2 * HEAD_DIM)


def stand(parts):
    if len(parts) == 1:
        parts = parts + [jnp.zeros_like(parts[0])]
    return jnp.concatenate(parts, axis=0).T


def only_head(values, number, heads):
    if heads == 1:
        return values
    lane = lax.broadcasted_iota(jnp.int32, values.shape, 1)
    inside = lane < HEAD_DIM if number == 0 else lane >= HEAD_DIM
    return jnp.where(inside, values, jnp.zeros_like(values))


def join_heads(parts):
    if len(parts) == 1:
        return parts[0]
    lane = lax.broadcasted_iota(jnp.int32, parts[0].shape, 1)
    return jnp.where(lane < HEAD_DIM, parts[0], parts[1])


def attend_kernel(
    own_ref, other_ref, query_ref, key_ref, mixed_ref, log_ref, low_bias, up_bias
):
    half = own_ref.shape[0] // 2
    low_bias[...] = bias_of(key_ref[: 2 * half], query_ref[:, :half])
    up_bias[...] = bias_of(key_ref[2 * half :], query_ref[:, half:])

    def one_pair(start, first, heads):
        q = own_ref[:, lanes_at(start, 0)] * jnp.asarray(HEAD_DIM**-0.5, jnp.bfloat16)
        k_own, v_own = own_ref[:, lanes_at(start, 1)], own_ref[:, lanes_at(start, 2)]
        k_other, v_other = other_ref[:, lanes_at(start, 0)], other_ref[:, lanes_at(start, 1)]
        k_low = jnp.concatenate([k_own[:half], k_other[:half]], axis=0)
        k_up = jnp.concatenate([k_own[half:], k_other[half:]], axis=0)
        v_low = jnp.concatenate([v_own[:half], v_other[:half]], axis=0).T
        v_up = jnp.concatenate([v_own[half:], v_other[half:]], axis=0).T
        low_parts, up_parts = [], []
        for number in range(heads):
            rows = slice(number * HEAD_DIM, (number + 1) * HEAD_DIM)
            q_head = only_head(q, number, heads)
            s = tail_dot(k_low, q_head[:half]) + low_bias[...]
            top = jnp.max(s, axis=0, keepdims=True)
            e = jnp.exp(s - top)
            total = jnp.sum(e, axis=0, keepdims=True)
            mixed = dot_rows(v_low[rows], e.astype(jnp.bfloat16)) / total
            low_parts.append(mixed)
            log_ref[pl.ds(first + number, 1), :half] = top + jnp.log(total)
            s_low = tail_dot(k_low, q_head[half:])
            s_up = tail_dot(k_up, q_head[half:]) + up_bias[...]
            top = jnp.maximum(
                jnp.max(s_low, axis=0, keepdims=True), jnp.max(s_up, axis=0, keepdims=True)
            )
            e_low = jnp.exp(s_low - top)
            e_up = jnp.exp(s_up - top)
            total = jnp.sum(e_low, axis=0, keepdims=True) + jnp.sum(e_up, axis=0, keepdims=True)
            mixed = dot_rows(v_low[rows], e_low.astype(jnp.bfloat16))
            mixed = mixed + dot_rows(v_up[rows], e_up.astype(jnp.bfloat16))
            up_parts.append(mixed / total)
            log_ref[pl.ds(first + number, 1), half:] = top + jnp.log(total)
        mixed_ref[:half, lanes_at(start, 0)] = stand(low_parts).astype(jnp.bfloat16)
        mixed_ref[half:, lanes_at(start, 0)] = stand(up_parts).astype(jnp.bfloat16)

    per_pair(one_pair)


def attend_back_kernel(
    own_ref,
    other_ref,
    query_ref,
    key_ref,
    mixed_ref,
    log_ref,
    grad_ref,
    own_out,
    other_out,
    low_bias,
    up_bias,
):
    half = own_ref.shape[0] // 2
    factor = HEAD_DIM**-0.5
    low_bias[...] = bias_of(key_ref[: 2 * half], query_ref[:, :half])
    up_bias[...] = bias_of(key_ref[2 * half :], query_ref[:, half:])

    def one_pair(start, first, heads):
        lanes = lanes_at(start, 0)
        q = own_ref[:, lanes] * jnp.asarray(factor, jnp.bfloat16)
        grad = grad_ref[:, lanes]
        product = (grad.astype(jnp.float32) * mixed_ref[:, lanes].astype(jnp.float32)).T
        q_heads = [only_head(q, number, heads) for number in range(heads)]
        grad_heads = [only_head(grad, number, heads) for number in range(heads)]
        deltas = [
            jnp.sum(product[number * HEAD_DIM : (number + 1) * HEAD_DIM], axis=0, keepdims=True)
            for number in range(heads)
        ]
        logs = [log_ref[pl.ds(first + number, 1), :] for number in range(heads)]
        dq_low = [None] * heads
        dq_up = [None] * heads
        for source, out, place, block in (
            (own_ref, own_out, 0, 1),
            (other_ref, other_out, 1, 0),
        ):
            klanes, vlanes = lanes_at(start, block), lanes_at(start, block + 1)
            bias_rows = slice(place * half, (place + 1) * half)
            for upper in (False, True):
                rows = slice(half, None) if upper else slice(0, half)
                k = source[rows, klanes]
                v = source[rows, vlanes]
                k_turned = k.T
                dk_parts, dv_parts = [], []
                for number in range(heads):
                    head_rows = slice(number * HEAD_DIM, (number + 1) * HEAD_DIM)
                    first_query = half if upper else 0
                    q_head = q_heads[number][first_query:]
                    grad_head = grad_heads[number][first_query:]
                    s = tail_dot(k, q_head)
                    if upper:
                        s = s + up_bias[bias_rows]
                    else:
                        s = jnp.concatenate([s[:, :half] + low_bias[bias_rows], s[:, half:]], axis=1)
                    p = jnp.exp(s - logs[number][:, first_query:])
                    dp = tail_dot(v, grad_head)
                    ds = (p * (dp - deltas[number][:, first_query:])).astype(jnp.bfloat16)
                    dv_parts.append(dot_rows(p.astype(jnp.bfloat16), grad[first_query:]))
                    dk_parts.append(dot_rows(ds, q[first_query:]))
                    turned = dot_rows(k_turned[head_rows], ds)
                    low = None if upper else turned[:, :half]
                    up = turned if upper else turned[:, half:]
                    if low is not None:
                        dq_low[number] = low if dq_low[number] is None else dq_low[number] + low
                    dq_up[number] = up if dq_up[number] is None else dq_up[number] + up
                out[rows, klanes] = join_heads(dk_parts).astype(jnp.bfloat16)
                out[rows, vlanes] = join_heads(dv_parts).astype(jnp.bfloat16)
        own_out[:half, lanes] = (stand(dq_low) * factor).astype(jnp.bfloat16)
        own_out[half:, lanes] = (stand(dq_up) * factor).astype(jnp.bfloat16)

    per_pair(one_pair)


def add_kernel(own_ref, got_ref, out_ref):
    total = own_ref[...].astype(jnp.float32) + got_ref[...].astype(jnp.float32)
    out_ref[...] = total.astype(out_ref.dtype)


def add_received(own, got):
    rows = own.shape[0]
    block = (rows, WIDE)
    return pl.pallas_call(
        add_kernel,
        grid=(2,),
        in_specs=[
            pl.BlockSpec(block, lambda i: (0, i + 1)),
            pl.BlockSpec(block, lambda i: (0, i)),
        ],
        out_specs=pl.BlockSpec(block, lambda i: (0, i + 1)),
        out_shape=jax.ShapeDtypeStruct(own.shape, own.dtype),
        input_output_aliases={0: 0},
        compiler_params=pltpu.CompilerParams(vmem_limit_bytes=32 * 1024 * 1024),
        cost_estimate=pl.CostEstimate(flops=1 << 20, bytes_accessed=7 << 20, transcendentals=0),
    )(own, got)


def kernel_call(body, outs, half, cost):
    return pl.pallas_call(
        body,
        out_shape=outs,
        scratch_shapes=[pltpu.VMEM((2 * half, half), jnp.float32)] * 2,
        compiler_params=pltpu.CompilerParams(vmem_limit_bytes=48 * 1024 * 1024),
        cost_estimate=pl.CostEstimate(flops=cost, bytes_accessed=12 << 20, transcendentals=cost // 256),
    )


def outer_kernel(left_ref, right_ref, first_ref, second_ref):
    part = lead_dot(left_ref[...], right_ref[...]).astype(first_ref.dtype)
    cut = first_ref.shape[1]
    first_ref[...] = part[:, :cut]
    second_ref[...] = part[:, cut:]


def outer(left, right):
    rows, count = left.shape
    width = right.shape[1]
    step = 256
    cut = (width // 256) * 128
    return pl.pallas_call(
        outer_kernel,
        grid=(count // step,),
        in_specs=[
            pl.BlockSpec((rows, step), lambda i: (0, i)),
            pl.BlockSpec((rows, width), lambda i: (0, 0)),
        ],
        out_specs=[
            pl.BlockSpec((step, cut), lambda i: (i, 0)),
            pl.BlockSpec((step, width - cut), lambda i: (i, 0)),
        ],
        out_shape=[
            jax.ShapeDtypeStruct((count, cut), jnp.bfloat16),
            jax.ShapeDtypeStruct((count, width - cut), jnp.bfloat16),
        ],
        compiler_params=pltpu.CompilerParams(vmem_limit_bytes=32 * 1024 * 1024),
        cost_estimate=pl.CostEstimate(
            flops=2 * rows * count * width, bytes_accessed=16 << 20, transcendentals=0
        ),
    )(left, right)


def input_grad_kernel(
    rows_ref,
    mat_ref,
    spread_ref,
    input_ref,
    gain_ref,
    resid_ref,
    out_ref,
    gain_out,
    bias_out,
    total,
):
    step = pl.program_id(0)
    part = tail_dot(rows_ref[...], mat_ref[...])

    @pl.when(step == 0)
    def _():
        total[...] = part

    @pl.when(step > 0)
    def _():
        total[...] += part

    @pl.when(step == pl.num_programs(0) - 1)
    def _():
        back = tail_dot(total[...].astype(jnp.bfloat16), spread_ref[...])
        normed, inverse = layer_stats(input_ref[...].astype(jnp.float32))
        gain_out[...] = jnp.sum(back * normed, axis=0, keepdims=True)
        bias_out[...] = jnp.sum(back, axis=0, keepdims=True)
        grad = resid_ref[...] + norm_back(back, normed, inverse, gain_ref[...])
        out_ref[...] = grad.astype(out_ref.dtype)


def input_grad(rows, mat, spread, inputs, gain, resid):
    count, width = inputs.shape
    held = mat.shape[0]
    step = 384

    def fixed(shape):
        return pl.BlockSpec(shape, lambda i: (0, 0))

    return pl.pallas_call(
        input_grad_kernel,
        grid=(3 * WIDE // step,),
        in_specs=[
            pl.BlockSpec((count, step), lambda i: (0, i)),
            pl.BlockSpec((held, step), lambda i: (0, i)),
            fixed((width, held)),
            fixed((count, width)),
            fixed((1, width)),
            fixed((count, width)),
        ],
        out_specs=[fixed((count, width)), fixed((1, width)), fixed((1, width))],
        out_shape=[
            jax.ShapeDtypeStruct((count, width), jnp.bfloat16),
            jax.ShapeDtypeStruct((1, width), jnp.float32),
            jax.ShapeDtypeStruct((1, width), jnp.float32),
        ],
        scratch_shapes=[pltpu.VMEM((count, held), jnp.float32)],
        compiler_params=pltpu.CompilerParams(vmem_limit_bytes=48 * 1024 * 1024),
        cost_estimate=pl.CostEstimate(flops=14 << 30, bytes_accessed=20 << 20, transcendentals=0),
    )(rows, mat, spread, inputs, gain, resid)


def project_kernel(left_ref, mat_ref, resid_ref, bias_ref, out_ref, total):
    step = pl.program_id(0)
    part = dot_rows(left_ref[...], mat_ref[...])

    @pl.when(step == 0)
    def _():
        total[...] = resid_ref[...] + bias_ref[...] + part

    @pl.when(step > 0)
    def _():
        total[...] += part

    @pl.when(step == pl.num_programs(0) - 1)
    def _():
        out_ref[...] = total[...].astype(out_ref.dtype)


def project(left, mat, resid, bias):
    count, depth = left.shape
    width = mat.shape[1]
    step = 256

    def fixed(shape):
        return pl.BlockSpec(shape, lambda i: (0, 0))

    return pl.pallas_call(
        project_kernel,
        grid=(depth // step,),
        in_specs=[
            pl.BlockSpec((count, step), lambda i: (0, i)),
            pl.BlockSpec((step, width), lambda i: (i, 0)),
            fixed((count, width)),
            fixed((1, width)),
        ],
        out_specs=fixed((count, width)),
        out_shape=jax.ShapeDtypeStruct((count, width), jnp.bfloat16),
        scratch_shapes=[pltpu.VMEM((count, width), jnp.float32)],
        compiler_params=pltpu.CompilerParams(vmem_limit_bytes=32 * 1024 * 1024),
        cost_estimate=pl.CostEstimate(flops=14 << 30, bytes_accessed=20 << 20, transcendentals=0),
    )(left, mat, resid, bias)


def attend(own, other, query_places, key_places):
    rows = own.shape[0]
    outs = (
        jax.ShapeDtypeStruct((rows, WIDE), jnp.bfloat16),
        jax.ShapeDtypeStruct((HEADS, rows), jnp.float32),
    )
    call = kernel_call(attend_kernel, outs, rows // 2, 20 << 30)
    return call(own, other, query_places, key_places)


def attend_back(own, other, query_places, key_places, mixed, logs, grad):
    outs = (
        jax.ShapeDtypeStruct(own.shape, jnp.bfloat16),
        jax.ShapeDtypeStruct(other.shape, jnp.bfloat16),
    )
    call = kernel_call(attend_back_kernel, outs, own.shape[0] // 2, 30 << 30)
    return call(own, other, query_places, key_places, mixed, logs, grad)


ALL = ("dp", "y", "core")


def round_low(values):
    return values.astype(jnp.bfloat16)


def one_hot_columns(targets, width):
    line = lax.broadcasted_iota(jnp.int32, (width, targets.shape[0]), 0)
    return (line == targets[None, :]).astype(jnp.bfloat16)


def swap_with(values, axis, bit):
    count = lax.axis_size(axis)
    return lax.ppermute(values, axis, [(here, here ^ (1 << bit)) for here in range(count)])


def near_owners(order, dp_bits, each):
    owner = (lax.axis_index("dp") * 2 + lax.axis_index("y")) * 2 + lax.axis_index("core")
    bits = dp_bits + 2
    column = jnp.arange(each << bits, dtype=jnp.int32)
    place, inner = column // each, column % each
    far = jnp.zeros_like(place)
    for number, (axis, bit) in enumerate(order):
        weight = {"core": 0, "y": 1, "dp": 2 + bit}[axis]
        far = far + (((place >> (bits - 1 - number)) & 1) << weight)
    return (owner ^ far) * each + inner


def give_first(left, right, order):
    half = left.shape[1] // 2
    return swap_with(round_low(lead_dot(left[:, half:], right)), *order[0])


def keep_first(left, right, got):
    half = left.shape[1] // 2
    kept = round_low(lead_dot(left[:, :half], right))
    return round_low(kept.astype(jnp.float32) + got.astype(jnp.float32))


def double(values, axis, bit):
    return jnp.concatenate([values, swap_with(values, axis, bit)], axis=0)


tie = lax.optimization_barrier


def send_half(values, axis, bit):
    return swap_with(values[values.shape[0] // 2 :], axis, bit)


def add_half(values, got):
    half = values.shape[0] // 2
    return round_low(values[:half].astype(jnp.float32) + got.astype(jnp.float32))


def halve(values, axis, bit):
    return add_half(values, send_half(values, axis, bit))


def spread_blocks(values, width):
    spare = jnp.zeros((values.shape[0], WIDE - width), values.dtype)
    parts = []
    for number in range(3):
        parts += [values[:, number * width : (number + 1) * width], spare]
    return jnp.concatenate(parts, axis=1)


def pick_blocks(values, width):
    return jnp.concatenate(
        [values[:, number * WIDE : number * WIDE + width] for number in range(3)], axis=1
    )


def local(tokens, positions, w_qkv, w_out, w_up, w_down, small_params, cotangent):
    seqs_here, local_len, model_width = tokens.shape
    span = local_len // 2
    rows = seqs_here * local_len
    half = rows // 2
    y = lax.axis_index("y")
    core = lax.axis_index("core")
    groups = lax.axis_size("dp")
    owners = groups * 4
    small_len = small_params.shape[0]
    whole_rows = model_width % owners == 0
    each = model_width // owners
    dp_bits = groups.bit_length() - 1

    def trade(values):
        mine = lax.dynamic_index_in_dim(values, y, 0, keepdims=False)
        give = lax.dynamic_index_in_dim(values, 1 - y, 0, keepdims=False)
        got = lax.ppermute(give, "y", SWAP)
        return jnp.concatenate([mine[:span], got[:span], mine[span:], got[span:]], axis=0)

    def trade_out(values):
        return lax.ppermute(
            jnp.concatenate([values[span:half], values[half + span :]], axis=0), "y", SWAP
        )

    def trade_join(values, got):
        mine = jnp.concatenate([values[:span], values[half : half + span]], axis=0)
        first = jnp.where(y == 0, mine, got)
        second = jnp.where(y == 0, got, mine)
        return jnp.stack([first, second])

    place_row = lax.dynamic_index_in_dim(positions, y, 0, keepdims=False)

    def places_of(core_index):
        near = lax.dynamic_slice_in_dim(place_row, (2 * y + core_index) * local_len, local_len)
        far = lax.dynamic_slice_in_dim(place_row, (2 - 2 * y + core_index) * local_len, local_len)
        return jnp.concatenate([near[:span], far[:span]]), jnp.concatenate([near[span:], far[span:]])

    own_low, own_up = places_of(core)
    other_low, other_up = places_of(1 - core)
    query_places = jnp.concatenate([own_low, own_up])[None, :]
    key_places = jnp.concatenate([own_low, other_low, own_up, other_up])[:, None]

    inputs = trade(tokens)
    grad_rows = trade(cotangent)
    if whole_rows:
        steps = [("dp", bit) for bit in range(dp_bits)]
        order_a = [("core", 0), steps[0], ("y", 0)] + steps[1:]
        order_b = [("core", 0), ("y", 0), steps[0]] + steps[1:]
        near_a = near_owners(order_a, dp_bits, each)
        near_b = near_owners(order_b, dp_bits, each)
        turn_a = one_hot_columns(near_a, model_width)
        turn_b = one_hot_columns(near_b, model_width)
        head_a = one_hot_columns(near_a, WIDE)
        head_b = one_hot_columns(near_b, WIDE)
        room = -(each + 1) % 8
        held = each + 1 + room
        column = jnp.arange(owners * held, dtype=jnp.int32)
        inside = column % held
        spread = jnp.where(inside < each, column // held * each + inside, -1)
        head_spread = one_hot_columns(spread, WIDE)
        spread = one_hot_columns(spread, model_width)
        blocks = jnp.concatenate(
            [
                spread_blocks(w_qkv.reshape(each, 3 * model_width), model_width),
                w_out.reshape(each, model_width),
            ],
            axis=1,
        )
        extra = jnp.pad(
            small_params.reshape(1, -1), [(0, room), (0, blocks.shape[1] - small_len)]
        )
        blocks = jnp.concatenate([blocks, extra], axis=0)
        blocks = lax.all_gather(blocks, ALL, axis=0, tiled=True)
        down_mat = lax.all_gather(w_down.reshape(-1, model_width), ALL, axis=0, tiled=True)
        up_part = w_up.reshape(each, FF)
        for step in order_a[:2:-1]:
            up_part = double(up_part, *step)
        up_cut = FF // 2
        blocks, up_part, inputs, grad_rows, query_places, key_places, turn_a, turn_b, spread = tie(
            (
                blocks,
                up_part,
                inputs,
                grad_rows,
                query_places,
                key_places,
                turn_a,
                turn_b,
                spread,
            )
        )
        head_a, head_b, head_spread = tie((head_a, head_b, head_spread))
        up_a, up_b = up_part[:, :up_cut], up_part[:, up_cut:]
        more_a, more_b = swap_with(up_a, *order_a[2]), swap_with(up_b, *order_b[2])
        grad_mat = blocks
        qkv_mat = blocks[:, : 3 * WIDE]
        out_mat = blocks[:, 3 * WIDE :]
        packed = blocks.reshape(owners, held, -1)[:, each, :small_len].reshape(-1)

        def widen(values):
            return round_low(dot_rows(values, spread))

        def turned(values, first, second):
            return round_low(dot_rows(values, first)), round_low(dot_rows(values, second))

    else:
        small_width = -(-small_len // LANES)
        qkv_width = w_qkv.shape[0] // LANES
        blocks = jnp.concatenate(
            [w_qkv.reshape(LANES, qkv_width), pack_small(small_params, small_width)], axis=1
        )
        blocks = gather_packed(blocks, core)
        qkv_mat = blocks[..., :qkv_width].reshape(model_width, 3 * model_width)
        qkv_mat = spread_blocks(qkv_mat, model_width)
        grad_mat = qkv_mat
        packed = blocks[..., qkv_width:].reshape(owners, -1)[:, :small_len].reshape(-1)
        out_mat = gather_packed(w_out.reshape(LANES, -1), core).reshape(model_width, model_width)
        up_mat = gather_packed(w_up.reshape(LANES, -1), core).reshape(model_width, FF)
        down_mat = gather_packed(w_down.reshape(LANES, -1), core).reshape(FF, model_width)

        spread = one_hot_columns(jnp.arange(model_width, dtype=jnp.int32), model_width)

        def widen(values):
            return values

        def send_sum(left, right, extra=None):
            grad = round_low(lead_dot(left, right)).reshape(groups * 2, 2, LANES, -1)
            if extra is not None:
                extra = extra.reshape(groups * 2, 2, small_len)
                grad = jnp.concatenate([grad, pack_small(extra, small_width)], axis=-1)
            return scatter_packed(grad, core)

    packed = packed.astype(jnp.float32)
    pieces = [packed[number * model_width : (number + 1) * model_width] for number in range(7)]
    gain_one, bias_one, bias_query, bias_value, bias_out, gain_two, bias_two = pieces
    up_bias = packed[7 * model_width : 7 * model_width + FF]
    down_bias = packed[7 * model_width + FF :]

    low_inputs = inputs
    inputs = inputs.astype(jnp.float32)
    normed_one, inverse_one = layer_stats(inputs)
    act_one = round_low(normed_one * gain_one + bias_one)
    qkv_bias = jnp.concatenate([bias_query, jnp.zeros_like(bias_query), bias_value])
    qkv_bias = spread_blocks(qkv_bias[None, :], model_width)
    own = round_low(dot_rows(widen(act_one), qkv_mat) + qkv_bias)
    other = lax.ppermute(own[:, WIDE:], "core", SWAP)
    if whole_rows:
        one_a, one_b = turned(act_one, turn_a, turn_b)
        one_a, one_b, more_a, more_b = tie((one_a, one_b, more_a, more_b))
        up_a = jnp.concatenate([up_a, more_a], axis=0)
        up_b = jnp.concatenate([up_b, more_b], axis=0)
        more_a, more_b = swap_with(up_a, *order_a[1]), swap_with(up_b, *order_b[1])
        other, one_a, one_b, up_a, up_b = tie((other, one_a, one_b, up_a, up_b))
    mixed, logs = attend(own, other, query_places, key_places)
    if whole_rows:
        mixed, more_a, more_b = tie((mixed, more_a, more_b))
        up_a = double(jnp.concatenate([up_a, more_a], axis=0), *order_a[0])
        up_b = double(jnp.concatenate([up_b, more_b], axis=0), *order_b[0])
        spread_mixed = round_low(dot_rows(mixed, head_spread))
    else:
        spread_mixed = mixed[:, :model_width]
    resid = inputs + dot_rows(spread_mixed, out_mat) + bias_out
    normed_two, inverse_two = layer_stats(resid)
    act_two = round_low(normed_two * gain_two + bias_two)
    if whole_rows:
        two_a, two_b = turned(act_two, turn_a, turn_b)
        gelu_a, slope_a = gate_and_slope(dot_rows(two_a, up_a) + up_bias[:up_cut])
        gelu_b, slope_b = gate_and_slope(dot_rows(two_b, up_b) + up_bias[up_cut:])
        slopes = [round_low(slope_a), round_low(slope_b)]
        gelu_rows = jnp.concatenate([round_low(gelu_a), round_low(gelu_b)], axis=1)
    else:
        gelu_rows, slope = gate_and_slope(dot_rows(act_two, up_mat) + up_bias)
        slopes = [round_low(slope)]
        gelu_rows = round_low(gelu_rows)
    down_parts = outer(gelu_rows, grad_rows)
    gelu_rows, down_parts, slopes = tie((gelu_rows, down_parts, slopes))
    down_a, down_b = [
        lax.psum_scatter(
            part.reshape(owners, -1, part.shape[1]), ALL, scatter_dimension=0, tiled=True
        )
        for part in down_parts
    ]

    grad_float = grad_rows.astype(jnp.float32)
    down_bias_term = jnp.sum(grad_float, axis=0)
    wide = FF // len(slopes)
    grad_pre = [
        round_low(
            tail_dot(grad_rows, down_mat[number * wide : (number + 1) * wide])
            * slope.astype(jnp.float32)
        )
        for number, slope in enumerate(slopes)
    ]
    up_bias_term = jnp.concatenate(
        [jnp.sum(part.astype(jnp.float32), axis=0) for part in grad_pre]
    )
    if whole_rows:
        pre_a, pre_b = grad_pre
        got_a = give_first(two_a, pre_a, order_a)
        got_b = give_first(two_b, pre_b, order_b)
        back_a, back_b = tail_dot(pre_a, up_a), tail_dot(pre_b, up_b)
        back_a, back_b, got_a, got_b = tie((back_a, back_b, got_a, got_b))
        sum_a = keep_first(two_a, pre_a, got_a)
        sum_b = keep_first(two_b, pre_b, got_b)
        back_a, back_b, sum_a, sum_b = tie((back_a, back_b, sum_a, sum_b))
        grad_act_two = tail_dot(round_low(back_a), turn_a) + tail_dot(round_low(back_b), turn_b)
    else:
        sum_up = send_sum(act_two, grad_pre[0])
        grad_act_two = tail_dot(grad_pre[0], up_mat)
    gain_two_term = jnp.sum(grad_act_two * normed_two, axis=0)
    bias_two_term = jnp.sum(grad_act_two, axis=0)
    grad_resid = grad_float + norm_back(grad_act_two, normed_two, inverse_two, gain_two)
    grad_attn = round_low(grad_resid)
    bias_out_term = jnp.sum(grad_attn.astype(jnp.float32), axis=0)
    grad_mixed = round_low(tail_dot(grad_attn, out_mat))
    if whole_rows:
        out_cut = (model_width // 256) * 128
        mixed_a, mixed_b = turned(mixed, head_a, head_b)
        out_got_a = give_first(mixed_a, grad_attn[:, :out_cut], order_a)
        out_got_b = give_first(mixed_b, grad_attn[:, out_cut:], order_b)
        grad_mixed = round_low(tail_dot(grad_mixed, head_spread))
        out_a = keep_first(mixed_a, grad_attn[:, :out_cut], out_got_a)
        out_b = keep_first(mixed_b, grad_attn[:, out_cut:], out_got_b)
        rest_a = jnp.concatenate([sum_a, out_a], axis=1)
        rest_b = jnp.concatenate([sum_b, out_b], axis=1)
        grad_mixed, rest_a, rest_b = tie((grad_mixed, rest_a, rest_b))
        got_a, got_b = send_half(rest_a, *order_a[1]), send_half(rest_b, *order_b[1])
    else:
        sum_out = send_sum(mixed[:, :model_width], grad_attn)
        grad_mixed = jnp.pad(grad_mixed, [(0, 0), (0, WIDE - model_width)])
    grad_own, grad_other = attend_back(
        own, other, query_places, key_places, mixed, logs, grad_mixed
    )
    grad_got = lax.ppermute(grad_other, "core", SWAP)
    if whole_rows:
        grad_own, got_a, got_b, gelu_rows = tie((grad_own, got_a, got_b, gelu_rows))
        rest_a, rest_b = add_half(rest_a, got_a), add_half(rest_b, got_b)
        got_a, got_b = send_half(rest_a, *order_a[2]), send_half(rest_b, *order_b[2])
        grad_got, down_a = tie((grad_got, down_a))
    grad_qkv_rows = add_received(grad_own, grad_got)
    rows_now = grad_qkv_rows
    if whole_rows:
        qkv_cut = (3 * WIDE // 256) * 128
        rows_a, rows_b = grad_qkv_rows[:, :qkv_cut], grad_qkv_rows[:, qkv_cut:]
        qkv_got_a = give_first(one_a, rows_a, order_a)
        qkv_got_b = give_first(one_b, rows_b, order_b)
        qkv_a = keep_first(one_a, rows_a, qkv_got_a)
        qkv_b = keep_first(one_b, rows_b, qkv_got_b)
        rows_now, qkv_a, qkv_b, got_a, got_b = tie((rows_now, qkv_a, qkv_b, got_a, got_b))
        rest = jnp.concatenate([add_half(rest_a, got_a), add_half(rest_b, got_b)], axis=1)
        qkv_got_a = send_half(qkv_a, *order_a[1])
        qkv_got_b = send_half(qkv_b, *order_b[1])
        rest_got = send_half(rest, *order_a[3])
    qkv_sums = jnp.sum(grad_qkv_rows.astype(jnp.float32), axis=0)
    early_small = jnp.concatenate(
        [
            qkv_sums[:model_width],
            qkv_sums[2 * WIDE : 2 * WIDE + model_width],
            bias_out_term,
            gain_two_term,
            bias_two_term,
            up_bias_term,
            down_bias_term,
        ]
    )
    grad_input, gain_one_term, bias_one_term = input_grad(
        rows_now, grad_mat, spread, low_inputs, gain_one[None, :], grad_resid
    )
    if whole_rows:
        (
            grad_input,
            gain_one_term,
            bias_one_term,
            early_small,
            gelu_rows,
            qkv_got_a,
            qkv_got_b,
            rest_got,
        ) = tie(
            (
                grad_input,
                gain_one_term,
                bias_one_term,
                early_small,
                gelu_rows,
                qkv_got_a,
                qkv_got_b,
                rest_got,
            )
        )
        qkv_a, qkv_b = add_half(qkv_a, qkv_got_a), add_half(qkv_b, qkv_got_b)
        qkv_got_a = send_half(qkv_a, *order_a[2])
        qkv_got_b = send_half(qkv_b, *order_b[2])
        rest = add_half(rest, rest_got)
        rest_got = send_half(rest, *order_a[4])
    outputs = project(gelu_rows, down_mat, resid, down_bias[None, :])
    small_grad = jnp.concatenate([gain_one_term[0], bias_one_term[0], early_small])
    small_grad = round_low(small_grad)
    if whole_rows:
        down_b, outputs, qkv_got_a, qkv_got_b, rest_got = tie(
            (down_b, outputs, qkv_got_a, qkv_got_b, rest_got)
        )
    result_got = trade_out(outputs)
    if whole_rows:
        qkv_a, qkv_b = add_half(qkv_a, qkv_got_a), add_half(qkv_b, qkv_got_b)
        sum_qkv = jnp.concatenate([qkv_a, qkv_b], axis=1)
        sum_got = send_half(sum_qkv, *order_a[3])
        rest = add_half(rest, rest_got)
        for step in order_a[5:]:
            rest = halve(rest, *step)
        small_grad = small_grad.reshape(owners, small_len)
        sum_got, result_got, small_grad = tie((sum_got, result_got, small_grad))
        sum_qkv = add_half(sum_qkv, sum_got)
        for step in order_a[4:]:
            sum_qkv = halve(sum_qkv, *step)
        small_parts = lax.all_to_all(small_grad, ALL, 0, 0, tiled=True)
        grad_small = jnp.sum(small_parts.astype(jnp.float32), axis=0)
        sides = [up_cut, up_cut + out_cut, FF + out_cut]
        sum_up = jnp.concatenate([rest[:, : sides[0]], rest[:, sides[1] : sides[2]]], axis=1)
        sum_out = jnp.concatenate([rest[:, sides[0] : sides[1]], rest[:, sides[2] :]], axis=1)
        grad_qkv = pick_blocks(sum_qkv, model_width)
    else:
        sum_qkv = send_sum(act_one, pick_blocks(grad_qkv_rows, model_width), small_grad)
        grad_qkv, grad_small = sum_qkv[:, :qkv_width], sum_qkv[:, qkv_width:]
    result = trade_join(outputs, result_got)
    grad_tokens = trade_join(grad_input, trade_out(grad_input))
    sum_down = jnp.concatenate([down_a, down_b], axis=2)
    grad_small = grad_small.astype(jnp.float32).reshape(-1)[:small_len]
    grad_qkv, grad_out, grad_up, grad_down = [
        piece.astype(jnp.float32).reshape(-1) for piece in (grad_qkv, sum_out, sum_up, sum_down)
    ]
    return (result, grad_tokens, grad_qkv, grad_out, grad_up, grad_down, grad_small)


def solution(mesh):
    groups, owners = mesh.shape["dp"], mesh.shape["ctx"]
    fine = Mesh(mesh.devices.reshape(groups, owners // 2, 2), ("dp", "y", "core"))
    rows = P("dp", ("y", "core"), None)
    flat = P(("dp", "y", "core"))
    return jax.shard_map(
        local,
        mesh=fine,
        in_specs=(rows, P("dp", None), flat, flat, flat, flat, flat, rows),
        out_specs=(rows, rows, flat, flat, flat, flat, flat),
        check_vma=False,
    )
```

```python
import jax
import jax.numpy as jnp
from jax import lax
from jax.experimental import pallas as pl
from jax.experimental.pallas import tpu as pltpu
from jax.sharding import Mesh, PartitionSpec as P

HEADS = 17
HEAD_DIM = 64
FF = 4352
LANES = 8
WIDE = 1152
SWAP = ((0, 1), (1, 0))
OWNERS = ("dp", "y")


def layer_stats(values):
    center = values - jnp.mean(values, axis=-1, keepdims=True)
    inverse = lax.rsqrt(jnp.mean(center * center, axis=-1, keepdims=True) + 1e-05)
    return (center * inverse, inverse)


def norm_back(upstream, normed, inverse, gain_vector):
    scaled = upstream * gain_vector
    return inverse * (
        scaled
        - jnp.mean(scaled, axis=-1, keepdims=True)
        - normed * jnp.mean(scaled * normed, axis=-1, keepdims=True)
    )


def lead_dot(left_side, right_side):
    return lax.dot_general(
        left_side, right_side, (((0,), (0,)), ((), ())), preferred_element_type=jnp.float32
    )


def tail_dot(left_side, right_side):
    return lax.dot_general(
        left_side, right_side, (((1,), (1,)), ((), ())), preferred_element_type=jnp.float32
    )


def gate_and_slope(values):
    rate = (2.0 / jnp.pi) ** 0.5
    square = values * values
    bend = jnp.tanh(rate * values * (1.0 + 0.044715 * square))
    share = 0.5 * (1.0 + bend)
    slope = share + 0.5 * values * (1.0 - bend * bend) * rate * (1.0 + 0.134145 * square)
    return values * share, slope


def pack_small(values, width):
    room = LANES * width - values.shape[-1]
    padded = jnp.pad(values, [(0, 0)] * (values.ndim - 1) + [(0, room)])
    return padded.reshape(values.shape[:-1] + (LANES, width))


def gather_packed(block, core):
    own = lax.all_gather(block, OWNERS, axis=0, tiled=True)
    other = lax.ppermute(own, "core", SWAP)
    even = jnp.where(core == 0, own, other)
    odd = jnp.where(core == 0, other, own)
    shape = (-1, 1, LANES, block.shape[1])
    return jnp.concatenate([even.reshape(shape), odd.reshape(shape)], axis=1)


def scatter_packed(packed, core):
    even, odd = packed[:, 0], packed[:, 1]
    keep = jnp.where(core == 0, even, odd)
    give = jnp.where(core == 0, odd, even)
    got = lax.ppermute(give, "core", SWAP)
    pair = (keep.astype(jnp.float32) + got.astype(jnp.float32)).astype(jnp.bfloat16)
    return lax.psum_scatter(pair, OWNERS, scatter_dimension=0, tiled=True)[0]


def dot_rows(left, right):
    return lax.dot_general(
        left, right, (((1,), (0,)), ((), ())), preferred_element_type=jnp.float32
    )


def bias_of(key_places, query_places):
    return jnp.where(key_places <= query_places, 0.0, -1e30).astype(jnp.float32)


def per_pair(one_pair):
    pair = 2 * HEAD_DIM
    full = HEADS // 2

    def step(number, carry):
        one_pair(pl.multiple_of(number * pair, pair), 2 * number, 2)
        return carry

    lax.fori_loop(0, full, step, 0)
    if HEADS % 2:
        one_pair(full * pair, 2 * full, 1)


def lanes_at(start, block):
    return pl.ds(block * WIDE + start, 2 * HEAD_DIM)


def stand(parts):
    if len(parts) == 1:
        parts = parts + [jnp.zeros_like(parts[0])]
    return jnp.concatenate(parts, axis=0).T


def only_head(values, number, heads):
    if heads == 1:
        return values
    lane = lax.broadcasted_iota(jnp.int32, values.shape, 1)
    inside = lane < HEAD_DIM if number == 0 else lane >= HEAD_DIM
    return jnp.where(inside, values, jnp.zeros_like(values))


def join_heads(parts):
    if len(parts) == 1:
        return parts[0]
    lane = lax.broadcasted_iota(jnp.int32, parts[0].shape, 1)
    return jnp.where(lane < HEAD_DIM, parts[0], parts[1])


def attend_kernel(
    own_ref, other_ref, query_ref, key_ref, mixed_ref, log_ref, low_bias, up_bias
):
    half = own_ref.shape[0] // 2
    low_bias[...] = bias_of(key_ref[: 2 * half], query_ref[:, :half])
    up_bias[...] = bias_of(key_ref[2 * half :], query_ref[:, half:])

    def one_pair(start, first, heads):
        q = own_ref[:, lanes_at(start, 0)] * jnp.asarray(HEAD_DIM**-0.5, jnp.bfloat16)
        k_own, v_own = own_ref[:, lanes_at(start, 1)], own_ref[:, lanes_at(start, 2)]
        k_other, v_other = other_ref[:, lanes_at(start, 0)], other_ref[:, lanes_at(start, 1)]
        k_low = jnp.concatenate([k_own[:half], k_other[:half]], axis=0)
        k_up = jnp.concatenate([k_own[half:], k_other[half:]], axis=0)
        v_low = jnp.concatenate([v_own[:half], v_other[:half]], axis=0).T
        v_up = jnp.concatenate([v_own[half:], v_other[half:]], axis=0).T
        low_parts, up_parts = [], []
        for number in range(heads):
            rows = slice(number * HEAD_DIM, (number + 1) * HEAD_DIM)
            q_head = only_head(q, number, heads)
            s = tail_dot(k_low, q_head[:half]) + low_bias[...]
            top = jnp.max(s, axis=0, keepdims=True)
            e = jnp.exp(s - top)
            total = jnp.sum(e, axis=0, keepdims=True)
            mixed = dot_rows(v_low[rows], e.astype(jnp.bfloat16)) / total
            low_parts.append(mixed)
            log_ref[pl.ds(first + number, 1), :half] = top + jnp.log(total)
            s_low = tail_dot(k_low, q_head[half:])
            s_up = tail_dot(k_up, q_head[half:]) + up_bias[...]
            top = jnp.maximum(
                jnp.max(s_low, axis=0, keepdims=True), jnp.max(s_up, axis=0, keepdims=True)
            )
            e_low = jnp.exp(s_low - top)
            e_up = jnp.exp(s_up - top)
            total = jnp.sum(e_low, axis=0, keepdims=True) + jnp.sum(e_up, axis=0, keepdims=True)
            mixed = dot_rows(v_low[rows], e_low.astype(jnp.bfloat16))
            mixed = mixed + dot_rows(v_up[rows], e_up.astype(jnp.bfloat16))
            up_parts.append(mixed / total)
            log_ref[pl.ds(first + number, 1), half:] = top + jnp.log(total)
        mixed_ref[:half, lanes_at(start, 0)] = stand(low_parts).astype(jnp.bfloat16)
        mixed_ref[half:, lanes_at(start, 0)] = stand(up_parts).astype(jnp.bfloat16)

    per_pair(one_pair)


def attend_back_kernel(
    own_ref,
    other_ref,
    query_ref,
    key_ref,
    mixed_ref,
    log_ref,
    grad_ref,
    own_out,
    other_out,
    low_bias,
    up_bias,
):
    half = own_ref.shape[0] // 2
    factor = HEAD_DIM**-0.5
    low_bias[...] = bias_of(key_ref[: 2 * half], query_ref[:, :half])
    up_bias[...] = bias_of(key_ref[2 * half :], query_ref[:, half:])

    def one_pair(start, first, heads):
        lanes = lanes_at(start, 0)
        q = own_ref[:, lanes] * jnp.asarray(factor, jnp.bfloat16)
        grad = grad_ref[:, lanes]
        product = (grad.astype(jnp.float32) * mixed_ref[:, lanes].astype(jnp.float32)).T
        q_heads = [only_head(q, number, heads) for number in range(heads)]
        grad_heads = [only_head(grad, number, heads) for number in range(heads)]
        deltas = [
            jnp.sum(product[number * HEAD_DIM : (number + 1) * HEAD_DIM], axis=0, keepdims=True)
            for number in range(heads)
        ]
        logs = [log_ref[pl.ds(first + number, 1), :] for number in range(heads)]
        dq_low = [None] * heads
        dq_up = [None] * heads
        for source, out, place, block in (
            (own_ref, own_out, 0, 1),
            (other_ref, other_out, 1, 0),
        ):
            klanes, vlanes = lanes_at(start, block), lanes_at(start, block + 1)
            bias_rows = slice(place * half, (place + 1) * half)
            for upper in (False, True):
                rows = slice(half, None) if upper else slice(0, half)
                k = source[rows, klanes]
                v = source[rows, vlanes]
                k_turned = k.T
                dk_parts, dv_parts = [], []
                for number in range(heads):
                    head_rows = slice(number * HEAD_DIM, (number + 1) * HEAD_DIM)
                    first_query = half if upper else 0
                    q_head = q_heads[number][first_query:]
                    grad_head = grad_heads[number][first_query:]
                    s = tail_dot(k, q_head)
                    if upper:
                        s = s + up_bias[bias_rows]
                    else:
                        s = jnp.concatenate([s[:, :half] + low_bias[bias_rows], s[:, half:]], axis=1)
                    p = jnp.exp(s - logs[number][:, first_query:])
                    dp = tail_dot(v, grad_head)
                    ds = (p * (dp - deltas[number][:, first_query:])).astype(jnp.bfloat16)
                    dv_parts.append(dot_rows(p.astype(jnp.bfloat16), grad[first_query:]))
                    dk_parts.append(dot_rows(ds, q[first_query:]))
                    turned = dot_rows(k_turned[head_rows], ds)
                    low = None if upper else turned[:, :half]
                    up = turned if upper else turned[:, half:]
                    if low is not None:
                        dq_low[number] = low if dq_low[number] is None else dq_low[number] + low
                    dq_up[number] = up if dq_up[number] is None else dq_up[number] + up
                out[rows, klanes] = join_heads(dk_parts).astype(jnp.bfloat16)
                out[rows, vlanes] = join_heads(dv_parts).astype(jnp.bfloat16)
        own_out[:half, lanes] = (stand(dq_low) * factor).astype(jnp.bfloat16)
        own_out[half:, lanes] = (stand(dq_up) * factor).astype(jnp.bfloat16)

    per_pair(one_pair)


def add_kernel(own_ref, got_ref, out_ref):
    total = own_ref[...].astype(jnp.float32) + got_ref[...].astype(jnp.float32)
    out_ref[...] = total.astype(out_ref.dtype)


def add_received(own, got):
    rows = own.shape[0]
    block = (rows, WIDE)
    return pl.pallas_call(
        add_kernel,
        grid=(2,),
        in_specs=[
            pl.BlockSpec(block, lambda i: (0, i + 1)),
            pl.BlockSpec(block, lambda i: (0, i)),
        ],
        out_specs=pl.BlockSpec(block, lambda i: (0, i + 1)),
        out_shape=jax.ShapeDtypeStruct(own.shape, own.dtype),
        input_output_aliases={0: 0},
        compiler_params=pltpu.CompilerParams(vmem_limit_bytes=32 * 1024 * 1024),
        cost_estimate=pl.CostEstimate(flops=1 << 20, bytes_accessed=7 << 20, transcendentals=0),
    )(own, got)


def kernel_call(body, outs, half, cost):
    return pl.pallas_call(
        body,
        out_shape=outs,
        scratch_shapes=[pltpu.VMEM((2 * half, half), jnp.float32)] * 2,
        compiler_params=pltpu.CompilerParams(vmem_limit_bytes=48 * 1024 * 1024),
        cost_estimate=pl.CostEstimate(flops=cost, bytes_accessed=12 << 20, transcendentals=cost // 256),
    )


def outer_kernel(left_ref, right_ref, first_ref, second_ref):
    part = lead_dot(left_ref[...], right_ref[...]).astype(first_ref.dtype)
    cut = first_ref.shape[1]
    first_ref[...] = part[:, :cut]
    second_ref[...] = part[:, cut:]


def outer(left, right):
    rows, count = left.shape
    width = right.shape[1]
    step = 256
    cut = (width // 256) * 128
    return pl.pallas_call(
        outer_kernel,
        grid=(count // step,),
        in_specs=[
            pl.BlockSpec((rows, step), lambda i: (0, i)),
            pl.BlockSpec((rows, width), lambda i: (0, 0)),
        ],
        out_specs=[
            pl.BlockSpec((step, cut), lambda i: (i, 0)),
            pl.BlockSpec((step, width - cut), lambda i: (i, 0)),
        ],
        out_shape=[
            jax.ShapeDtypeStruct((count, cut), jnp.bfloat16),
            jax.ShapeDtypeStruct((count, width - cut), jnp.bfloat16),
        ],
        compiler_params=pltpu.CompilerParams(vmem_limit_bytes=32 * 1024 * 1024),
        cost_estimate=pl.CostEstimate(
            flops=2 * rows * count * width, bytes_accessed=16 << 20, transcendentals=0
        ),
    )(left, right)


def input_grad_kernel(
    rows_ref,
    mat_ref,
    spread_ref,
    input_ref,
    gain_ref,
    resid_ref,
    out_ref,
    gain_out,
    bias_out,
    total,
):
    step = pl.program_id(0)
    part = tail_dot(rows_ref[...], mat_ref[...])

    @pl.when(step == 0)
    def _():
        total[...] = part

    @pl.when(step > 0)
    def _():
        total[...] += part

    @pl.when(step == pl.num_programs(0) - 1)
    def _():
        back = tail_dot(total[...].astype(jnp.bfloat16), spread_ref[...])
        normed, inverse = layer_stats(input_ref[...].astype(jnp.float32))
        gain_out[...] = jnp.sum(back * normed, axis=0, keepdims=True)
        bias_out[...] = jnp.sum(back, axis=0, keepdims=True)
        grad = resid_ref[...] + norm_back(back, normed, inverse, gain_ref[...])
        out_ref[...] = grad.astype(out_ref.dtype)


def input_grad(rows, mat, spread, inputs, gain, resid):
    count, width = inputs.shape
    held = mat.shape[0]
    step = 384

    def fixed(shape):
        return pl.BlockSpec(shape, lambda i: (0, 0))

    return pl.pallas_call(
        input_grad_kernel,
        grid=(3 * WIDE // step,),
        in_specs=[
            pl.BlockSpec((count, step), lambda i: (0, i)),
            pl.BlockSpec((held, step), lambda i: (0, i)),
            fixed((width, held)),
            fixed((count, width)),
            fixed((1, width)),
            fixed((count, width)),
        ],
        out_specs=[fixed((count, width)), fixed((1, width)), fixed((1, width))],
        out_shape=[
            jax.ShapeDtypeStruct((count, width), jnp.bfloat16),
            jax.ShapeDtypeStruct((1, width), jnp.float32),
            jax.ShapeDtypeStruct((1, width), jnp.float32),
        ],
        scratch_shapes=[pltpu.VMEM((count, held), jnp.float32)],
        compiler_params=pltpu.CompilerParams(vmem_limit_bytes=48 * 1024 * 1024),
        cost_estimate=pl.CostEstimate(flops=14 << 30, bytes_accessed=20 << 20, transcendentals=0),
    )(rows, mat, spread, inputs, gain, resid)


def project_kernel(left_ref, mat_ref, resid_ref, bias_ref, out_ref, total):
    step = pl.program_id(0)
    part = dot_rows(left_ref[...], mat_ref[...])

    @pl.when(step == 0)
    def _():
        total[...] = resid_ref[...] + bias_ref[...] + part

    @pl.when(step > 0)
    def _():
        total[...] += part

    @pl.when(step == pl.num_programs(0) - 1)
    def _():
        out_ref[...] = total[...].astype(out_ref.dtype)


def project(left, mat, resid, bias):
    count, depth = left.shape
    width = mat.shape[1]
    step = 256

    def fixed(shape):
        return pl.BlockSpec(shape, lambda i: (0, 0))

    return pl.pallas_call(
        project_kernel,
        grid=(depth // step,),
        in_specs=[
            pl.BlockSpec((count, step), lambda i: (0, i)),
            pl.BlockSpec((step, width), lambda i: (i, 0)),
            fixed((count, width)),
            fixed((1, width)),
        ],
        out_specs=fixed((count, width)),
        out_shape=jax.ShapeDtypeStruct((count, width), jnp.bfloat16),
        scratch_shapes=[pltpu.VMEM((count, width), jnp.float32)],
        compiler_params=pltpu.CompilerParams(vmem_limit_bytes=32 * 1024 * 1024),
        cost_estimate=pl.CostEstimate(flops=14 << 30, bytes_accessed=20 << 20, transcendentals=0),
    )(left, mat, resid, bias)


def attend(own, other, query_places, key_places):
    rows = own.shape[0]
    outs = (
        jax.ShapeDtypeStruct((rows, WIDE), jnp.bfloat16),
        jax.ShapeDtypeStruct((HEADS, rows), jnp.float32),
    )
    call = kernel_call(attend_kernel, outs, rows // 2, 20 << 30)
    return call(own, other, query_places, key_places)


def attend_back(own, other, query_places, key_places, mixed, logs, grad):
    outs = (
        jax.ShapeDtypeStruct(own.shape, jnp.bfloat16),
        jax.ShapeDtypeStruct(other.shape, jnp.bfloat16),
    )
    call = kernel_call(attend_back_kernel, outs, own.shape[0] // 2, 30 << 30)
    return call(own, other, query_places, key_places, mixed, logs, grad)


ALL = ("dp", "y", "core")


def round_low(values):
    return values.astype(jnp.bfloat16)


def one_hot_columns(targets, width):
    line = lax.broadcasted_iota(jnp.int32, (width, targets.shape[0]), 0)
    return (line == targets[None, :]).astype(jnp.bfloat16)


def swap_with(values, axis, bit):
    count = lax.axis_size(axis)
    return lax.ppermute(values, axis, [(here, here ^ (1 << bit)) for here in range(count)])


def near_owners(order, dp_bits, each):
    owner = (lax.axis_index("dp") * 2 + lax.axis_index("y")) * 2 + lax.axis_index("core")
    bits = dp_bits + 2
    column = jnp.arange(each << bits, dtype=jnp.int32)
    place, inner = column // each, column % each
    far = jnp.zeros_like(place)
    for number, (axis, bit) in enumerate(order):
        weight = {"core": 0, "y": 1, "dp": 2 + bit}[axis]
        far = far + (((place >> (bits - 1 - number)) & 1) << weight)
    return (owner ^ far) * each + inner


def give_first(left, right, order):
    half = left.shape[1] // 2
    return swap_with(round_low(lead_dot(left[:, half:], right)), *order[0])


def keep_first(left, right, got):
    half = left.shape[1] // 2
    kept = round_low(lead_dot(left[:, :half], right))
    return round_low(kept.astype(jnp.float32) + got.astype(jnp.float32))


def pick_half(values, axis, bit, other):
    here = (lax.axis_index(axis) >> bit) & 1
    return lax.dynamic_index_in_dim(values, here ^ other, 1, keepdims=False)


def pair_up(values, low):
    lead, rest = values.shape[0], values.shape[1:]
    return values.reshape((lead // (2 * low), 2, low) + rest)


def send_block(values, axis, bit, low):
    return swap_with(pick_half(pair_up(values, low), axis, bit, 1), axis, bit)


def add_block(values, got, axis, bit, low):
    kept = pick_half(pair_up(values, low), axis, bit, 0)
    total = round_low(kept.astype(jnp.float32) + got.astype(jnp.float32))
    return total.reshape((-1,) + values.shape[1:])


def double(values, axis, bit):
    return jnp.concatenate([values, swap_with(values, axis, bit)], axis=0)


tie = lax.optimization_barrier


def send_half(values, axis, bit):
    return swap_with(values[values.shape[0] // 2 :], axis, bit)


def add_half(values, got):
    half = values.shape[0] // 2
    return round_low(values[:half].astype(jnp.float32) + got.astype(jnp.float32))


def halve(values, axis, bit):
    return add_half(values, send_half(values, axis, bit))


def spread_blocks(values, width):
    spare = jnp.zeros((values.shape[0], WIDE - width), values.dtype)
    parts = []
    for number in range(3):
        parts += [values[:, number * width : (number + 1) * width], spare]
    return jnp.concatenate(parts, axis=1)


def pick_blocks(values, width):
    return jnp.concatenate(
        [values[:, number * WIDE : number * WIDE + width] for number in range(3)], axis=1
    )


def local(tokens, positions, w_qkv, w_out, w_up, w_down, small_params, cotangent):
    seqs_here, local_len, model_width = tokens.shape
    span = local_len // 2
    rows = seqs_here * local_len
    half = rows // 2
    y = lax.axis_index("y")
    core = lax.axis_index("core")
    groups = lax.axis_size("dp")
    owners = groups * 4
    small_len = small_params.shape[0]
    whole_rows = model_width % owners == 0
    each = model_width // owners
    dp_bits = groups.bit_length() - 1

    def trade(values):
        mine = lax.dynamic_index_in_dim(values, y, 0, keepdims=False)
        give = lax.dynamic_index_in_dim(values, 1 - y, 0, keepdims=False)
        got = lax.ppermute(give, "y", SWAP)
        return jnp.concatenate([mine[:span], got[:span], mine[span:], got[span:]], axis=0)

    def trade_out(values):
        return lax.ppermute(
            jnp.concatenate([values[span:half], values[half + span :]], axis=0), "y", SWAP
        )

    def trade_join(values, got):
        mine = jnp.concatenate([values[:span], values[half : half + span]], axis=0)
        first = jnp.where(y == 0, mine, got)
        second = jnp.where(y == 0, got, mine)
        return jnp.stack([first, second])

    place_row = lax.dynamic_index_in_dim(positions, y, 0, keepdims=False)

    def places_of(core_index):
        near = lax.dynamic_slice_in_dim(place_row, (2 * y + core_index) * local_len, local_len)
        far = lax.dynamic_slice_in_dim(place_row, (2 - 2 * y + core_index) * local_len, local_len)
        return jnp.concatenate([near[:span], far[:span]]), jnp.concatenate([near[span:], far[span:]])

    own_low, own_up = places_of(core)
    other_low, other_up = places_of(1 - core)
    query_places = jnp.concatenate([own_low, own_up])[None, :]
    key_places = jnp.concatenate([own_low, other_low, own_up, other_up])[:, None]

    inputs = trade(tokens)
    grad_rows = trade(cotangent)
    if whole_rows:
        steps = [("dp", bit) for bit in range(dp_bits)]
        order_a = [("core", 0), steps[0], ("y", 0)] + steps[1:]
        order_b = [("core", 0), ("y", 0), steps[0]] + steps[1:]
        near_a = near_owners(order_a, dp_bits, each)
        near_b = near_owners(order_b, dp_bits, each)
        turn_a = one_hot_columns(near_a, model_width)
        turn_b = one_hot_columns(near_b, model_width)
        head_a = one_hot_columns(near_a, WIDE)
        head_b = one_hot_columns(near_b, WIDE)
        room = -(each + 1) % 8
        held = each + 1 + room
        column = jnp.arange(owners * held, dtype=jnp.int32)
        inside = column % held
        spread = jnp.where(inside < each, column // held * each + inside, -1)
        head_spread = one_hot_columns(spread, WIDE)
        spread = one_hot_columns(spread, model_width)
        blocks = jnp.concatenate(
            [
                spread_blocks(w_qkv.reshape(each, 3 * model_width), model_width),
                w_out.reshape(each, model_width),
            ],
            axis=1,
        )
        extra = jnp.pad(
            small_params.reshape(1, -1), [(0, room), (0, blocks.shape[1] - small_len)]
        )
        blocks = jnp.concatenate([blocks, extra], axis=0)
        blocks = lax.all_gather(blocks, ALL, axis=0, tiled=True)
        down_mat = lax.all_gather(w_down.reshape(-1, model_width), ALL, axis=0, tiled=True)
        up_part = w_up.reshape(each, FF)
        for step in order_a[:2:-1]:
            up_part = double(up_part, *step)
        up_cut = FF // 2
        blocks, up_part, inputs, grad_rows, query_places, key_places, turn_a, turn_b, spread = tie(
            (
                blocks,
                up_part,
                inputs,
                grad_rows,
                query_places,
                key_places,
                turn_a,
                turn_b,
                spread,
            )
        )
        head_a, head_b, head_spread = tie((head_a, head_b, head_spread))
        up_a, up_b = up_part[:, :up_cut], up_part[:, up_cut:]
        more_a, more_b = swap_with(up_a, *order_a[2]), swap_with(up_b, *order_b[2])
        grad_mat = blocks
        qkv_mat = blocks[:, : 3 * WIDE]
        out_mat = blocks[:, 3 * WIDE :]
        packed = blocks.reshape(owners, held, -1)[:, each, :small_len].reshape(-1)

        def widen(values):
            return round_low(dot_rows(values, spread))

        def turned(values, first, second):
            return round_low(dot_rows(values, first)), round_low(dot_rows(values, second))

    else:
        small_width = -(-small_len // LANES)
        qkv_width = w_qkv.shape[0] // LANES
        blocks = jnp.concatenate(
            [w_qkv.reshape(LANES, qkv_width), pack_small(small_params, small_width)], axis=1
        )
        blocks = gather_packed(blocks, core)
        qkv_mat = blocks[..., :qkv_width].reshape(model_width, 3 * model_width)
        qkv_mat = spread_blocks(qkv_mat, model_width)
        grad_mat = qkv_mat
        packed = blocks[..., qkv_width:].reshape(owners, -1)[:, :small_len].reshape(-1)
        out_mat = gather_packed(w_out.reshape(LANES, -1), core).reshape(model_width, model_width)
        up_mat = gather_packed(w_up.reshape(LANES, -1), core).reshape(model_width, FF)
        down_mat = gather_packed(w_down.reshape(LANES, -1), core).reshape(FF, model_width)

        spread = one_hot_columns(jnp.arange(model_width, dtype=jnp.int32), model_width)

        def widen(values):
            return values

        def send_sum(left, right, extra=None):
            grad = round_low(lead_dot(left, right)).reshape(groups * 2, 2, LANES, -1)
            if extra is not None:
                extra = extra.reshape(groups * 2, 2, small_len)
                grad = jnp.concatenate([grad, pack_small(extra, small_width)], axis=-1)
            return scatter_packed(grad, core)

    packed = packed.astype(jnp.float32)
    pieces = [packed[number * model_width : (number + 1) * model_width] for number in range(7)]
    gain_one, bias_one, bias_query, bias_value, bias_out, gain_two, bias_two = pieces
    up_bias = packed[7 * model_width : 7 * model_width + FF]
    down_bias = packed[7 * model_width + FF :]

    low_inputs = inputs
    inputs = inputs.astype(jnp.float32)
    normed_one, inverse_one = layer_stats(inputs)
    act_one = round_low(normed_one * gain_one + bias_one)
    qkv_bias = jnp.concatenate([bias_query, jnp.zeros_like(bias_query), bias_value])
    qkv_bias = spread_blocks(qkv_bias[None, :], model_width)
    own = round_low(dot_rows(widen(act_one), qkv_mat) + qkv_bias)
    other = lax.ppermute(own[:, WIDE:], "core", SWAP)
    if whole_rows:
        one_a, one_b = turned(act_one, turn_a, turn_b)
        one_a, one_b, more_a, more_b = tie((one_a, one_b, more_a, more_b))
        up_a = jnp.concatenate([up_a, more_a], axis=0)
        up_b = jnp.concatenate([up_b, more_b], axis=0)
        more_a, more_b = swap_with(up_a, *order_a[1]), swap_with(up_b, *order_b[1])
        other, one_a, one_b, up_a, up_b = tie((other, one_a, one_b, up_a, up_b))
    mixed, logs = attend(own, other, query_places, key_places)
    if whole_rows:
        mixed, more_a, more_b = tie((mixed, more_a, more_b))
        up_a = double(jnp.concatenate([up_a, more_a], axis=0), *order_a[0])
        up_b = double(jnp.concatenate([up_b, more_b], axis=0), *order_b[0])
        spread_mixed = round_low(dot_rows(mixed, head_spread))
    else:
        spread_mixed = mixed[:, :model_width]
    resid = inputs + dot_rows(spread_mixed, out_mat) + bias_out
    normed_two, inverse_two = layer_stats(resid)
    act_two = round_low(normed_two * gain_two + bias_two)
    if whole_rows:
        two_a, two_b = turned(act_two, turn_a, turn_b)
        gelu_a, slope_a = gate_and_slope(dot_rows(two_a, up_a) + up_bias[:up_cut])
        gelu_b, slope_b = gate_and_slope(dot_rows(two_b, up_b) + up_bias[up_cut:])
        slopes = [round_low(slope_a), round_low(slope_b)]
        gelu_rows = jnp.concatenate([round_low(gelu_a), round_low(gelu_b)], axis=1)
    else:
        gelu_rows, slope = gate_and_slope(dot_rows(act_two, up_mat) + up_bias)
        slopes = [round_low(slope)]
        gelu_rows = round_low(gelu_rows)
    down_parts = outer(gelu_rows, grad_rows)
    gelu_rows, down_parts, slopes = tie((gelu_rows, down_parts, slopes))
    down_a, down_b = [part.reshape(owners, -1, part.shape[1]) for part in down_parts]
    if whole_rows:
        down_got_a = send_block(down_a, "core", 0, 1)
        down_got_b = send_block(down_b, "core", 0, 1)
    else:
        down_a, down_b = [
            lax.psum_scatter(part, ALL, scatter_dimension=0, tiled=True)
            for part in (down_a, down_b)
        ]

    grad_float = grad_rows.astype(jnp.float32)
    down_bias_term = jnp.sum(grad_float, axis=0)
    wide = FF // len(slopes)
    grad_pre = [
        round_low(
            tail_dot(grad_rows, down_mat[number * wide : (number + 1) * wide])
            * slope.astype(jnp.float32)
        )
        for number, slope in enumerate(slopes)
    ]
    up_bias_term = jnp.concatenate(
        [jnp.sum(part.astype(jnp.float32), axis=0) for part in grad_pre]
    )
    if whole_rows:
        pre_a, pre_b = grad_pre
        got_a = give_first(two_a, pre_a, order_a)
        got_b = give_first(two_b, pre_b, order_b)
        back_a, back_b = tail_dot(pre_a, up_a), tail_dot(pre_b, up_b)
        back_a, back_b, got_a, got_b, down_got_a, down_got_b = tie(
            (back_a, back_b, got_a, got_b, down_got_a, down_got_b)
        )
        down_a = add_block(down_a, down_got_a, "core", 0, 1)
        down_b = add_block(down_b, down_got_b, "core", 0, 1)
        down_got_a = send_block(down_a, *order_a[1], 2)
        down_got_b = send_block(down_b, *order_b[1], 1)
        sum_a = keep_first(two_a, pre_a, got_a)
        sum_b = keep_first(two_b, pre_b, got_b)
        back_a, back_b, sum_a, sum_b = tie((back_a, back_b, sum_a, sum_b))
        grad_act_two = tail_dot(round_low(back_a), turn_a) + tail_dot(round_low(back_b), turn_b)
    else:
        sum_up = send_sum(act_two, grad_pre[0])
        grad_act_two = tail_dot(grad_pre[0], up_mat)
    gain_two_term = jnp.sum(grad_act_two * normed_two, axis=0)
    bias_two_term = jnp.sum(grad_act_two, axis=0)
    grad_resid = grad_float + norm_back(grad_act_two, normed_two, inverse_two, gain_two)
    grad_attn = round_low(grad_resid)
    bias_out_term = jnp.sum(grad_attn.astype(jnp.float32), axis=0)
    grad_mixed = round_low(tail_dot(grad_attn, out_mat))
    if whole_rows:
        out_cut = (model_width // 256) * 128
        mixed_a, mixed_b = turned(mixed, head_a, head_b)
        out_got_a = give_first(mixed_a, grad_attn[:, :out_cut], order_a)
        out_got_b = give_first(mixed_b, grad_attn[:, out_cut:], order_b)
        grad_mixed = round_low(tail_dot(grad_mixed, head_spread))
        out_a = keep_first(mixed_a, grad_attn[:, :out_cut], out_got_a)
        out_b = keep_first(mixed_b, grad_attn[:, out_cut:], out_got_b)
        rest_a = jnp.concatenate([sum_a, out_a], axis=1)
        rest_b = jnp.concatenate([sum_b, out_b], axis=1)
        grad_mixed, rest_a, rest_b, down_got_a, down_got_b = tie(
            (grad_mixed, rest_a, rest_b, down_got_a, down_got_b)
        )
        down_a = add_block(down_a, down_got_a, *order_a[1], 2)
        down_b = add_block(down_b, down_got_b, *order_b[1], 1)
        down_got_a = send_block(down_a, *order_a[2], 1)
        down_got_b = send_block(down_b, *order_b[2], 1)
        got_a, got_b = send_half(rest_a, *order_a[1]), send_half(rest_b, *order_b[1])
    else:
        sum_out = send_sum(mixed[:, :model_width], grad_attn)
        grad_mixed = jnp.pad(grad_mixed, [(0, 0), (0, WIDE - model_width)])
    grad_own, grad_other = attend_back(
        own, other, query_places, key_places, mixed, logs, grad_mixed
    )
    grad_got = lax.ppermute(grad_other, "core", SWAP)
    if whole_rows:
        grad_own, got_a, got_b, gelu_rows, down_got_a, down_got_b = tie(
            (grad_own, got_a, got_b, gelu_rows, down_got_a, down_got_b)
        )
        rest_a, rest_b = add_half(rest_a, got_a), add_half(rest_b, got_b)
        got_a, got_b = send_half(rest_a, *order_a[2]), send_half(rest_b, *order_b[2])
        down_a = add_block(down_a, down_got_a, *order_a[2], 1)
        down_b = add_block(down_b, down_got_b, *order_b[2], 1)
        sum_down = jnp.concatenate([down_a, down_b], axis=2)
        down_got = send_block(sum_down, *order_a[3], 1)
    outputs = project(gelu_rows, down_mat, resid, down_bias[None, :])
    if whole_rows:
        grad_got, outputs = tie((grad_got, outputs))
    grad_qkv_rows = add_received(grad_own, grad_got)
    rows_now = grad_qkv_rows
    if whole_rows:
        qkv_cut = (3 * WIDE // 256) * 128
        rows_a, rows_b = grad_qkv_rows[:, :qkv_cut], grad_qkv_rows[:, qkv_cut:]
        qkv_got_a = give_first(one_a, rows_a, order_a)
        qkv_got_b = give_first(one_b, rows_b, order_b)
        qkv_a = keep_first(one_a, rows_a, qkv_got_a)
        qkv_b = keep_first(one_b, rows_b, qkv_got_b)
        rows_now, qkv_a, qkv_b, got_a, got_b, down_got = tie(
            (rows_now, qkv_a, qkv_b, got_a, got_b, down_got)
        )
        sum_down = add_block(sum_down, down_got, *order_a[3], 1)
        rest = jnp.concatenate([add_half(rest_a, got_a), add_half(rest_b, got_b)], axis=1)
        qkv_got_a = send_half(qkv_a, *order_a[1])
        qkv_got_b = send_half(qkv_b, *order_b[1])
        rest_got = send_half(rest, *order_a[3])
    qkv_sums = jnp.sum(grad_qkv_rows.astype(jnp.float32), axis=0)
    early_small = jnp.concatenate(
        [
            qkv_sums[:model_width],
            qkv_sums[2 * WIDE : 2 * WIDE + model_width],
            bias_out_term,
            gain_two_term,
            bias_two_term,
            up_bias_term,
            down_bias_term,
        ]
    )
    grad_input, gain_one_term, bias_one_term = input_grad(
        rows_now, grad_mat, spread, low_inputs, gain_one[None, :], grad_resid
    )
    if whole_rows:
        (
            grad_input,
            gain_one_term,
            bias_one_term,
            early_small,
            qkv_got_a,
            qkv_got_b,
            rest_got,
        ) = tie(
            (
                grad_input,
                gain_one_term,
                bias_one_term,
                early_small,
                qkv_got_a,
                qkv_got_b,
                rest_got,
            )
        )
        qkv_a, qkv_b = add_half(qkv_a, qkv_got_a), add_half(qkv_b, qkv_got_b)
        qkv_got_a = send_half(qkv_a, *order_a[2])
        qkv_got_b = send_half(qkv_b, *order_b[2])
        rest = add_half(rest, rest_got)
        rest_got = send_half(rest, *order_a[4])
        for step in order_a[4:]:
            sum_down = add_block(sum_down, send_block(sum_down, *step, 1), *step, 1)
    small_grad = jnp.concatenate([gain_one_term[0], bias_one_term[0], early_small])
    small_grad = round_low(small_grad)
    if whole_rows:
        outputs, sum_down, qkv_got_a, qkv_got_b, rest_got = tie(
            (outputs, sum_down, qkv_got_a, qkv_got_b, rest_got)
        )
    result_got = trade_out(outputs)
    if whole_rows:
        qkv_a, qkv_b = add_half(qkv_a, qkv_got_a), add_half(qkv_b, qkv_got_b)
        sum_qkv = jnp.concatenate([qkv_a, qkv_b], axis=1)
        sum_got = send_half(sum_qkv, *order_a[3])
        rest = add_half(rest, rest_got)
        for step in order_a[5:]:
            rest = halve(rest, *step)
        small_grad = small_grad.reshape(owners, small_len)
        sum_got, result_got, small_grad = tie((sum_got, result_got, small_grad))
        sum_qkv = add_half(sum_qkv, sum_got)
        for step in order_a[4:]:
            sum_qkv = halve(sum_qkv, *step)
        small_parts = lax.all_to_all(small_grad, ALL, 0, 0, tiled=True)
        grad_small = jnp.sum(small_parts.astype(jnp.float32), axis=0)
        sides = [up_cut, up_cut + out_cut, FF + out_cut]
        sum_up = jnp.concatenate([rest[:, : sides[0]], rest[:, sides[1] : sides[2]]], axis=1)
        sum_out = jnp.concatenate([rest[:, sides[0] : sides[1]], rest[:, sides[2] :]], axis=1)
        grad_qkv = pick_blocks(sum_qkv, model_width)
    else:
        sum_qkv = send_sum(act_one, pick_blocks(grad_qkv_rows, model_width), small_grad)
        grad_qkv, grad_small = sum_qkv[:, :qkv_width], sum_qkv[:, qkv_width:]
    result = trade_join(outputs, result_got)
    grad_tokens = trade_join(grad_input, trade_out(grad_input))
    if not whole_rows:
        sum_down = jnp.concatenate([down_a, down_b], axis=2)
    grad_small = grad_small.astype(jnp.float32).reshape(-1)[:small_len]
    grad_qkv, grad_out, grad_up, grad_down = [
        piece.astype(jnp.float32).reshape(-1) for piece in (grad_qkv, sum_out, sum_up, sum_down)
    ]
    return (result, grad_tokens, grad_qkv, grad_out, grad_up, grad_down, grad_small)


def solution(mesh):
    groups, owners = mesh.shape["dp"], mesh.shape["ctx"]
    fine = Mesh(mesh.devices.reshape(groups, owners // 2, 2), ("dp", "y", "core"))
    rows = P("dp", ("y", "core"), None)
    flat = P(("dp", "y", "core"))
    return jax.shard_map(
        local,
        mesh=fine,
        in_specs=(rows, P("dp", None), flat, flat, flat, flat, flat, rows),
        out_specs=(rows, rows, flat, flat, flat, flat, flat),
        check_vma=False,
    )
```

```python
import jax
import jax.numpy as jnp
from jax import lax
from jax.experimental import pallas as pl
from jax.experimental.pallas import tpu as pltpu
from jax.sharding import Mesh, PartitionSpec as P

HEADS = 17
HEAD_DIM = 64
FF = 4352
LANES = 8
WIDE = 1152
SWAP = ((0, 1), (1, 0))
OWNERS = ("dp", "y")


def layer_stats(values):
    center = values - jnp.mean(values, axis=-1, keepdims=True)
    inverse = lax.rsqrt(jnp.mean(center * center, axis=-1, keepdims=True) + 1e-05)
    return (center * inverse, inverse)


def norm_back(upstream, normed, inverse, gain_vector):
    scaled = upstream * gain_vector
    return inverse * (
        scaled
        - jnp.mean(scaled, axis=-1, keepdims=True)
        - normed * jnp.mean(scaled * normed, axis=-1, keepdims=True)
    )


def lead_dot(left_side, right_side):
    return lax.dot_general(
        left_side, right_side, (((0,), (0,)), ((), ())), preferred_element_type=jnp.float32
    )


def tail_dot(left_side, right_side):
    return lax.dot_general(
        left_side, right_side, (((1,), (1,)), ((), ())), preferred_element_type=jnp.float32
    )


def gate_and_slope(values):
    rate = (2.0 / jnp.pi) ** 0.5
    square = values * values
    bend = jnp.tanh(rate * values * (1.0 + 0.044715 * square))
    share = 0.5 * (1.0 + bend)
    slope = share + 0.5 * values * (1.0 - bend * bend) * rate * (1.0 + 0.134145 * square)
    return values * share, slope


def pack_small(values, width):
    room = LANES * width - values.shape[-1]
    padded = jnp.pad(values, [(0, 0)] * (values.ndim - 1) + [(0, room)])
    return padded.reshape(values.shape[:-1] + (LANES, width))


def gather_packed(block, core):
    own = lax.all_gather(block, OWNERS, axis=0, tiled=True)
    other = lax.ppermute(own, "core", SWAP)
    even = jnp.where(core == 0, own, other)
    odd = jnp.where(core == 0, other, own)
    shape = (-1, 1, LANES, block.shape[1])
    return jnp.concatenate([even.reshape(shape), odd.reshape(shape)], axis=1)


def scatter_packed(packed, core):
    even, odd = packed[:, 0], packed[:, 1]
    keep = jnp.where(core == 0, even, odd)
    give = jnp.where(core == 0, odd, even)
    got = lax.ppermute(give, "core", SWAP)
    pair = (keep.astype(jnp.float32) + got.astype(jnp.float32)).astype(jnp.bfloat16)
    return lax.psum_scatter(pair, OWNERS, scatter_dimension=0, tiled=True)[0]


def dot_rows(left, right):
    return lax.dot_general(
        left, right, (((1,), (0,)), ((), ())), preferred_element_type=jnp.float32
    )


def bias_of(key_places, query_places):
    return jnp.where(key_places <= query_places, 0.0, -1e30).astype(jnp.float32)


def per_pair(one_pair):
    pair = 2 * HEAD_DIM
    full = HEADS // 2

    def step(number, carry):
        one_pair(pl.multiple_of(number * pair, pair), 2 * number, 2)
        return carry

    lax.fori_loop(0, full, step, 0)
    if HEADS % 2:
        one_pair(full * pair, 2 * full, 1)


def lanes_at(start, block):
    return pl.ds(block * WIDE + start, 2 * HEAD_DIM)


def stand(parts):
    if len(parts) == 1:
        parts = parts + [jnp.zeros_like(parts[0])]
    return jnp.concatenate(parts, axis=0).T


def only_head(values, number, heads):
    if heads == 1:
        return values
    lane = lax.broadcasted_iota(jnp.int32, values.shape, 1)
    inside = lane < HEAD_DIM if number == 0 else lane >= HEAD_DIM
    return jnp.where(inside, values, jnp.zeros_like(values))


def join_heads(parts):
    if len(parts) == 1:
        return parts[0]
    lane = lax.broadcasted_iota(jnp.int32, parts[0].shape, 1)
    return jnp.where(lane < HEAD_DIM, parts[0], parts[1])


def attend_kernel(
    own_ref, other_ref, query_ref, key_ref, mixed_ref, log_ref, low_bias, up_bias
):
    half = own_ref.shape[0] // 2
    low_bias[...] = bias_of(key_ref[: 2 * half], query_ref[:, :half])
    up_bias[...] = bias_of(key_ref[2 * half :], query_ref[:, half:])

    def one_pair(start, first, heads):
        q = own_ref[:, lanes_at(start, 0)] * jnp.asarray(HEAD_DIM**-0.5, jnp.bfloat16)
        k_own, v_own = own_ref[:, lanes_at(start, 1)], own_ref[:, lanes_at(start, 2)]
        k_other, v_other = other_ref[:, lanes_at(start, 0)], other_ref[:, lanes_at(start, 1)]
        k_low = jnp.concatenate([k_own[:half], k_other[:half]], axis=0)
        k_up = jnp.concatenate([k_own[half:], k_other[half:]], axis=0)
        v_low = jnp.concatenate([v_own[:half], v_other[:half]], axis=0).T
        v_up = jnp.concatenate([v_own[half:], v_other[half:]], axis=0).T
        low_parts, up_parts = [], []
        for number in range(heads):
            rows = slice(number * HEAD_DIM, (number + 1) * HEAD_DIM)
            q_head = only_head(q, number, heads)
            s = tail_dot(k_low, q_head[:half]) + low_bias[...]
            top = jnp.max(s, axis=0, keepdims=True)
            e = jnp.exp(s - top)
            total = jnp.sum(e, axis=0, keepdims=True)
            mixed = dot_rows(v_low[rows], e.astype(jnp.bfloat16)) / total
            low_parts.append(mixed)
            log_ref[pl.ds(first + number, 1), :half] = top + jnp.log(total)
            s_low = tail_dot(k_low, q_head[half:])
            s_up = tail_dot(k_up, q_head[half:]) + up_bias[...]
            top = jnp.maximum(
                jnp.max(s_low, axis=0, keepdims=True), jnp.max(s_up, axis=0, keepdims=True)
            )
            e_low = jnp.exp(s_low - top)
            e_up = jnp.exp(s_up - top)
            total = jnp.sum(e_low, axis=0, keepdims=True) + jnp.sum(e_up, axis=0, keepdims=True)
            mixed = dot_rows(v_low[rows], e_low.astype(jnp.bfloat16))
            mixed = mixed + dot_rows(v_up[rows], e_up.astype(jnp.bfloat16))
            up_parts.append(mixed / total)
            log_ref[pl.ds(first + number, 1), half:] = top + jnp.log(total)
        mixed_ref[:half, lanes_at(start, 0)] = stand(low_parts).astype(jnp.bfloat16)
        mixed_ref[half:, lanes_at(start, 0)] = stand(up_parts).astype(jnp.bfloat16)

    per_pair(one_pair)


def attend_back_kernel(
    own_ref,
    other_ref,
    query_ref,
    key_ref,
    mixed_ref,
    log_ref,
    grad_ref,
    own_out,
    other_out,
    low_bias,
    up_bias,
):
    half = own_ref.shape[0] // 2
    factor = HEAD_DIM**-0.5
    low_bias[...] = bias_of(key_ref[: 2 * half], query_ref[:, :half])
    up_bias[...] = bias_of(key_ref[2 * half :], query_ref[:, half:])

    def one_pair(start, first, heads):
        lanes = lanes_at(start, 0)
        q = own_ref[:, lanes] * jnp.asarray(factor, jnp.bfloat16)
        grad = grad_ref[:, lanes]
        product = (grad.astype(jnp.float32) * mixed_ref[:, lanes].astype(jnp.float32)).T
        q_heads = [only_head(q, number, heads) for number in range(heads)]
        grad_heads = [only_head(grad, number, heads) for number in range(heads)]
        deltas = [
            jnp.sum(product[number * HEAD_DIM : (number + 1) * HEAD_DIM], axis=0, keepdims=True)
            for number in range(heads)
        ]
        logs = [log_ref[pl.ds(first + number, 1), :] for number in range(heads)]
        dq_low = [None] * heads
        dq_up = [None] * heads
        for source, out, place, block in (
            (own_ref, own_out, 0, 1),
            (other_ref, other_out, 1, 0),
        ):
            klanes, vlanes = lanes_at(start, block), lanes_at(start, block + 1)
            bias_rows = slice(place * half, (place + 1) * half)
            for upper in (False, True):
                rows = slice(half, None) if upper else slice(0, half)
                k = source[rows, klanes]
                v = source[rows, vlanes]
                k_turned = k.T
                dk_parts, dv_parts = [], []
                for number in range(heads):
                    head_rows = slice(number * HEAD_DIM, (number + 1) * HEAD_DIM)
                    first_query = half if upper else 0
                    q_head = q_heads[number][first_query:]
                    grad_head = grad_heads[number][first_query:]
                    s = tail_dot(k, q_head)
                    if upper:
                        s = s + up_bias[bias_rows]
                    else:
                        s = jnp.concatenate([s[:, :half] + low_bias[bias_rows], s[:, half:]], axis=1)
                    p = jnp.exp(s - logs[number][:, first_query:])
                    dp = tail_dot(v, grad_head)
                    ds = (p * (dp - deltas[number][:, first_query:])).astype(jnp.bfloat16)
                    dv_parts.append(dot_rows(p.astype(jnp.bfloat16), grad[first_query:]))
                    dk_parts.append(dot_rows(ds, q[first_query:]))
                    turned = dot_rows(k_turned[head_rows], ds)
                    low = None if upper else turned[:, :half]
                    up = turned if upper else turned[:, half:]
                    if low is not None:
                        dq_low[number] = low if dq_low[number] is None else dq_low[number] + low
                    dq_up[number] = up if dq_up[number] is None else dq_up[number] + up
                out[rows, klanes] = join_heads(dk_parts).astype(jnp.bfloat16)
                out[rows, vlanes] = join_heads(dv_parts).astype(jnp.bfloat16)
        own_out[:half, lanes] = (stand(dq_low) * factor).astype(jnp.bfloat16)
        own_out[half:, lanes] = (stand(dq_up) * factor).astype(jnp.bfloat16)

    per_pair(one_pair)


def add_kernel(own_ref, got_ref, out_ref):
    total = own_ref[...].astype(jnp.float32) + got_ref[...].astype(jnp.float32)
    out_ref[...] = total.astype(out_ref.dtype)


def add_received(own, got):
    rows = own.shape[0]
    block = (rows, WIDE)
    return pl.pallas_call(
        add_kernel,
        grid=(2,),
        in_specs=[
            pl.BlockSpec(block, lambda i: (0, i + 1)),
            pl.BlockSpec(block, lambda i: (0, i)),
        ],
        out_specs=pl.BlockSpec(block, lambda i: (0, i + 1)),
        out_shape=jax.ShapeDtypeStruct(own.shape, own.dtype),
        input_output_aliases={0: 0},
        compiler_params=pltpu.CompilerParams(vmem_limit_bytes=32 * 1024 * 1024),
        cost_estimate=pl.CostEstimate(flops=1 << 20, bytes_accessed=7 << 20, transcendentals=0),
    )(own, got)


def kernel_call(body, outs, half, cost):
    return pl.pallas_call(
        body,
        out_shape=outs,
        scratch_shapes=[pltpu.VMEM((2 * half, half), jnp.float32)] * 2,
        compiler_params=pltpu.CompilerParams(vmem_limit_bytes=48 * 1024 * 1024),
        cost_estimate=pl.CostEstimate(flops=cost, bytes_accessed=12 << 20, transcendentals=cost // 256),
    )


def outer_kernel(left_ref, right_ref, first_ref, second_ref):
    part = lead_dot(left_ref[...], right_ref[...]).astype(first_ref.dtype)
    cut = first_ref.shape[1]
    first_ref[...] = part[:, :cut]
    second_ref[...] = part[:, cut:]


def outer(left, right):
    rows, count = left.shape
    width = right.shape[1]
    step = 256
    cut = (width // 256) * 128
    return pl.pallas_call(
        outer_kernel,
        grid=(count // step,),
        in_specs=[
            pl.BlockSpec((rows, step), lambda i: (0, i)),
            pl.BlockSpec((rows, width), lambda i: (0, 0)),
        ],
        out_specs=[
            pl.BlockSpec((step, cut), lambda i: (i, 0)),
            pl.BlockSpec((step, width - cut), lambda i: (i, 0)),
        ],
        out_shape=[
            jax.ShapeDtypeStruct((count, cut), jnp.bfloat16),
            jax.ShapeDtypeStruct((count, width - cut), jnp.bfloat16),
        ],
        compiler_params=pltpu.CompilerParams(vmem_limit_bytes=32 * 1024 * 1024),
        cost_estimate=pl.CostEstimate(
            flops=2 * rows * count * width, bytes_accessed=16 << 20, transcendentals=0
        ),
    )(left, right)


def input_grad_kernel(
    rows_ref,
    mat_ref,
    spread_ref,
    input_ref,
    gain_ref,
    resid_ref,
    out_ref,
    gain_out,
    bias_out,
    total,
):
    step = pl.program_id(0)
    part = tail_dot(rows_ref[...], mat_ref[...])

    @pl.when(step == 0)
    def _():
        total[...] = part

    @pl.when(step > 0)
    def _():
        total[...] += part

    @pl.when(step == pl.num_programs(0) - 1)
    def _():
        back = tail_dot(total[...].astype(jnp.bfloat16), spread_ref[...])
        normed, inverse = layer_stats(input_ref[...].astype(jnp.float32))
        gain_out[...] = jnp.sum(back * normed, axis=0, keepdims=True)
        bias_out[...] = jnp.sum(back, axis=0, keepdims=True)
        grad = resid_ref[...] + norm_back(back, normed, inverse, gain_ref[...])
        out_ref[...] = grad.astype(out_ref.dtype)


def input_grad(rows, mat, spread, inputs, gain, resid):
    count, width = inputs.shape
    held = mat.shape[0]
    step = 384

    def fixed(shape):
        return pl.BlockSpec(shape, lambda i: (0, 0))

    return pl.pallas_call(
        input_grad_kernel,
        grid=(3 * WIDE // step,),
        in_specs=[
            pl.BlockSpec((count, step), lambda i: (0, i)),
            pl.BlockSpec((held, step), lambda i: (0, i)),
            fixed((width, held)),
            fixed((count, width)),
            fixed((1, width)),
            fixed((count, width)),
        ],
        out_specs=[fixed((count, width)), fixed((1, width)), fixed((1, width))],
        out_shape=[
            jax.ShapeDtypeStruct((count, width), jnp.bfloat16),
            jax.ShapeDtypeStruct((1, width), jnp.float32),
            jax.ShapeDtypeStruct((1, width), jnp.float32),
        ],
        scratch_shapes=[pltpu.VMEM((count, held), jnp.float32)],
        compiler_params=pltpu.CompilerParams(vmem_limit_bytes=48 * 1024 * 1024),
        cost_estimate=pl.CostEstimate(flops=14 << 30, bytes_accessed=20 << 20, transcendentals=0),
    )(rows, mat, spread, inputs, gain, resid)


def project_kernel(left_ref, mat_ref, resid_ref, bias_ref, out_ref, total):
    step = pl.program_id(0)
    part = dot_rows(left_ref[...], mat_ref[...])

    @pl.when(step == 0)
    def _():
        total[...] = resid_ref[...] + bias_ref[...] + part

    @pl.when(step > 0)
    def _():
        total[...] += part

    @pl.when(step == pl.num_programs(0) - 1)
    def _():
        out_ref[...] = total[...].astype(out_ref.dtype)


def project(left, mat, resid, bias):
    count, depth = left.shape
    width = mat.shape[1]
    step = 256

    def fixed(shape):
        return pl.BlockSpec(shape, lambda i: (0, 0))

    return pl.pallas_call(
        project_kernel,
        grid=(depth // step,),
        in_specs=[
            pl.BlockSpec((count, step), lambda i: (0, i)),
            pl.BlockSpec((step, width), lambda i: (i, 0)),
            fixed((count, width)),
            fixed((1, width)),
        ],
        out_specs=fixed((count, width)),
        out_shape=jax.ShapeDtypeStruct((count, width), jnp.bfloat16),
        scratch_shapes=[pltpu.VMEM((count, width), jnp.float32)],
        compiler_params=pltpu.CompilerParams(vmem_limit_bytes=32 * 1024 * 1024),
        cost_estimate=pl.CostEstimate(flops=14 << 30, bytes_accessed=20 << 20, transcendentals=0),
    )(left, mat, resid, bias)


def attend(own, other, query_places, key_places):
    rows = own.shape[0]
    outs = (
        jax.ShapeDtypeStruct((rows, WIDE), jnp.bfloat16),
        jax.ShapeDtypeStruct((HEADS, rows), jnp.float32),
    )
    call = kernel_call(attend_kernel, outs, rows // 2, 20 << 30)
    return call(own, other, query_places, key_places)


def attend_back(own, other, query_places, key_places, mixed, logs, grad):
    outs = (
        jax.ShapeDtypeStruct(own.shape, jnp.bfloat16),
        jax.ShapeDtypeStruct(other.shape, jnp.bfloat16),
    )
    call = kernel_call(attend_back_kernel, outs, own.shape[0] // 2, 30 << 30)
    return call(own, other, query_places, key_places, mixed, logs, grad)


ALL = ("dp", "y", "core")


def round_low(values):
    return values.astype(jnp.bfloat16)


def one_hot_columns(targets, width):
    line = lax.broadcasted_iota(jnp.int32, (width, targets.shape[0]), 0)
    return (line == targets[None, :]).astype(jnp.bfloat16)


def swap_with(values, axis, bit):
    count = lax.axis_size(axis)
    return lax.ppermute(values, axis, [(here, here ^ (1 << bit)) for here in range(count)])


def near_owners(order, dp_bits, each):
    owner = (lax.axis_index("dp") * 2 + lax.axis_index("y")) * 2 + lax.axis_index("core")
    bits = dp_bits + 2
    column = jnp.arange(each << bits, dtype=jnp.int32)
    place, inner = column // each, column % each
    far = jnp.zeros_like(place)
    for number, (axis, bit) in enumerate(order):
        weight = {"core": 0, "y": 1, "dp": 2 + bit}[axis]
        far = far + (((place >> (bits - 1 - number)) & 1) << weight)
    return (owner ^ far) * each + inner


def give_first(left, right, order):
    half = left.shape[1] // 2
    return swap_with(round_low(lead_dot(left[:, half:], right)), *order[0])


def keep_first(left, right, got):
    half = left.shape[1] // 2
    kept = round_low(lead_dot(left[:, :half], right))
    return round_low(kept.astype(jnp.float32) + got.astype(jnp.float32))


def pick_half(values, axis, bit, other):
    here = (lax.axis_index(axis) >> bit) & 1
    return lax.dynamic_index_in_dim(values, here ^ other, 1, keepdims=False)


def pair_up(values, low):
    lead, rest = values.shape[0], values.shape[1:]
    return values.reshape((lead // (2 * low), 2, low) + rest)


def send_block(values, axis, bit, low):
    return swap_with(pick_half(pair_up(values, low), axis, bit, 1), axis, bit)


def add_block(values, got, axis, bit, low):
    kept = pick_half(pair_up(values, low), axis, bit, 0)
    total = round_low(kept.astype(jnp.float32) + got.astype(jnp.float32))
    return total.reshape((-1,) + values.shape[1:])


def double(values, axis, bit):
    return jnp.concatenate([values, swap_with(values, axis, bit)], axis=0)


tie = lax.optimization_barrier


def send_half(values, axis, bit):
    return swap_with(values[values.shape[0] // 2 :], axis, bit)


def add_half(values, got):
    half = values.shape[0] // 2
    return round_low(values[:half].astype(jnp.float32) + got.astype(jnp.float32))


def halve(values, axis, bit):
    return add_half(values, send_half(values, axis, bit))


def spread_blocks(values, width):
    spare = jnp.zeros((values.shape[0], WIDE - width), values.dtype)
    parts = []
    for number in range(3):
        parts += [values[:, number * width : (number + 1) * width], spare]
    return jnp.concatenate(parts, axis=1)


def pick_blocks(values, width):
    return jnp.concatenate(
        [values[:, number * WIDE : number * WIDE + width] for number in range(3)], axis=1
    )


def local(tokens, positions, w_qkv, w_out, w_up, w_down, small_params, cotangent):
    seqs_here, local_len, model_width = tokens.shape
    span = local_len // 2
    rows = seqs_here * local_len
    half = rows // 2
    y = lax.axis_index("y")
    core = lax.axis_index("core")
    groups = lax.axis_size("dp")
    owners = groups * 4
    small_len = small_params.shape[0]
    whole_rows = model_width % owners == 0
    each = model_width // owners
    dp_bits = groups.bit_length() - 1

    def trade(values):
        mine = lax.dynamic_index_in_dim(values, y, 0, keepdims=False)
        give = lax.dynamic_index_in_dim(values, 1 - y, 0, keepdims=False)
        got = lax.ppermute(give, "y", SWAP)
        return jnp.concatenate([mine[:span], got[:span], mine[span:], got[span:]], axis=0)

    def trade_out(values):
        return lax.ppermute(
            jnp.concatenate([values[span:half], values[half + span :]], axis=0), "y", SWAP
        )

    def trade_join(values, got):
        mine = jnp.concatenate([values[:span], values[half : half + span]], axis=0)
        first = jnp.where(y == 0, mine, got)
        second = jnp.where(y == 0, got, mine)
        return jnp.stack([first, second])

    place_row = lax.dynamic_index_in_dim(positions, y, 0, keepdims=False)

    def places_of(core_index):
        near = lax.dynamic_slice_in_dim(place_row, (2 * y + core_index) * local_len, local_len)
        far = lax.dynamic_slice_in_dim(place_row, (2 - 2 * y + core_index) * local_len, local_len)
        return jnp.concatenate([near[:span], far[:span]]), jnp.concatenate([near[span:], far[span:]])

    own_low, own_up = places_of(core)
    other_low, other_up = places_of(1 - core)
    query_places = jnp.concatenate([own_low, own_up])[None, :]
    key_places = jnp.concatenate([own_low, other_low, own_up, other_up])[:, None]

    inputs = trade(tokens)
    grad_rows = trade(cotangent)
    if whole_rows:
        steps = [("dp", bit) for bit in range(dp_bits)]
        order_a = [("core", 0), steps[0], ("y", 0)] + steps[1:]
        order_b = [("core", 0), ("y", 0), steps[0]] + steps[1:]
        near_a = near_owners(order_a, dp_bits, each)
        near_b = near_owners(order_b, dp_bits, each)
        turn_a = one_hot_columns(near_a, model_width)
        turn_b = one_hot_columns(near_b, model_width)
        head_a = one_hot_columns(near_a, WIDE)
        head_b = one_hot_columns(near_b, WIDE)
        room = -(each + 1) % 8
        held = each + 1 + room
        column = jnp.arange(owners * held, dtype=jnp.int32)
        inside = column % held
        spread = jnp.where(inside < each, column // held * each + inside, -1)
        head_spread = one_hot_columns(spread, WIDE)
        spread = one_hot_columns(spread, model_width)
        blocks = jnp.concatenate(
            [
                spread_blocks(w_qkv.reshape(each, 3 * model_width), model_width),
                w_out.reshape(each, model_width),
            ],
            axis=1,
        )
        extra = jnp.pad(
            small_params.reshape(1, -1), [(0, room), (0, blocks.shape[1] - small_len)]
        )
        blocks = jnp.concatenate([blocks, extra], axis=0)
        blocks = lax.all_gather(blocks, ALL, axis=0, tiled=True)
        down_mat = lax.all_gather(w_down.reshape(-1, model_width), ALL, axis=0, tiled=True)
        up_part = w_up.reshape(each, FF)
        for step in order_a[:2:-1]:
            up_part = double(up_part, *step)
        up_cut = FF // 2
        up_a, up_b = up_part[:, :up_cut], up_part[:, up_cut:]
        more_a, more_b = swap_with(up_a, *order_a[2]), swap_with(up_b, *order_b[2])
        (
            blocks,
            up_a,
            up_b,
            more_a,
            more_b,
            inputs,
            grad_rows,
            query_places,
            key_places,
            turn_a,
            turn_b,
            spread,
        ) = tie(
            (
                blocks,
                up_a,
                up_b,
                more_a,
                more_b,
                inputs,
                grad_rows,
                query_places,
                key_places,
                turn_a,
                turn_b,
                spread,
            )
        )
        head_a, head_b, head_spread = tie((head_a, head_b, head_spread))
        up_a = jnp.concatenate([up_a, more_a], axis=0)
        up_b = jnp.concatenate([up_b, more_b], axis=0)
        more_a, more_b = swap_with(up_a, *order_a[1]), swap_with(up_b, *order_b[1])
        grad_mat = blocks
        qkv_mat = blocks[:, : 3 * WIDE]
        out_mat = blocks[:, 3 * WIDE :]
        packed = blocks.reshape(owners, held, -1)[:, each, :small_len].reshape(-1)

        def widen(values):
            return round_low(dot_rows(values, spread))

        def turned(values, first, second):
            return round_low(dot_rows(values, first)), round_low(dot_rows(values, second))

    else:
        small_width = -(-small_len // LANES)
        qkv_width = w_qkv.shape[0] // LANES
        blocks = jnp.concatenate(
            [w_qkv.reshape(LANES, qkv_width), pack_small(small_params, small_width)], axis=1
        )
        blocks = gather_packed(blocks, core)
        qkv_mat = blocks[..., :qkv_width].reshape(model_width, 3 * model_width)
        qkv_mat = spread_blocks(qkv_mat, model_width)
        grad_mat = qkv_mat
        packed = blocks[..., qkv_width:].reshape(owners, -1)[:, :small_len].reshape(-1)
        out_mat = gather_packed(w_out.reshape(LANES, -1), core).reshape(model_width, model_width)
        up_mat = gather_packed(w_up.reshape(LANES, -1), core).reshape(model_width, FF)
        down_mat = gather_packed(w_down.reshape(LANES, -1), core).reshape(FF, model_width)

        spread = one_hot_columns(jnp.arange(model_width, dtype=jnp.int32), model_width)

        def widen(values):
            return values

        def send_sum(left, right, extra=None):
            grad = round_low(lead_dot(left, right)).reshape(groups * 2, 2, LANES, -1)
            if extra is not None:
                extra = extra.reshape(groups * 2, 2, small_len)
                grad = jnp.concatenate([grad, pack_small(extra, small_width)], axis=-1)
            return scatter_packed(grad, core)

    packed = packed.astype(jnp.float32)
    pieces = [packed[number * model_width : (number + 1) * model_width] for number in range(7)]
    gain_one, bias_one, bias_query, bias_value, bias_out, gain_two, bias_two = pieces
    up_bias = packed[7 * model_width : 7 * model_width + FF]
    down_bias = packed[7 * model_width + FF :]

    low_inputs = inputs
    inputs = inputs.astype(jnp.float32)
    normed_one, inverse_one = layer_stats(inputs)
    act_one = round_low(normed_one * gain_one + bias_one)
    qkv_bias = jnp.concatenate([bias_query, jnp.zeros_like(bias_query), bias_value])
    qkv_bias = spread_blocks(qkv_bias[None, :], model_width)
    own = round_low(dot_rows(widen(act_one), qkv_mat) + qkv_bias)
    other = lax.ppermute(own[:, WIDE:], "core", SWAP)
    if whole_rows:
        one_a, one_b = turned(act_one, turn_a, turn_b)
        other, one_a, one_b, more_a, more_b = tie((other, one_a, one_b, more_a, more_b))
        up_a = jnp.concatenate([up_a, more_a], axis=0)
        up_b = jnp.concatenate([up_b, more_b], axis=0)
        more_a, more_b = swap_with(up_a, *order_a[0]), swap_with(up_b, *order_b[0])
    mixed, logs = attend(own, other, query_places, key_places)
    if whole_rows:
        mixed, more_a, more_b = tie((mixed, more_a, more_b))
        up_a = jnp.concatenate([up_a, more_a], axis=0)
        up_b = jnp.concatenate([up_b, more_b], axis=0)
        spread_mixed = round_low(dot_rows(mixed, head_spread))
    else:
        spread_mixed = mixed[:, :model_width]
    resid = inputs + dot_rows(spread_mixed, out_mat) + bias_out
    normed_two, inverse_two = layer_stats(resid)
    act_two = round_low(normed_two * gain_two + bias_two)
    if whole_rows:
        two_a, two_b = turned(act_two, turn_a, turn_b)
        gelu_a, slope_a = gate_and_slope(dot_rows(two_a, up_a) + up_bias[:up_cut])
        gelu_b, slope_b = gate_and_slope(dot_rows(two_b, up_b) + up_bias[up_cut:])
        slopes = [round_low(slope_a), round_low(slope_b)]
        gelu_rows = jnp.concatenate([round_low(gelu_a), round_low(gelu_b)], axis=1)
    else:
        gelu_rows, slope = gate_and_slope(dot_rows(act_two, up_mat) + up_bias)
        slopes = [round_low(slope)]
        gelu_rows = round_low(gelu_rows)
    down_parts = outer(gelu_rows, grad_rows)
    gelu_rows, down_parts, slopes = tie((gelu_rows, down_parts, slopes))
    down_a, down_b = [part.reshape(owners, -1, part.shape[1]) for part in down_parts]
    if whole_rows:
        down_got_a = send_block(down_a, "core", 0, 1)
        down_got_b = send_block(down_b, "core", 0, 1)
    else:
        down_a, down_b = [
            lax.psum_scatter(part, ALL, scatter_dimension=0, tiled=True)
            for part in (down_a, down_b)
        ]

    grad_float = grad_rows.astype(jnp.float32)
    down_bias_term = jnp.sum(grad_float, axis=0)
    wide = FF // len(slopes)
    grad_pre = [
        round_low(
            tail_dot(grad_rows, down_mat[number * wide : (number + 1) * wide])
            * slope.astype(jnp.float32)
        )
        for number, slope in enumerate(slopes)
    ]
    up_bias_term = jnp.concatenate(
        [jnp.sum(part.astype(jnp.float32), axis=0) for part in grad_pre]
    )
    if whole_rows:
        pre_a, pre_b = grad_pre
        got_a = give_first(two_a, pre_a, order_a)
        got_b = give_first(two_b, pre_b, order_b)
        back_a, back_b = tail_dot(pre_a, up_a), tail_dot(pre_b, up_b)
        back_a, back_b, got_a, got_b, down_got_a, down_got_b = tie(
            (back_a, back_b, got_a, got_b, down_got_a, down_got_b)
        )
        down_a = add_block(down_a, down_got_a, "core", 0, 1)
        down_b = add_block(down_b, down_got_b, "core", 0, 1)
        down_got_a = send_block(down_a, *order_a[1], 2)
        down_got_b = send_block(down_b, *order_b[1], 1)
        sum_a = keep_first(two_a, pre_a, got_a)
        sum_b = keep_first(two_b, pre_b, got_b)
        back_a, back_b, sum_a, sum_b = tie((back_a, back_b, sum_a, sum_b))
        grad_act_two = tail_dot(round_low(back_a), turn_a) + tail_dot(round_low(back_b), turn_b)
    else:
        sum_up = send_sum(act_two, grad_pre[0])
        grad_act_two = tail_dot(grad_pre[0], up_mat)
    gain_two_term = jnp.sum(grad_act_two * normed_two, axis=0)
    bias_two_term = jnp.sum(grad_act_two, axis=0)
    grad_resid = grad_float + norm_back(grad_act_two, normed_two, inverse_two, gain_two)
    grad_attn = round_low(grad_resid)
    bias_out_term = jnp.sum(grad_attn.astype(jnp.float32), axis=0)
    grad_mixed = round_low(tail_dot(grad_attn, out_mat))
    if whole_rows:
        out_cut = (model_width // 256) * 128
        mixed_a, mixed_b = turned(mixed, head_a, head_b)
        out_got_a = give_first(mixed_a, grad_attn[:, :out_cut], order_a)
        out_got_b = give_first(mixed_b, grad_attn[:, out_cut:], order_b)
        grad_mixed = round_low(tail_dot(grad_mixed, head_spread))
        out_a = keep_first(mixed_a, grad_attn[:, :out_cut], out_got_a)
        out_b = keep_first(mixed_b, grad_attn[:, out_cut:], out_got_b)
        rest_a = jnp.concatenate([sum_a, out_a], axis=1)
        rest_b = jnp.concatenate([sum_b, out_b], axis=1)
        grad_mixed, rest_a, rest_b = tie((grad_mixed, rest_a, rest_b))
        got_a, got_b = send_half(rest_a, *order_a[1]), send_half(rest_b, *order_b[1])
    else:
        sum_out = send_sum(mixed[:, :model_width], grad_attn)
        grad_mixed = jnp.pad(grad_mixed, [(0, 0), (0, WIDE - model_width)])
    early_small = jnp.concatenate(
        [bias_out_term, gain_two_term, bias_two_term, up_bias_term, down_bias_term]
    )
    grad_own, grad_other = attend_back(
        own, other, query_places, key_places, mixed, logs, grad_mixed
    )
    grad_got = lax.ppermute(grad_other, "core", SWAP)
    if whole_rows:
        grad_own, gelu_rows, early_small, got_a, got_b, down_got_a, down_got_b = tie(
            (grad_own, gelu_rows, early_small, got_a, got_b, down_got_a, down_got_b)
        )
        rest_a, rest_b = add_half(rest_a, got_a), add_half(rest_b, got_b)
        got_a, got_b = send_half(rest_a, *order_a[2]), send_half(rest_b, *order_b[2])
        down_a = add_block(down_a, down_got_a, *order_a[1], 2)
        down_b = add_block(down_b, down_got_b, *order_b[1], 1)
        down_got_a = send_block(down_a, *order_a[2], 1)
        down_got_b = send_block(down_b, *order_b[2], 1)
    outputs = project(gelu_rows, down_mat, resid, down_bias[None, :])
    if whole_rows:
        grad_got, outputs = tie((grad_got, outputs))
    grad_qkv_rows = add_received(grad_own, grad_got)
    rows_now = grad_qkv_rows
    if whole_rows:
        qkv_cut = (3 * WIDE // 256) * 128
        rows_a, rows_b = grad_qkv_rows[:, :qkv_cut], grad_qkv_rows[:, qkv_cut:]
        qkv_got_a = give_first(one_a, rows_a, order_a)
        qkv_got_b = give_first(one_b, rows_b, order_b)
        qkv_a = keep_first(one_a, rows_a, qkv_got_a)
        qkv_b = keep_first(one_b, rows_b, qkv_got_b)
        rows_now, qkv_a, qkv_b, got_a, got_b, down_got_a, down_got_b = tie(
            (rows_now, qkv_a, qkv_b, got_a, got_b, down_got_a, down_got_b)
        )
        down_a = add_block(down_a, down_got_a, *order_a[2], 1)
        down_b = add_block(down_b, down_got_b, *order_b[2], 1)
        sum_down = jnp.concatenate([down_a, down_b], axis=2)
        down_got = send_block(sum_down, *order_a[3], 1)
        rest = jnp.concatenate([add_half(rest_a, got_a), add_half(rest_b, got_b)], axis=1)
        qkv_got_a = send_half(qkv_a, *order_a[1])
        qkv_got_b = send_half(qkv_b, *order_b[1])
        rest_got = send_half(rest, *order_a[3])
    qkv_sums = jnp.sum(rows_now.astype(jnp.float32), axis=0)
    grad_input, gain_one_term, bias_one_term = input_grad(
        rows_now, grad_mat, spread, low_inputs, gain_one[None, :], grad_resid
    )
    if whole_rows:
        (
            grad_input,
            gain_one_term,
            bias_one_term,
            qkv_sums,
            qkv_got_a,
            qkv_got_b,
            rest_got,
            down_got,
        ) = tie(
            (
                grad_input,
                gain_one_term,
                bias_one_term,
                qkv_sums,
                qkv_got_a,
                qkv_got_b,
                rest_got,
                down_got,
            )
        )
        qkv_a, qkv_b = add_half(qkv_a, qkv_got_a), add_half(qkv_b, qkv_got_b)
        qkv_got_a = send_half(qkv_a, *order_a[2])
        qkv_got_b = send_half(qkv_b, *order_b[2])
        rest = add_half(rest, rest_got)
        rest_got = send_half(rest, *order_a[4])
        sum_down = add_block(sum_down, down_got, *order_a[3], 1)
        for step in order_a[4:]:
            sum_down = add_block(sum_down, send_block(sum_down, *step, 1), *step, 1)
    small_grad = jnp.concatenate(
        [
            gain_one_term[0],
            bias_one_term[0],
            qkv_sums[:model_width],
            qkv_sums[2 * WIDE : 2 * WIDE + model_width],
            early_small,
        ]
    )
    small_grad = round_low(small_grad)
    if whole_rows:
        outputs, sum_down, qkv_got_a, qkv_got_b, rest_got = tie(
            (outputs, sum_down, qkv_got_a, qkv_got_b, rest_got)
        )
    result_got = trade_out(outputs)
    if whole_rows:
        qkv_a, qkv_b = add_half(qkv_a, qkv_got_a), add_half(qkv_b, qkv_got_b)
        sum_qkv = jnp.concatenate([qkv_a, qkv_b], axis=1)
        sum_got = send_half(sum_qkv, *order_a[3])
        rest = add_half(rest, rest_got)
        for step in order_a[5:]:
            rest = halve(rest, *step)
        small_grad = small_grad.reshape(owners, small_len)
        sum_got, result_got, small_grad = tie((sum_got, result_got, small_grad))
        sum_qkv = add_half(sum_qkv, sum_got)
        for step in order_a[4:]:
            sum_qkv = halve(sum_qkv, *step)
        small_parts = lax.all_to_all(small_grad, ALL, 0, 0, tiled=True)
        grad_small = jnp.sum(small_parts.astype(jnp.float32), axis=0)
        sides = [up_cut, up_cut + out_cut, FF + out_cut]
        sum_up = jnp.concatenate([rest[:, : sides[0]], rest[:, sides[1] : sides[2]]], axis=1)
        sum_out = jnp.concatenate([rest[:, sides[0] : sides[1]], rest[:, sides[2] :]], axis=1)
        grad_qkv = pick_blocks(sum_qkv, model_width)
    else:
        sum_qkv = send_sum(act_one, pick_blocks(grad_qkv_rows, model_width), small_grad)
        grad_qkv, grad_small = sum_qkv[:, :qkv_width], sum_qkv[:, qkv_width:]
    result = trade_join(outputs, result_got)
    grad_tokens = trade_join(grad_input, trade_out(grad_input))
    if not whole_rows:
        sum_down = jnp.concatenate([down_a, down_b], axis=2)
    grad_small = grad_small.astype(jnp.float32).reshape(-1)[:small_len]
    grad_qkv, grad_out, grad_up, grad_down = [
        piece.astype(jnp.float32).reshape(-1) for piece in (grad_qkv, sum_out, sum_up, sum_down)
    ]
    return (result, grad_tokens, grad_qkv, grad_out, grad_up, grad_down, grad_small)


def solution(mesh):
    groups, owners = mesh.shape["dp"], mesh.shape["ctx"]
    fine = Mesh(mesh.devices.reshape(groups, owners // 2, 2), ("dp", "y", "core"))
    rows = P("dp", ("y", "core"), None)
    flat = P(("dp", "y", "core"))
    return jax.shard_map(
        local,
        mesh=fine,
        in_specs=(rows, P("dp", None), flat, flat, flat, flat, flat, rows),
        out_specs=(rows, rows, flat, flat, flat, flat, flat),
        check_vma=False,
    )
```

```python
import jax
import jax.numpy as jnp
from jax import lax
from jax.experimental import pallas as pl
from jax.experimental.pallas import tpu as pltpu
from jax.sharding import Mesh, PartitionSpec as P

HEADS = 17
HEAD_DIM = 64
FF = 4352
LANES = 8
WIDE = 1152
SWAP = ((0, 1), (1, 0))
OWNERS = ("dp", "y")


def layer_stats(values):
    center = values - jnp.mean(values, axis=-1, keepdims=True)
    inverse = lax.rsqrt(jnp.mean(center * center, axis=-1, keepdims=True) + 1e-05)
    return (center * inverse, inverse)


def norm_back(upstream, normed, inverse, gain_vector):
    scaled = upstream * gain_vector
    return inverse * (
        scaled
        - jnp.mean(scaled, axis=-1, keepdims=True)
        - normed * jnp.mean(scaled * normed, axis=-1, keepdims=True)
    )


def lead_dot(left_side, right_side):
    return lax.dot_general(
        left_side, right_side, (((0,), (0,)), ((), ())), preferred_element_type=jnp.float32
    )


def tail_dot(left_side, right_side):
    return lax.dot_general(
        left_side, right_side, (((1,), (1,)), ((), ())), preferred_element_type=jnp.float32
    )


def gate_and_slope(values):
    rate = (2.0 / jnp.pi) ** 0.5
    square = values * values
    bend = jnp.tanh(rate * values * (1.0 + 0.044715 * square))
    share = 0.5 * (1.0 + bend)
    slope = share + 0.5 * values * (1.0 - bend * bend) * rate * (1.0 + 0.134145 * square)
    return values * share, slope


def pack_small(values, width):
    room = LANES * width - values.shape[-1]
    padded = jnp.pad(values, [(0, 0)] * (values.ndim - 1) + [(0, room)])
    return padded.reshape(values.shape[:-1] + (LANES, width))


def gather_packed(block, core):
    own = lax.all_gather(block, OWNERS, axis=0, tiled=True)
    other = lax.ppermute(own, "core", SWAP)
    even = jnp.where(core == 0, own, other)
    odd = jnp.where(core == 0, other, own)
    shape = (-1, 1, LANES, block.shape[1])
    return jnp.concatenate([even.reshape(shape), odd.reshape(shape)], axis=1)


def scatter_packed(packed, core):
    even, odd = packed[:, 0], packed[:, 1]
    keep = jnp.where(core == 0, even, odd)
    give = jnp.where(core == 0, odd, even)
    got = lax.ppermute(give, "core", SWAP)
    pair = (keep.astype(jnp.float32) + got.astype(jnp.float32)).astype(jnp.bfloat16)
    return lax.psum_scatter(pair, OWNERS, scatter_dimension=0, tiled=True)[0]


def dot_rows(left, right):
    return lax.dot_general(
        left, right, (((1,), (0,)), ((), ())), preferred_element_type=jnp.float32
    )


def bias_of(key_places, query_places):
    return jnp.where(key_places <= query_places, 0.0, -1e30).astype(jnp.float32)


def per_pair(one_pair):
    pair = 2 * HEAD_DIM
    full = HEADS // 2

    def step(number, carry):
        one_pair(pl.multiple_of(number * pair, pair), 2 * number, 2)
        return carry

    lax.fori_loop(0, full, step, 0)
    if HEADS % 2:
        one_pair(full * pair, 2 * full, 1)


def lanes_at(start, block):
    return pl.ds(block * WIDE + start, 2 * HEAD_DIM)


def stand(parts):
    if len(parts) == 1:
        parts = parts + [jnp.zeros_like(parts[0])]
    return jnp.concatenate(parts, axis=0).T


def only_head(values, number, heads):
    if heads == 1:
        return values
    lane = lax.broadcasted_iota(jnp.int32, values.shape, 1)
    inside = lane < HEAD_DIM if number == 0 else lane >= HEAD_DIM
    return jnp.where(inside, values, jnp.zeros_like(values))


def join_heads(parts):
    if len(parts) == 1:
        return parts[0]
    lane = lax.broadcasted_iota(jnp.int32, parts[0].shape, 1)
    return jnp.where(lane < HEAD_DIM, parts[0], parts[1])


def attend_kernel(
    own_ref, other_ref, query_ref, key_ref, mixed_ref, log_ref, low_bias, up_bias
):
    half = own_ref.shape[0] // 2
    low_bias[...] = bias_of(key_ref[: 2 * half], query_ref[:, :half])
    up_bias[...] = bias_of(key_ref[2 * half :], query_ref[:, half:])

    def one_pair(start, first, heads):
        q = own_ref[:, lanes_at(start, 0)] * jnp.asarray(HEAD_DIM**-0.5, jnp.bfloat16)
        k_own, v_own = own_ref[:, lanes_at(start, 1)], own_ref[:, lanes_at(start, 2)]
        k_other, v_other = other_ref[:, lanes_at(start, 0)], other_ref[:, lanes_at(start, 1)]
        k_low = jnp.concatenate([k_own[:half], k_other[:half]], axis=0)
        k_up = jnp.concatenate([k_own[half:], k_other[half:]], axis=0)
        v_low = jnp.concatenate([v_own[:half], v_other[:half]], axis=0).T
        v_up = jnp.concatenate([v_own[half:], v_other[half:]], axis=0).T
        low_parts, up_parts = [], []
        for number in range(heads):
            rows = slice(number * HEAD_DIM, (number + 1) * HEAD_DIM)
            q_head = only_head(q, number, heads)
            s = tail_dot(k_low, q_head[:half]) + low_bias[...]
            top = jnp.max(s, axis=0, keepdims=True)
            e = jnp.exp(s - top)
            total = jnp.sum(e, axis=0, keepdims=True)
            mixed = dot_rows(v_low[rows], e.astype(jnp.bfloat16)) / total
            low_parts.append(mixed)
            log_ref[pl.ds(first + number, 1), :half] = top + jnp.log(total)
            s_low = tail_dot(k_low, q_head[half:])
            s_up = tail_dot(k_up, q_head[half:]) + up_bias[...]
            top = jnp.maximum(
                jnp.max(s_low, axis=0, keepdims=True), jnp.max(s_up, axis=0, keepdims=True)
            )
            e_low = jnp.exp(s_low - top)
            e_up = jnp.exp(s_up - top)
            total = jnp.sum(e_low, axis=0, keepdims=True) + jnp.sum(e_up, axis=0, keepdims=True)
            mixed = dot_rows(v_low[rows], e_low.astype(jnp.bfloat16))
            mixed = mixed + dot_rows(v_up[rows], e_up.astype(jnp.bfloat16))
            up_parts.append(mixed / total)
            log_ref[pl.ds(first + number, 1), half:] = top + jnp.log(total)
        mixed_ref[:half, lanes_at(start, 0)] = stand(low_parts).astype(jnp.bfloat16)
        mixed_ref[half:, lanes_at(start, 0)] = stand(up_parts).astype(jnp.bfloat16)

    per_pair(one_pair)


def attend_back_kernel(
    own_ref,
    other_ref,
    query_ref,
    key_ref,
    mixed_ref,
    log_ref,
    grad_ref,
    own_out,
    other_out,
    low_bias,
    up_bias,
):
    half = own_ref.shape[0] // 2
    factor = HEAD_DIM**-0.5
    low_bias[...] = bias_of(key_ref[: 2 * half], query_ref[:, :half])
    up_bias[...] = bias_of(key_ref[2 * half :], query_ref[:, half:])

    def one_pair(start, first, heads):
        lanes = lanes_at(start, 0)
        q = own_ref[:, lanes] * jnp.asarray(factor, jnp.bfloat16)
        grad = grad_ref[:, lanes]
        product = (grad.astype(jnp.float32) * mixed_ref[:, lanes].astype(jnp.float32)).T
        q_heads = [only_head(q, number, heads) for number in range(heads)]
        grad_heads = [only_head(grad, number, heads) for number in range(heads)]
        deltas = [
            jnp.sum(product[number * HEAD_DIM : (number + 1) * HEAD_DIM], axis=0, keepdims=True)
            for number in range(heads)
        ]
        logs = [log_ref[pl.ds(first + number, 1), :] for number in range(heads)]
        dq_low = [None] * heads
        dq_up = [None] * heads
        for source, out, place, block in (
            (own_ref, own_out, 0, 1),
            (other_ref, other_out, 1, 0),
        ):
            klanes, vlanes = lanes_at(start, block), lanes_at(start, block + 1)
            bias_rows = slice(place * half, (place + 1) * half)
            for upper in (False, True):
                rows = slice(half, None) if upper else slice(0, half)
                k = source[rows, klanes]
                v = source[rows, vlanes]
                k_turned = k.T
                dk_parts, dv_parts = [], []
                for number in range(heads):
                    head_rows = slice(number * HEAD_DIM, (number + 1) * HEAD_DIM)
                    first_query = half if upper else 0
                    q_head = q_heads[number][first_query:]
                    grad_head = grad_heads[number][first_query:]
                    s = tail_dot(k, q_head)
                    if upper:
                        s = s + up_bias[bias_rows]
                    else:
                        s = jnp.concatenate([s[:, :half] + low_bias[bias_rows], s[:, half:]], axis=1)
                    p = jnp.exp(s - logs[number][:, first_query:])
                    dp = tail_dot(v, grad_head)
                    ds = (p * (dp - deltas[number][:, first_query:])).astype(jnp.bfloat16)
                    dv_parts.append(dot_rows(p.astype(jnp.bfloat16), grad[first_query:]))
                    dk_parts.append(dot_rows(ds, q[first_query:]))
                    turned = dot_rows(k_turned[head_rows], ds)
                    low = None if upper else turned[:, :half]
                    up = turned if upper else turned[:, half:]
                    if low is not None:
                        dq_low[number] = low if dq_low[number] is None else dq_low[number] + low
                    dq_up[number] = up if dq_up[number] is None else dq_up[number] + up
                out[rows, klanes] = join_heads(dk_parts).astype(jnp.bfloat16)
                out[rows, vlanes] = join_heads(dv_parts).astype(jnp.bfloat16)
        own_out[:half, lanes] = (stand(dq_low) * factor).astype(jnp.bfloat16)
        own_out[half:, lanes] = (stand(dq_up) * factor).astype(jnp.bfloat16)

    per_pair(one_pair)


def add_kernel(own_ref, got_ref, out_ref):
    total = own_ref[...].astype(jnp.float32) + got_ref[...].astype(jnp.float32)
    out_ref[...] = total.astype(out_ref.dtype)


def add_received(own, got):
    rows = own.shape[0]
    block = (rows, WIDE)
    return pl.pallas_call(
        add_kernel,
        grid=(2,),
        in_specs=[
            pl.BlockSpec(block, lambda i: (0, i + 1)),
            pl.BlockSpec(block, lambda i: (0, i)),
        ],
        out_specs=pl.BlockSpec(block, lambda i: (0, i + 1)),
        out_shape=jax.ShapeDtypeStruct(own.shape, own.dtype),
        input_output_aliases={0: 0},
        compiler_params=pltpu.CompilerParams(vmem_limit_bytes=32 * 1024 * 1024),
        cost_estimate=pl.CostEstimate(flops=1 << 20, bytes_accessed=7 << 20, transcendentals=0),
    )(own, got)


def kernel_call(body, outs, half, cost):
    return pl.pallas_call(
        body,
        out_shape=outs,
        scratch_shapes=[pltpu.VMEM((2 * half, half), jnp.float32)] * 2,
        compiler_params=pltpu.CompilerParams(vmem_limit_bytes=48 * 1024 * 1024),
        cost_estimate=pl.CostEstimate(flops=cost, bytes_accessed=12 << 20, transcendentals=cost // 256),
    )


def outer_kernel(left_ref, right_ref, out_ref):
    out_ref[...] = lead_dot(left_ref[...], right_ref[...]).astype(out_ref.dtype)


def outer(left, right):
    rows, count = left.shape
    width = right.shape[1]
    step = 256
    return pl.pallas_call(
        outer_kernel,
        grid=(count // step,),
        in_specs=[
            pl.BlockSpec((rows, step), lambda i: (0, i)),
            pl.BlockSpec((rows, width), lambda i: (0, 0)),
        ],
        out_specs=pl.BlockSpec((step, width), lambda i: (i, 0)),
        out_shape=jax.ShapeDtypeStruct((count, width), jnp.bfloat16),
        compiler_params=pltpu.CompilerParams(vmem_limit_bytes=32 * 1024 * 1024),
        cost_estimate=pl.CostEstimate(
            flops=2 * rows * count * width, bytes_accessed=16 << 20, transcendentals=0
        ),
    )(left, right)


def input_grad_kernel(
    rows_ref,
    mat_ref,
    spread_ref,
    input_ref,
    gain_ref,
    resid_ref,
    out_ref,
    gain_out,
    bias_out,
    total,
):
    step = pl.program_id(0)
    part = tail_dot(rows_ref[...], mat_ref[...])

    @pl.when(step == 0)
    def _():
        total[...] = part

    @pl.when(step > 0)
    def _():
        total[...] += part

    @pl.when(step == pl.num_programs(0) - 1)
    def _():
        back = tail_dot(total[...].astype(jnp.bfloat16), spread_ref[...])
        normed, inverse = layer_stats(input_ref[...].astype(jnp.float32))
        gain_out[...] = jnp.sum(back * normed, axis=0, keepdims=True)
        bias_out[...] = jnp.sum(back, axis=0, keepdims=True)
        grad = resid_ref[...] + norm_back(back, normed, inverse, gain_ref[...])
        out_ref[...] = grad.astype(out_ref.dtype)


def input_grad(rows, mat, spread, inputs, gain, resid):
    count, width = inputs.shape
    held = mat.shape[0]
    step = 384

    def fixed(shape):
        return pl.BlockSpec(shape, lambda i: (0, 0))

    return pl.pallas_call(
        input_grad_kernel,
        grid=(3 * WIDE // step,),
        in_specs=[
            pl.BlockSpec((count, step), lambda i: (0, i)),
            pl.BlockSpec((held, step), lambda i: (0, i)),
            fixed((width, held)),
            fixed((count, width)),
            fixed((1, width)),
            fixed((count, width)),
        ],
        out_specs=[fixed((count, width)), fixed((1, width)), fixed((1, width))],
        out_shape=[
            jax.ShapeDtypeStruct((count, width), jnp.bfloat16),
            jax.ShapeDtypeStruct((1, width), jnp.float32),
            jax.ShapeDtypeStruct((1, width), jnp.float32),
        ],
        scratch_shapes=[pltpu.VMEM((count, held), jnp.float32)],
        compiler_params=pltpu.CompilerParams(vmem_limit_bytes=48 * 1024 * 1024),
        cost_estimate=pl.CostEstimate(flops=14 << 30, bytes_accessed=20 << 20, transcendentals=0),
    )(rows, mat, spread, inputs, gain, resid)


def project_kernel(left_ref, mat_ref, resid_ref, bias_ref, out_ref, total):
    step = pl.program_id(0)
    part = dot_rows(left_ref[...], mat_ref[...])

    @pl.when(step == 0)
    def _():
        total[...] = resid_ref[...] + bias_ref[...] + part

    @pl.when(step > 0)
    def _():
        total[...] += part

    @pl.when(step == pl.num_programs(0) - 1)
    def _():
        out_ref[...] = total[...].astype(out_ref.dtype)


def project(left, mat, resid, bias):
    count, depth = left.shape
    width = mat.shape[1]
    step = 256

    def fixed(shape):
        return pl.BlockSpec(shape, lambda i: (0, 0))

    return pl.pallas_call(
        project_kernel,
        grid=(depth // step,),
        in_specs=[
            pl.BlockSpec((count, step), lambda i: (0, i)),
            pl.BlockSpec((step, width), lambda i: (i, 0)),
            fixed((count, width)),
            fixed((1, width)),
        ],
        out_specs=fixed((count, width)),
        out_shape=jax.ShapeDtypeStruct((count, width), jnp.bfloat16),
        scratch_shapes=[pltpu.VMEM((count, width), jnp.float32)],
        compiler_params=pltpu.CompilerParams(vmem_limit_bytes=32 * 1024 * 1024),
        cost_estimate=pl.CostEstimate(flops=14 << 30, bytes_accessed=20 << 20, transcendentals=0),
    )(left, mat, resid, bias)


def attend(own, other, query_places, key_places):
    rows = own.shape[0]
    outs = (
        jax.ShapeDtypeStruct((rows, WIDE), jnp.bfloat16),
        jax.ShapeDtypeStruct((HEADS, rows), jnp.float32),
    )
    call = kernel_call(attend_kernel, outs, rows // 2, 20 << 30)
    return call(own, other, query_places, key_places)


def attend_back(own, other, query_places, key_places, mixed, logs, grad):
    outs = (
        jax.ShapeDtypeStruct(own.shape, jnp.bfloat16),
        jax.ShapeDtypeStruct(other.shape, jnp.bfloat16),
    )
    call = kernel_call(attend_back_kernel, outs, own.shape[0] // 2, 30 << 30)
    return call(own, other, query_places, key_places, mixed, logs, grad)


ALL = ("dp", "y", "core")


def round_low(values):
    return values.astype(jnp.bfloat16)


def one_hot_columns(targets, width):
    line = lax.broadcasted_iota(jnp.int32, (width, targets.shape[0]), 0)
    return (line == targets[None, :]).astype(jnp.bfloat16)


def swap_with(values, axis, bit):
    count = lax.axis_size(axis)
    return lax.ppermute(values, axis, [(here, here ^ (1 << bit)) for here in range(count)])


def near_owners(order, dp_bits, each):
    owner = (lax.axis_index("dp") * 2 + lax.axis_index("y")) * 2 + lax.axis_index("core")
    bits = dp_bits + 2
    column = jnp.arange(each << bits, dtype=jnp.int32)
    place, inner = column // each, column % each
    far = jnp.zeros_like(place)
    for number, (axis, bit) in enumerate(order):
        weight = {"core": 0, "y": 1, "dp": 2 + bit}[axis]
        far = far + (((place >> (bits - 1 - number)) & 1) << weight)
    return (owner ^ far) * each + inner


def give_first(left, right, order):
    half = left.shape[1] // 2
    return swap_with(round_low(lead_dot(left[:, half:], right)), *order[0])


def keep_first(left, right, got):
    half = left.shape[1] // 2
    kept = round_low(lead_dot(left[:, :half], right))
    return round_low(kept.astype(jnp.float32) + got.astype(jnp.float32))


def double(values, axis, bit):
    return jnp.concatenate([values, swap_with(values, axis, bit)], axis=0)


tie = lax.optimization_barrier


def send_half(values, axis, bit):
    return swap_with(values[values.shape[0] // 2 :], axis, bit)


def add_half(values, got):
    half = values.shape[0] // 2
    return round_low(values[:half].astype(jnp.float32) + got.astype(jnp.float32))


def halve(values, axis, bit):
    return add_half(values, send_half(values, axis, bit))


def spread_blocks(values, width):
    spare = jnp.zeros((values.shape[0], WIDE - width), values.dtype)
    parts = []
    for number in range(3):
        parts += [values[:, number * width : (number + 1) * width], spare]
    return jnp.concatenate(parts, axis=1)


def pick_blocks(values, width):
    return jnp.concatenate(
        [values[:, number * WIDE : number * WIDE + width] for number in range(3)], axis=1
    )


def local(tokens, positions, w_qkv, w_out, w_up, w_down, small_params, cotangent):
    seqs_here, local_len, model_width = tokens.shape
    span = local_len // 2
    rows = seqs_here * local_len
    half = rows // 2
    y = lax.axis_index("y")
    core = lax.axis_index("core")
    groups = lax.axis_size("dp")
    owners = groups * 4
    small_len = small_params.shape[0]
    whole_rows = model_width % owners == 0
    each = model_width // owners
    dp_bits = groups.bit_length() - 1

    def trade(values):
        mine = lax.dynamic_index_in_dim(values, y, 0, keepdims=False)
        give = lax.dynamic_index_in_dim(values, 1 - y, 0, keepdims=False)
        got = lax.ppermute(give, "y", SWAP)
        return jnp.concatenate([mine[:span], got[:span], mine[span:], got[span:]], axis=0)

    def trade_out(values):
        return lax.ppermute(
            jnp.concatenate([values[span:half], values[half + span :]], axis=0), "y", SWAP
        )

    def trade_join(values, got):
        mine = jnp.concatenate([values[:span], values[half : half + span]], axis=0)
        first = jnp.where(y == 0, mine, got)
        second = jnp.where(y == 0, got, mine)
        return jnp.stack([first, second])

    place_row = lax.dynamic_index_in_dim(positions, y, 0, keepdims=False)

    def places_of(core_index):
        near = lax.dynamic_slice_in_dim(place_row, (2 * y + core_index) * local_len, local_len)
        far = lax.dynamic_slice_in_dim(place_row, (2 - 2 * y + core_index) * local_len, local_len)
        return jnp.concatenate([near[:span], far[:span]]), jnp.concatenate([near[span:], far[span:]])

    own_low, own_up = places_of(core)
    other_low, other_up = places_of(1 - core)
    query_places = jnp.concatenate([own_low, own_up])[None, :]
    key_places = jnp.concatenate([own_low, other_low, own_up, other_up])[:, None]

    inputs = trade(tokens)
    grad_rows = trade(cotangent)
    if whole_rows:
        steps = [("dp", bit) for bit in range(dp_bits)]
        order_a = [("core", 0), steps[0], ("y", 0)] + steps[1:]
        order_b = [("core", 0), ("y", 0), steps[0]] + steps[1:]
        near_a = near_owners(order_a, dp_bits, each)
        near_b = near_owners(order_b, dp_bits, each)
        turn_a = one_hot_columns(near_a, model_width)
        turn_b = one_hot_columns(near_b, model_width)
        head_a = one_hot_columns(near_a, WIDE)
        head_b = one_hot_columns(near_b, WIDE)
        room = -(each + 1) % 8
        held = each + 1 + room
        column = jnp.arange(owners * held, dtype=jnp.int32)
        inside = column % held
        spread = jnp.where(inside < each, column // held * each + inside, -1)
        head_spread = one_hot_columns(spread, WIDE)
        spread = one_hot_columns(spread, model_width)
        blocks = jnp.concatenate(
            [
                spread_blocks(w_qkv.reshape(each, 3 * model_width), model_width),
                w_out.reshape(each, model_width),
            ],
            axis=1,
        )
        extra = jnp.pad(
            small_params.reshape(1, -1), [(0, room), (0, blocks.shape[1] - small_len)]
        )
        blocks = jnp.concatenate([blocks, extra], axis=0)
        blocks = lax.all_gather(blocks, ALL, axis=0, tiled=True)
        down_mat = lax.all_gather(w_down.reshape(-1, model_width), ALL, axis=0, tiled=True)
        up_part = w_up.reshape(each, FF)
        for step in order_a[:2:-1]:
            up_part = double(up_part, *step)
        up_cut = FF // 2
        up_a, up_b = up_part[:, :up_cut], up_part[:, up_cut:]
        more_a, more_b = swap_with(up_a, *order_a[2]), swap_with(up_b, *order_b[2])
        (
            blocks,
            up_a,
            up_b,
            more_a,
            more_b,
            inputs,
            grad_rows,
            query_places,
            key_places,
            turn_a,
            turn_b,
            spread,
        ) = tie(
            (
                blocks,
                up_a,
                up_b,
                more_a,
                more_b,
                inputs,
                grad_rows,
                query_places,
                key_places,
                turn_a,
                turn_b,
                spread,
            )
        )
        head_a, head_b, head_spread = tie((head_a, head_b, head_spread))
        up_a = jnp.concatenate([up_a, more_a], axis=0)
        up_b = jnp.concatenate([up_b, more_b], axis=0)
        more_a, more_b = swap_with(up_a, *order_a[1]), swap_with(up_b, *order_b[1])
        grad_mat = blocks
        qkv_mat = blocks[:, : 3 * WIDE]
        out_mat = blocks[:, 3 * WIDE :]
        packed = blocks.reshape(owners, held, -1)[:, each, :small_len].reshape(-1)

        def widen(values):
            return round_low(dot_rows(values, spread))

        def turned(values, first, second):
            return round_low(dot_rows(values, first)), round_low(dot_rows(values, second))

    else:
        small_width = -(-small_len // LANES)
        qkv_width = w_qkv.shape[0] // LANES
        blocks = jnp.concatenate(
            [w_qkv.reshape(LANES, qkv_width), pack_small(small_params, small_width)], axis=1
        )
        blocks = gather_packed(blocks, core)
        qkv_mat = blocks[..., :qkv_width].reshape(model_width, 3 * model_width)
        qkv_mat = spread_blocks(qkv_mat, model_width)
        grad_mat = qkv_mat
        packed = blocks[..., qkv_width:].reshape(owners, -1)[:, :small_len].reshape(-1)
        out_mat = gather_packed(w_out.reshape(LANES, -1), core).reshape(model_width, model_width)
        up_mat = gather_packed(w_up.reshape(LANES, -1), core).reshape(model_width, FF)
        down_mat = gather_packed(w_down.reshape(LANES, -1), core).reshape(FF, model_width)

        spread = one_hot_columns(jnp.arange(model_width, dtype=jnp.int32), model_width)

        def widen(values):
            return values

        def send_sum(left, right, extra=None):
            grad = round_low(lead_dot(left, right)).reshape(groups * 2, 2, LANES, -1)
            if extra is not None:
                extra = extra.reshape(groups * 2, 2, small_len)
                grad = jnp.concatenate([grad, pack_small(extra, small_width)], axis=-1)
            return scatter_packed(grad, core)

    packed = packed.astype(jnp.float32)
    pieces = [packed[number * model_width : (number + 1) * model_width] for number in range(7)]
    gain_one, bias_one, bias_query, bias_value, bias_out, gain_two, bias_two = pieces
    up_bias = packed[7 * model_width : 7 * model_width + FF]
    down_bias = packed[7 * model_width + FF :]

    low_inputs = inputs
    inputs = inputs.astype(jnp.float32)
    normed_one, inverse_one = layer_stats(inputs)
    act_one = round_low(normed_one * gain_one + bias_one)
    qkv_bias = jnp.concatenate([bias_query, jnp.zeros_like(bias_query), bias_value])
    qkv_bias = spread_blocks(qkv_bias[None, :], model_width)
    own = round_low(dot_rows(widen(act_one), qkv_mat) + qkv_bias)
    other = lax.ppermute(own[:, WIDE:], "core", SWAP)
    if whole_rows:
        one_a, one_b = turned(act_one, turn_a, turn_b)
        other, one_a, one_b = tie((other, one_a, one_b))
    mixed, logs = attend(own, other, query_places, key_places)
    if whole_rows:
        mixed, more_a, more_b = tie((mixed, more_a, more_b))
        up_a = double(jnp.concatenate([up_a, more_a], axis=0), *order_a[0])
        up_b = double(jnp.concatenate([up_b, more_b], axis=0), *order_b[0])
        spread_mixed = round_low(dot_rows(mixed, head_spread))
    else:
        spread_mixed = mixed[:, :model_width]
    resid = inputs + dot_rows(spread_mixed, out_mat) + bias_out
    normed_two, inverse_two = layer_stats(resid)
    act_two = round_low(normed_two * gain_two + bias_two)
    if whole_rows:
        two_a, two_b = turned(act_two, turn_a, turn_b)
        gelu_a, slope_a = gate_and_slope(dot_rows(two_a, up_a) + up_bias[:up_cut])
        gelu_b, slope_b = gate_and_slope(dot_rows(two_b, up_b) + up_bias[up_cut:])
        slopes = [round_low(slope_a), round_low(slope_b)]
        gelu_rows = jnp.concatenate([round_low(gelu_a), round_low(gelu_b)], axis=1)
    else:
        gelu_rows, slope = gate_and_slope(dot_rows(act_two, up_mat) + up_bias)
        slopes = [round_low(slope)]
        gelu_rows = round_low(gelu_rows)
    sum_down = outer(gelu_rows, grad_rows)
    gelu_rows, sum_down, slopes = tie((gelu_rows, sum_down, slopes))
    sum_down = sum_down.reshape(owners, -1, model_width)
    sum_down = lax.psum_scatter(sum_down, ALL, scatter_dimension=0, tiled=True)

    grad_float = grad_rows.astype(jnp.float32)
    down_bias_term = jnp.sum(grad_float, axis=0)
    wide = FF // len(slopes)
    grad_pre = [
        round_low(
            tail_dot(grad_rows, down_mat[number * wide : (number + 1) * wide])
            * slope.astype(jnp.float32)
        )
        for number, slope in enumerate(slopes)
    ]
    up_bias_term = jnp.concatenate(
        [jnp.sum(part.astype(jnp.float32), axis=0) for part in grad_pre]
    )
    if whole_rows:
        pre_a, pre_b = grad_pre
        got_a = give_first(two_a, pre_a, order_a)
        got_b = give_first(two_b, pre_b, order_b)
        back_a, back_b = tail_dot(pre_a, up_a), tail_dot(pre_b, up_b)
        back_a, back_b, got_a, got_b = tie((back_a, back_b, got_a, got_b))
        sum_a = keep_first(two_a, pre_a, got_a)
        sum_b = keep_first(two_b, pre_b, got_b)
        back_a, back_b, sum_a, sum_b = tie((back_a, back_b, sum_a, sum_b))
        grad_act_two = tail_dot(round_low(back_a), turn_a) + tail_dot(round_low(back_b), turn_b)
    else:
        sum_up = send_sum(act_two, grad_pre[0])
        grad_act_two = tail_dot(grad_pre[0], up_mat)
    gain_two_term = jnp.sum(grad_act_two * normed_two, axis=0)
    bias_two_term = jnp.sum(grad_act_two, axis=0)
    grad_resid = grad_float + norm_back(grad_act_two, normed_two, inverse_two, gain_two)
    grad_attn = round_low(grad_resid)
    bias_out_term = jnp.sum(grad_attn.astype(jnp.float32), axis=0)
    grad_mixed = round_low(tail_dot(grad_attn, out_mat))
    if whole_rows:
        out_cut = (model_width // 256) * 128
        mixed_a, mixed_b = turned(mixed, head_a, head_b)
        out_got_a = give_first(mixed_a, grad_attn[:, :out_cut], order_a)
        out_got_b = give_first(mixed_b, grad_attn[:, out_cut:], order_b)
        grad_mixed = round_low(tail_dot(grad_mixed, head_spread))
        out_a = keep_first(mixed_a, grad_attn[:, :out_cut], out_got_a)
        out_b = keep_first(mixed_b, grad_attn[:, out_cut:], out_got_b)
        rest_a = jnp.concatenate([sum_a, out_a], axis=1)
        rest_b = jnp.concatenate([sum_b, out_b], axis=1)
        grad_mixed, rest_a, rest_b = tie((grad_mixed, rest_a, rest_b))
        got_a, got_b = send_half(rest_a, *order_a[1]), send_half(rest_b, *order_b[1])
    else:
        sum_out = send_sum(mixed[:, :model_width], grad_attn)
        grad_mixed = jnp.pad(grad_mixed, [(0, 0), (0, WIDE - model_width)])
    early_small = jnp.concatenate(
        [bias_out_term, gain_two_term, bias_two_term, up_bias_term, down_bias_term]
    )
    grad_own, grad_other = attend_back(
        own, other, query_places, key_places, mixed, logs, grad_mixed
    )
    grad_got = lax.ppermute(grad_other, "core", SWAP)
    if whole_rows:
        grad_own, gelu_rows, early_small, got_a, got_b = tie(
            (grad_own, gelu_rows, early_small, got_a, got_b)
        )
        rest_a, rest_b = add_half(rest_a, got_a), add_half(rest_b, got_b)
        got_a, got_b = send_half(rest_a, *order_a[2]), send_half(rest_b, *order_b[2])
    outputs = project(gelu_rows, down_mat, resid, down_bias[None, :])
    if whole_rows:
        grad_got, outputs = tie((grad_got, outputs))
    grad_qkv_rows = add_received(grad_own, grad_got)
    rows_now = grad_qkv_rows
    if whole_rows:
        qkv_cut = (3 * WIDE // 256) * 128
        rows_a, rows_b = grad_qkv_rows[:, :qkv_cut], grad_qkv_rows[:, qkv_cut:]
        qkv_got_a = give_first(one_a, rows_a, order_a)
        qkv_got_b = give_first(one_b, rows_b, order_b)
        qkv_a = keep_first(one_a, rows_a, qkv_got_a)
        qkv_b = keep_first(one_b, rows_b, qkv_got_b)
        rows_now, qkv_a, qkv_b, got_a, got_b = tie((rows_now, qkv_a, qkv_b, got_a, got_b))
        rest = jnp.concatenate([add_half(rest_a, got_a), add_half(rest_b, got_b)], axis=1)
        qkv_got_a = send_half(qkv_a, *order_a[1])
        qkv_got_b = send_half(qkv_b, *order_b[1])
        rest_got = send_half(rest, *order_a[3])
    qkv_sums = jnp.sum(rows_now.astype(jnp.float32), axis=0)
    grad_input, gain_one_term, bias_one_term = input_grad(
        rows_now, grad_mat, spread, low_inputs, gain_one[None, :], grad_resid
    )
    if whole_rows:
        (
            grad_input,
            gain_one_term,
            bias_one_term,
            qkv_sums,
            qkv_got_a,
            qkv_got_b,
            rest_got,
        ) = tie(
            (
                grad_input,
                gain_one_term,
                bias_one_term,
                qkv_sums,
                qkv_got_a,
                qkv_got_b,
                rest_got,
            )
        )
        qkv_a, qkv_b = add_half(qkv_a, qkv_got_a), add_half(qkv_b, qkv_got_b)
        qkv_got_a = send_half(qkv_a, *order_a[2])
        qkv_got_b = send_half(qkv_b, *order_b[2])
        rest = add_half(rest, rest_got)
        rest_got = send_half(rest, *order_a[4])
    small_grad = jnp.concatenate(
        [
            gain_one_term[0],
            bias_one_term[0],
            qkv_sums[:model_width],
            qkv_sums[2 * WIDE : 2 * WIDE + model_width],
            early_small,
        ]
    )
    small_grad = round_low(small_grad)
    if whole_rows:
        outputs, qkv_got_a, qkv_got_b, rest_got = tie(
            (outputs, qkv_got_a, qkv_got_b, rest_got)
        )
    result_got = trade_out(outputs)
    if whole_rows:
        qkv_a, qkv_b = add_half(qkv_a, qkv_got_a), add_half(qkv_b, qkv_got_b)
        sum_qkv = jnp.concatenate([qkv_a, qkv_b], axis=1)
        sum_got = send_half(sum_qkv, *order_a[3])
        rest = add_half(rest, rest_got)
        for step in order_a[5:]:
            rest = halve(rest, *step)
        small_grad = small_grad.reshape(owners, small_len)
        sum_got, result_got, small_grad = tie((sum_got, result_got, small_grad))
        sum_qkv = add_half(sum_qkv, sum_got)
        for step in order_a[4:]:
            sum_qkv = halve(sum_qkv, *step)
        small_parts = lax.all_to_all(small_grad, ALL, 0, 0, tiled=True)
        grad_small = jnp.sum(small_parts.astype(jnp.float32), axis=0)
        sides = [up_cut, up_cut + out_cut, FF + out_cut]
        sum_up = jnp.concatenate([rest[:, : sides[0]], rest[:, sides[1] : sides[2]]], axis=1)
        sum_out = jnp.concatenate([rest[:, sides[0] : sides[1]], rest[:, sides[2] :]], axis=1)
        grad_qkv = pick_blocks(sum_qkv, model_width)
    else:
        sum_qkv = send_sum(act_one, pick_blocks(grad_qkv_rows, model_width), small_grad)
        grad_qkv, grad_small = sum_qkv[:, :qkv_width], sum_qkv[:, qkv_width:]
    result = trade_join(outputs, result_got)
    grad_tokens = trade_join(grad_input, trade_out(grad_input))
    grad_small = grad_small.astype(jnp.float32).reshape(-1)[:small_len]
    grad_qkv, grad_out, grad_up, grad_down = [
        piece.astype(jnp.float32).reshape(-1) for piece in (grad_qkv, sum_out, sum_up, sum_down)
    ]
    return (result, grad_tokens, grad_qkv, grad_out, grad_up, grad_down, grad_small)


def solution(mesh):
    groups, owners = mesh.shape["dp"], mesh.shape["ctx"]
    fine = Mesh(mesh.devices.reshape(groups, owners // 2, 2), ("dp", "y", "core"))
    rows = P("dp", ("y", "core"), None)
    flat = P(("dp", "y", "core"))
    return jax.shard_map(
        local,
        mesh=fine,
        in_specs=(rows, P("dp", None), flat, flat, flat, flat, flat, rows),
        out_specs=(rows, rows, flat, flat, flat, flat, flat),
        check_vma=False,
    )
```

```python
import jax
import jax.numpy as jnp
from jax import lax
from jax.experimental import pallas as pl
from jax.experimental.pallas import tpu as pltpu
from jax.sharding import Mesh, PartitionSpec as P

HEADS = 17
HEAD_DIM = 64
FF = 4352
LANES = 8
WIDE = 1152
SWAP = ((0, 1), (1, 0))
OWNERS = ("dp", "y")


def layer_stats(values):
    center = values - jnp.mean(values, axis=-1, keepdims=True)
    inverse = lax.rsqrt(jnp.mean(center * center, axis=-1, keepdims=True) + 1e-05)
    return (center * inverse, inverse)


def norm_back(upstream, normed, inverse, gain_vector):
    scaled = upstream * gain_vector
    return inverse * (
        scaled
        - jnp.mean(scaled, axis=-1, keepdims=True)
        - normed * jnp.mean(scaled * normed, axis=-1, keepdims=True)
    )


def lead_dot(left_side, right_side):
    return lax.dot_general(
        left_side, right_side, (((0,), (0,)), ((), ())), preferred_element_type=jnp.float32
    )


def tail_dot(left_side, right_side):
    return lax.dot_general(
        left_side, right_side, (((1,), (1,)), ((), ())), preferred_element_type=jnp.float32
    )


def gate_and_slope(values):
    rate = (2.0 / jnp.pi) ** 0.5
    square = values * values
    bend = jnp.tanh(rate * values * (1.0 + 0.044715 * square))
    share = 0.5 * (1.0 + bend)
    slope = share + 0.5 * values * (1.0 - bend * bend) * rate * (1.0 + 0.134145 * square)
    return values * share, slope


def pack_small(values, width):
    room = LANES * width - values.shape[-1]
    padded = jnp.pad(values, [(0, 0)] * (values.ndim - 1) + [(0, room)])
    return padded.reshape(values.shape[:-1] + (LANES, width))


def gather_packed(block, core):
    own = lax.all_gather(block, OWNERS, axis=0, tiled=True)
    other = lax.ppermute(own, "core", SWAP)
    even = jnp.where(core == 0, own, other)
    odd = jnp.where(core == 0, other, own)
    shape = (-1, 1, LANES, block.shape[1])
    return jnp.concatenate([even.reshape(shape), odd.reshape(shape)], axis=1)


def scatter_packed(packed, core):
    even, odd = packed[:, 0], packed[:, 1]
    keep = jnp.where(core == 0, even, odd)
    give = jnp.where(core == 0, odd, even)
    got = lax.ppermute(give, "core", SWAP)
    pair = (keep.astype(jnp.float32) + got.astype(jnp.float32)).astype(jnp.bfloat16)
    return lax.psum_scatter(pair, OWNERS, scatter_dimension=0, tiled=True)[0]


def dot_rows(left, right):
    return lax.dot_general(
        left, right, (((1,), (0,)), ((), ())), preferred_element_type=jnp.float32
    )


def bias_of(key_places, query_places):
    return jnp.where(key_places <= query_places, 0.0, -1e30).astype(jnp.float32)


def per_pair(one_pair):
    pair = 2 * HEAD_DIM
    full = HEADS // 2

    def step(number, carry):
        one_pair(pl.multiple_of(number * pair, pair), 2 * number, 2)
        return carry

    lax.fori_loop(0, full, step, 0)
    if HEADS % 2:
        one_pair(full * pair, 2 * full, 1)


def lanes_at(start, block):
    return pl.ds(block * WIDE + start, 2 * HEAD_DIM)


def stand(parts):
    if len(parts) == 1:
        parts = parts + [jnp.zeros_like(parts[0])]
    return jnp.concatenate(parts, axis=0).T


def only_head(values, number, heads):
    if heads == 1:
        return values
    lane = lax.broadcasted_iota(jnp.int32, values.shape, 1)
    inside = lane < HEAD_DIM if number == 0 else lane >= HEAD_DIM
    return jnp.where(inside, values, jnp.zeros_like(values))


def join_heads(parts):
    if len(parts) == 1:
        return parts[0]
    lane = lax.broadcasted_iota(jnp.int32, parts[0].shape, 1)
    return jnp.where(lane < HEAD_DIM, parts[0], parts[1])


def attend_kernel(
    own_ref, other_ref, query_ref, key_ref, mixed_ref, log_ref, low_bias, up_bias
):
    half = own_ref.shape[0] // 2
    low_bias[...] = bias_of(key_ref[: 2 * half], query_ref[:, :half])
    up_bias[...] = bias_of(key_ref[2 * half :], query_ref[:, half:])

    def one_pair(start, first, heads):
        q = own_ref[:, lanes_at(start, 0)] * jnp.asarray(HEAD_DIM**-0.5, jnp.bfloat16)
        k_own, v_own = own_ref[:, lanes_at(start, 1)], own_ref[:, lanes_at(start, 2)]
        k_other, v_other = other_ref[:, lanes_at(start, 0)], other_ref[:, lanes_at(start, 1)]
        k_low = jnp.concatenate([k_own[:half], k_other[:half]], axis=0)
        k_up = jnp.concatenate([k_own[half:], k_other[half:]], axis=0)
        v_low = jnp.concatenate([v_own[:half], v_other[:half]], axis=0).T
        v_up = jnp.concatenate([v_own[half:], v_other[half:]], axis=0).T
        low_parts, up_parts = [], []
        for number in range(heads):
            rows = slice(number * HEAD_DIM, (number + 1) * HEAD_DIM)
            q_head = only_head(q, number, heads)
            s = tail_dot(k_low, q_head[:half]) + low_bias[...]
            top = jnp.max(s, axis=0, keepdims=True)
            e = jnp.exp(s - top)
            total = jnp.sum(e, axis=0, keepdims=True)
            mixed = dot_rows(v_low[rows], e.astype(jnp.bfloat16)) / total
            low_parts.append(mixed)
            log_ref[pl.ds(first + number, 1), :half] = top + jnp.log(total)
            s_low = tail_dot(k_low, q_head[half:])
            s_up = tail_dot(k_up, q_head[half:]) + up_bias[...]
            top = jnp.maximum(
                jnp.max(s_low, axis=0, keepdims=True), jnp.max(s_up, axis=0, keepdims=True)
            )
            e_low = jnp.exp(s_low - top)
            e_up = jnp.exp(s_up - top)
            total = jnp.sum(e_low, axis=0, keepdims=True) + jnp.sum(e_up, axis=0, keepdims=True)
            mixed = dot_rows(v_low[rows], e_low.astype(jnp.bfloat16))
            mixed = mixed + dot_rows(v_up[rows], e_up.astype(jnp.bfloat16))
            up_parts.append(mixed / total)
            log_ref[pl.ds(first + number, 1), half:] = top + jnp.log(total)
        mixed_ref[:half, lanes_at(start, 0)] = stand(low_parts).astype(jnp.bfloat16)
        mixed_ref[half:, lanes_at(start, 0)] = stand(up_parts).astype(jnp.bfloat16)

    per_pair(one_pair)


def attend_back_kernel(
    own_ref,
    other_ref,
    query_ref,
    key_ref,
    mixed_ref,
    log_ref,
    grad_ref,
    own_out,
    other_out,
    low_bias,
    up_bias,
):
    half = own_ref.shape[0] // 2
    factor = HEAD_DIM**-0.5
    low_bias[...] = bias_of(key_ref[: 2 * half], query_ref[:, :half])
    up_bias[...] = bias_of(key_ref[2 * half :], query_ref[:, half:])

    def one_pair(start, first, heads):
        lanes = lanes_at(start, 0)
        q = own_ref[:, lanes] * jnp.asarray(factor, jnp.bfloat16)
        grad = grad_ref[:, lanes]
        product = (grad.astype(jnp.float32) * mixed_ref[:, lanes].astype(jnp.float32)).T
        q_heads = [only_head(q, number, heads) for number in range(heads)]
        grad_heads = [only_head(grad, number, heads) for number in range(heads)]
        deltas = [
            jnp.sum(product[number * HEAD_DIM : (number + 1) * HEAD_DIM], axis=0, keepdims=True)
            for number in range(heads)
        ]
        logs = [log_ref[pl.ds(first + number, 1), :] for number in range(heads)]
        dq_low = [None] * heads
        dq_up = [None] * heads
        for source, out, place, block in (
            (own_ref, own_out, 0, 1),
            (other_ref, other_out, 1, 0),
        ):
            klanes, vlanes = lanes_at(start, block), lanes_at(start, block + 1)
            bias_rows = slice(place * half, (place + 1) * half)
            for upper in (False, True):
                rows = slice(half, None) if upper else slice(0, half)
                k = source[rows, klanes]
                v = source[rows, vlanes]
                k_turned = k.T
                dk_parts, dv_parts = [], []
                for number in range(heads):
                    head_rows = slice(number * HEAD_DIM, (number + 1) * HEAD_DIM)
                    first_query = half if upper else 0
                    q_head = q_heads[number][first_query:]
                    grad_head = grad_heads[number][first_query:]
                    s = tail_dot(k, q_head)
                    if upper:
                        s = s + up_bias[bias_rows]
                    else:
                        s = jnp.concatenate([s[:, :half] + low_bias[bias_rows], s[:, half:]], axis=1)
                    p = jnp.exp(s - logs[number][:, first_query:])
                    dp = tail_dot(v, grad_head)
                    ds = (p * (dp - deltas[number][:, first_query:])).astype(jnp.bfloat16)
                    dv_parts.append(dot_rows(p.astype(jnp.bfloat16), grad[first_query:]))
                    dk_parts.append(dot_rows(ds, q[first_query:]))
                    turned = dot_rows(k_turned[head_rows], ds)
                    low = None if upper else turned[:, :half]
                    up = turned if upper else turned[:, half:]
                    if low is not None:
                        dq_low[number] = low if dq_low[number] is None else dq_low[number] + low
                    dq_up[number] = up if dq_up[number] is None else dq_up[number] + up
                out[rows, klanes] = join_heads(dk_parts).astype(jnp.bfloat16)
                out[rows, vlanes] = join_heads(dv_parts).astype(jnp.bfloat16)
        own_out[:half, lanes] = (stand(dq_low) * factor).astype(jnp.bfloat16)
        own_out[half:, lanes] = (stand(dq_up) * factor).astype(jnp.bfloat16)

    per_pair(one_pair)


def add_kernel(own_ref, got_ref, out_ref):
    total = own_ref[...].astype(jnp.float32) + got_ref[...].astype(jnp.float32)
    out_ref[...] = total.astype(out_ref.dtype)


def add_received(own, got):
    rows = own.shape[0]
    block = (rows, WIDE)
    return pl.pallas_call(
        add_kernel,
        grid=(2,),
        in_specs=[
            pl.BlockSpec(block, lambda i: (0, i + 1)),
            pl.BlockSpec(block, lambda i: (0, i)),
        ],
        out_specs=pl.BlockSpec(block, lambda i: (0, i + 1)),
        out_shape=jax.ShapeDtypeStruct(own.shape, own.dtype),
        input_output_aliases={0: 0},
        compiler_params=pltpu.CompilerParams(vmem_limit_bytes=32 * 1024 * 1024),
        cost_estimate=pl.CostEstimate(flops=1 << 20, bytes_accessed=7 << 20, transcendentals=0),
    )(own, got)


def kernel_call(body, outs, half, cost):
    return pl.pallas_call(
        body,
        out_shape=outs,
        scratch_shapes=[pltpu.VMEM((2 * half, half), jnp.float32)] * 2,
        compiler_params=pltpu.CompilerParams(vmem_limit_bytes=48 * 1024 * 1024),
        cost_estimate=pl.CostEstimate(flops=cost, bytes_accessed=12 << 20, transcendentals=cost // 256),
    )


def outer_kernel(left_ref, right_ref, out_ref):
    out_ref[...] = lead_dot(left_ref[...], right_ref[...]).astype(out_ref.dtype)


def outer(left, right):
    rows, count = left.shape
    width = right.shape[1]
    step = 256
    return pl.pallas_call(
        outer_kernel,
        grid=(count // step,),
        in_specs=[
            pl.BlockSpec((rows, step), lambda i: (0, i)),
            pl.BlockSpec((rows, width), lambda i: (0, 0)),
        ],
        out_specs=pl.BlockSpec((step, width), lambda i: (i, 0)),
        out_shape=jax.ShapeDtypeStruct((count, width), jnp.bfloat16),
        compiler_params=pltpu.CompilerParams(vmem_limit_bytes=32 * 1024 * 1024),
        cost_estimate=pl.CostEstimate(
            flops=2 * rows * count * width, bytes_accessed=16 << 20, transcendentals=0
        ),
    )(left, right)


def input_grad_kernel(
    rows_ref,
    mat_ref,
    spread_ref,
    input_ref,
    gain_ref,
    resid_ref,
    out_ref,
    gain_out,
    bias_out,
    total,
):
    step = pl.program_id(0)
    part = tail_dot(rows_ref[...], mat_ref[...])

    @pl.when(step == 0)
    def _():
        total[...] = part

    @pl.when(step > 0)
    def _():
        total[...] += part

    @pl.when(step == pl.num_programs(0) - 1)
    def _():
        back = tail_dot(total[...].astype(jnp.bfloat16), spread_ref[...])
        normed, inverse = layer_stats(input_ref[...].astype(jnp.float32))
        gain_out[...] = jnp.sum(back * normed, axis=0, keepdims=True)
        bias_out[...] = jnp.sum(back, axis=0, keepdims=True)
        grad = resid_ref[...] + norm_back(back, normed, inverse, gain_ref[...])
        out_ref[...] = grad.astype(out_ref.dtype)


def input_grad(rows, mat, spread, inputs, gain, resid):
    count, width = inputs.shape
    held = mat.shape[0]
    step = 384

    def fixed(shape):
        return pl.BlockSpec(shape, lambda i: (0, 0))

    return pl.pallas_call(
        input_grad_kernel,
        grid=(3 * WIDE // step,),
        in_specs=[
            pl.BlockSpec((count, step), lambda i: (0, i)),
            pl.BlockSpec((held, step), lambda i: (0, i)),
            fixed((width, held)),
            fixed((count, width)),
            fixed((1, width)),
            fixed((count, width)),
        ],
        out_specs=[fixed((count, width)), fixed((1, width)), fixed((1, width))],
        out_shape=[
            jax.ShapeDtypeStruct((count, width), jnp.bfloat16),
            jax.ShapeDtypeStruct((1, width), jnp.float32),
            jax.ShapeDtypeStruct((1, width), jnp.float32),
        ],
        scratch_shapes=[pltpu.VMEM((count, held), jnp.float32)],
        compiler_params=pltpu.CompilerParams(vmem_limit_bytes=48 * 1024 * 1024),
        cost_estimate=pl.CostEstimate(flops=14 << 30, bytes_accessed=20 << 20, transcendentals=0),
    )(rows, mat, spread, inputs, gain, resid)


def project_kernel(left_ref, mat_ref, resid_ref, bias_ref, out_ref, total):
    step = pl.program_id(0)
    part = dot_rows(left_ref[...], mat_ref[...])

    @pl.when(step == 0)
    def _():
        total[...] = resid_ref[...] + bias_ref[...] + part

    @pl.when(step > 0)
    def _():
        total[...] += part

    @pl.when(step == pl.num_programs(0) - 1)
    def _():
        out_ref[...] = total[...].astype(out_ref.dtype)


def project(left, mat, resid, bias):
    count, depth = left.shape
    width = mat.shape[1]
    step = 256

    def fixed(shape):
        return pl.BlockSpec(shape, lambda i: (0, 0))

    return pl.pallas_call(
        project_kernel,
        grid=(depth // step,),
        in_specs=[
            pl.BlockSpec((count, step), lambda i: (0, i)),
            pl.BlockSpec((step, width), lambda i: (i, 0)),
            fixed((count, width)),
            fixed((1, width)),
        ],
        out_specs=fixed((count, width)),
        out_shape=jax.ShapeDtypeStruct((count, width), jnp.bfloat16),
        scratch_shapes=[pltpu.VMEM((count, width), jnp.float32)],
        compiler_params=pltpu.CompilerParams(vmem_limit_bytes=32 * 1024 * 1024),
        cost_estimate=pl.CostEstimate(flops=14 << 30, bytes_accessed=20 << 20, transcendentals=0),
    )(left, mat, resid, bias)


def attend(own, other, query_places, key_places):
    rows = own.shape[0]
    outs = (
        jax.ShapeDtypeStruct((rows, WIDE), jnp.bfloat16),
        jax.ShapeDtypeStruct((HEADS, rows), jnp.float32),
    )
    call = kernel_call(attend_kernel, outs, rows // 2, 20 << 30)
    return call(own, other, query_places, key_places)


def attend_back(own, other, query_places, key_places, mixed, logs, grad):
    outs = (
        jax.ShapeDtypeStruct(own.shape, jnp.bfloat16),
        jax.ShapeDtypeStruct(other.shape, jnp.bfloat16),
    )
    call = kernel_call(attend_back_kernel, outs, own.shape[0] // 2, 30 << 30)
    return call(own, other, query_places, key_places, mixed, logs, grad)


ALL = ("dp", "y", "core")


def round_low(values):
    return values.astype(jnp.bfloat16)


def one_hot_columns(targets, width):
    line = lax.broadcasted_iota(jnp.int32, (width, targets.shape[0]), 0)
    return (line == targets[None, :]).astype(jnp.bfloat16)


def swap_with(values, axis, bit):
    count = lax.axis_size(axis)
    return lax.ppermute(values, axis, [(here, here ^ (1 << bit)) for here in range(count)])


def near_owners(order, dp_bits, each):
    owner = (lax.axis_index("dp") * 2 + lax.axis_index("y")) * 2 + lax.axis_index("core")
    bits = dp_bits + 2
    column = jnp.arange(each << bits, dtype=jnp.int32)
    place, inner = column // each, column % each
    far = jnp.zeros_like(place)
    for number, (axis, bit) in enumerate(order):
        weight = {"core": 0, "y": 1, "dp": 2 + bit}[axis]
        far = far + (((place >> (bits - 1 - number)) & 1) << weight)
    return (owner ^ far) * each + inner


def give_first(left, right, order):
    half = left.shape[1] // 2
    return swap_with(round_low(lead_dot(left[:, half:], right)), *order[0])


def keep_first(left, right, got):
    half = left.shape[1] // 2
    kept = round_low(lead_dot(left[:, :half], right))
    return round_low(kept.astype(jnp.float32) + got.astype(jnp.float32))


def double(values, axis, bit):
    return jnp.concatenate([values, swap_with(values, axis, bit)], axis=0)


tie = lax.optimization_barrier


def send_half(values, axis, bit):
    return swap_with(values[values.shape[0] // 2 :], axis, bit)


def add_half(values, got):
    half = values.shape[0] // 2
    return round_low(values[:half].astype(jnp.float32) + got.astype(jnp.float32))


def halve(values, axis, bit):
    return add_half(values, send_half(values, axis, bit))


def spread_blocks(values, width):
    spare = jnp.zeros((values.shape[0], WIDE - width), values.dtype)
    parts = []
    for number in range(3):
        parts += [values[:, number * width : (number + 1) * width], spare]
    return jnp.concatenate(parts, axis=1)


def pick_blocks(values, width):
    return jnp.concatenate(
        [values[:, number * WIDE : number * WIDE + width] for number in range(3)], axis=1
    )


def local(tokens, positions, w_qkv, w_out, w_up, w_down, small_params, cotangent):
    seqs_here, local_len, model_width = tokens.shape
    span = local_len // 2
    rows = seqs_here * local_len
    half = rows // 2
    y = lax.axis_index("y")
    core = lax.axis_index("core")
    groups = lax.axis_size("dp")
    owners = groups * 4
    small_len = small_params.shape[0]
    whole_rows = model_width % owners == 0
    each = model_width // owners
    dp_bits = groups.bit_length() - 1

    def trade(values):
        mine = lax.dynamic_index_in_dim(values, y, 0, keepdims=False)
        give = lax.dynamic_index_in_dim(values, 1 - y, 0, keepdims=False)
        got = lax.ppermute(give, "y", SWAP)
        return jnp.concatenate([mine[:span], got[:span], mine[span:], got[span:]], axis=0)

    def trade_out(values):
        return lax.ppermute(
            jnp.concatenate([values[span:half], values[half + span :]], axis=0), "y", SWAP
        )

    def trade_join(values, got):
        mine = jnp.concatenate([values[:span], values[half : half + span]], axis=0)
        first = jnp.where(y == 0, mine, got)
        second = jnp.where(y == 0, got, mine)
        return jnp.stack([first, second])

    place_row = lax.dynamic_index_in_dim(positions, y, 0, keepdims=False)

    def places_of(core_index):
        near = lax.dynamic_slice_in_dim(place_row, (2 * y + core_index) * local_len, local_len)
        far = lax.dynamic_slice_in_dim(place_row, (2 - 2 * y + core_index) * local_len, local_len)
        return jnp.concatenate([near[:span], far[:span]]), jnp.concatenate([near[span:], far[span:]])

    own_low, own_up = places_of(core)
    other_low, other_up = places_of(1 - core)
    query_places = jnp.concatenate([own_low, own_up])[None, :]
    key_places = jnp.concatenate([own_low, other_low, own_up, other_up])[:, None]

    inputs = trade(tokens)
    grad_rows = trade(cotangent)
    if whole_rows:
        steps = [("dp", bit) for bit in range(dp_bits)]
        order_a = [("core", 0), steps[0], ("y", 0)] + steps[1:]
        order_b = [("core", 0), ("y", 0), steps[0]] + steps[1:]
        near_a = near_owners(order_a, dp_bits, each)
        near_b = near_owners(order_b, dp_bits, each)
        turn_a = one_hot_columns(near_a, model_width)
        turn_b = one_hot_columns(near_b, model_width)
        head_a = one_hot_columns(near_a, WIDE)
        head_b = one_hot_columns(near_b, WIDE)
        room = -(each + 1) % 8
        held = each + 1 + room
        column = jnp.arange(owners * held, dtype=jnp.int32)
        inside = column % held
        spread = jnp.where(inside < each, column // held * each + inside, -1)
        head_spread = one_hot_columns(spread, WIDE)
        spread = one_hot_columns(spread, model_width)
        blocks = jnp.concatenate(
            [
                spread_blocks(w_qkv.reshape(each, 3 * model_width), model_width),
                w_out.reshape(each, model_width),
            ],
            axis=1,
        )
        extra = jnp.pad(
            small_params.reshape(1, -1), [(0, room), (0, blocks.shape[1] - small_len)]
        )
        blocks = jnp.concatenate([blocks, extra], axis=0)
        blocks = lax.all_gather(blocks, ALL, axis=0, tiled=True)
        down_mat = lax.all_gather(w_down.reshape(-1, model_width), ALL, axis=0, tiled=True)
        up_part = w_up.reshape(each, FF)
        for step in order_a[:2:-1]:
            up_part = double(up_part, *step)
        up_cut = FF // 2
        up_a, up_b = up_part[:, :up_cut], up_part[:, up_cut:]
        more_a, more_b = swap_with(up_a, *order_a[2]), swap_with(up_b, *order_b[2])
        (
            blocks,
            up_a,
            up_b,
            more_a,
            more_b,
            inputs,
            grad_rows,
            query_places,
            key_places,
            turn_a,
            turn_b,
            spread,
        ) = tie(
            (
                blocks,
                up_a,
                up_b,
                more_a,
                more_b,
                inputs,
                grad_rows,
                query_places,
                key_places,
                turn_a,
                turn_b,
                spread,
            )
        )
        head_a, head_b, head_spread = tie((head_a, head_b, head_spread))
        up_a = jnp.concatenate([up_a, more_a], axis=0)
        up_b = jnp.concatenate([up_b, more_b], axis=0)
        more_a, more_b = swap_with(up_a, *order_a[1]), swap_with(up_b, *order_b[1])
        grad_mat = blocks
        qkv_mat = blocks[:, : 3 * WIDE]
        out_mat = blocks[:, 3 * WIDE :]
        packed = blocks.reshape(owners, held, -1)[:, each, :small_len].reshape(-1)

        def widen(values):
            return round_low(dot_rows(values, spread))

        def turned(values, first, second):
            return round_low(dot_rows(values, first)), round_low(dot_rows(values, second))

    else:
        small_width = -(-small_len // LANES)
        qkv_width = w_qkv.shape[0] // LANES
        blocks = jnp.concatenate(
            [w_qkv.reshape(LANES, qkv_width), pack_small(small_params, small_width)], axis=1
        )
        blocks = gather_packed(blocks, core)
        qkv_mat = blocks[..., :qkv_width].reshape(model_width, 3 * model_width)
        qkv_mat = spread_blocks(qkv_mat, model_width)
        grad_mat = qkv_mat
        packed = blocks[..., qkv_width:].reshape(owners, -1)[:, :small_len].reshape(-1)
        out_mat = gather_packed(w_out.reshape(LANES, -1), core).reshape(model_width, model_width)
        up_mat = gather_packed(w_up.reshape(LANES, -1), core).reshape(model_width, FF)
        down_mat = gather_packed(w_down.reshape(LANES, -1), core).reshape(FF, model_width)

        spread = one_hot_columns(jnp.arange(model_width, dtype=jnp.int32), model_width)

        def widen(values):
            return values

        def send_sum(left, right, extra=None):
            grad = round_low(lead_dot(left, right)).reshape(groups * 2, 2, LANES, -1)
            if extra is not None:
                extra = extra.reshape(groups * 2, 2, small_len)
                grad = jnp.concatenate([grad, pack_small(extra, small_width)], axis=-1)
            return scatter_packed(grad, core)

    packed = packed.astype(jnp.float32)
    pieces = [packed[number * model_width : (number + 1) * model_width] for number in range(7)]
    gain_one, bias_one, bias_query, bias_value, bias_out, gain_two, bias_two = pieces
    up_bias = packed[7 * model_width : 7 * model_width + FF]
    down_bias = packed[7 * model_width + FF :]

    low_inputs = inputs
    inputs = inputs.astype(jnp.float32)
    normed_one, inverse_one = layer_stats(inputs)
    act_one = round_low(normed_one * gain_one + bias_one)
    qkv_bias = jnp.concatenate([bias_query, jnp.zeros_like(bias_query), bias_value])
    qkv_bias = spread_blocks(qkv_bias[None, :], model_width)
    own = round_low(dot_rows(widen(act_one), qkv_mat) + qkv_bias)
    other = lax.ppermute(own[:, WIDE:], "core", SWAP)
    if whole_rows:
        one_a, one_b = turned(act_one, turn_a, turn_b)
        other, one_a, one_b = tie((other, one_a, one_b))
    mixed, logs = attend(own, other, query_places, key_places)
    if whole_rows:
        mixed, more_a, more_b = tie((mixed, more_a, more_b))
        up_a = double(jnp.concatenate([up_a, more_a], axis=0), *order_a[0])
        up_b = double(jnp.concatenate([up_b, more_b], axis=0), *order_b[0])
        spread_mixed = round_low(dot_rows(mixed, head_spread))
    else:
        spread_mixed = mixed[:, :model_width]
    resid = inputs + dot_rows(spread_mixed, out_mat) + bias_out
    normed_two, inverse_two = layer_stats(resid)
    act_two = round_low(normed_two * gain_two + bias_two)
    if whole_rows:
        two_a, two_b = turned(act_two, turn_a, turn_b)
        gelu_a, slope_a = gate_and_slope(dot_rows(two_a, up_a) + up_bias[:up_cut])
        gelu_b, slope_b = gate_and_slope(dot_rows(two_b, up_b) + up_bias[up_cut:])
        slopes = [round_low(slope_a), round_low(slope_b)]
        gelu_rows = jnp.concatenate([round_low(gelu_a), round_low(gelu_b)], axis=1)
    else:
        gelu_rows, slope = gate_and_slope(dot_rows(act_two, up_mat) + up_bias)
        slopes = [round_low(slope)]
        gelu_rows = round_low(gelu_rows)
    sum_down = outer(gelu_rows, grad_rows)
    gelu_rows, sum_down, slopes = tie((gelu_rows, sum_down, slopes))
    sum_down = sum_down.reshape(owners, -1, model_width)
    sum_down = lax.psum_scatter(sum_down, ALL, scatter_dimension=0, tiled=True)

    grad_float = grad_rows.astype(jnp.float32)
    down_bias_term = jnp.sum(grad_float, axis=0)
    wide = FF // len(slopes)
    grad_pre = [
        round_low(
            tail_dot(grad_rows, down_mat[number * wide : (number + 1) * wide])
            * slope.astype(jnp.float32)
        )
        for number, slope in enumerate(slopes)
    ]
    up_bias_term = jnp.concatenate(
        [jnp.sum(part.astype(jnp.float32), axis=0) for part in grad_pre]
    )
    if whole_rows:
        pre_a, pre_b = grad_pre
        got_a = give_first(two_a, pre_a, order_a)
        got_b = give_first(two_b, pre_b, order_b)
        back_a, back_b = tail_dot(pre_a, up_a), tail_dot(pre_b, up_b)
        back_a, back_b, got_a, got_b = tie((back_a, back_b, got_a, got_b))
        sum_a = keep_first(two_a, pre_a, got_a)
        sum_b = keep_first(two_b, pre_b, got_b)
        back_a, back_b, sum_a, sum_b = tie((back_a, back_b, sum_a, sum_b))
        grad_act_two = tail_dot(round_low(back_a), turn_a) + tail_dot(round_low(back_b), turn_b)
    else:
        sum_up = send_sum(act_two, grad_pre[0])
        grad_act_two = tail_dot(grad_pre[0], up_mat)
    gain_two_term = jnp.sum(grad_act_two * normed_two, axis=0)
    bias_two_term = jnp.sum(grad_act_two, axis=0)
    grad_resid = grad_float + norm_back(grad_act_two, normed_two, inverse_two, gain_two)
    grad_attn = round_low(grad_resid)
    bias_out_term = jnp.sum(grad_attn.astype(jnp.float32), axis=0)
    grad_mixed = round_low(tail_dot(grad_attn, out_mat))
    if whole_rows:
        out_cut = (model_width // 256) * 128
        mixed_a, mixed_b = turned(mixed, head_a, head_b)
        out_got_a = give_first(mixed_a, grad_attn[:, :out_cut], order_a)
        out_got_b = give_first(mixed_b, grad_attn[:, out_cut:], order_b)
        grad_mixed = round_low(tail_dot(grad_mixed, head_spread))
        out_a = keep_first(mixed_a, grad_attn[:, :out_cut], out_got_a)
        out_b = keep_first(mixed_b, grad_attn[:, out_cut:], out_got_b)
        rest_a = jnp.concatenate([sum_a, out_a], axis=1)
        rest_b = jnp.concatenate([sum_b, out_b], axis=1)
        grad_mixed, rest_a, rest_b = tie((grad_mixed, rest_a, rest_b))
        got_a, got_b = send_half(rest_a, *order_a[1]), send_half(rest_b, *order_b[1])
    else:
        sum_out = send_sum(mixed[:, :model_width], grad_attn)
        grad_mixed = jnp.pad(grad_mixed, [(0, 0), (0, WIDE - model_width)])
    early_small = jnp.concatenate(
        [bias_out_term, gain_two_term, bias_two_term, up_bias_term, down_bias_term]
    )
    grad_own, grad_other = attend_back(
        own, other, query_places, key_places, mixed, logs, grad_mixed
    )
    grad_got = lax.ppermute(grad_other, "core", SWAP)
    if whole_rows:
        grad_own, gelu_rows, early_small, got_a, got_b = tie(
            (grad_own, gelu_rows, early_small, got_a, got_b)
        )
        rest_a, rest_b = add_half(rest_a, got_a), add_half(rest_b, got_b)
        got_a, got_b = send_half(rest_a, *order_a[2]), send_half(rest_b, *order_b[2])
    outputs = project(gelu_rows, down_mat, resid, down_bias[None, :])
    if whole_rows:
        grad_got, outputs = tie((grad_got, outputs))
    grad_qkv_rows = add_received(grad_own, grad_got)
    rows_now = grad_qkv_rows
    if whole_rows:
        qkv_cut = (3 * WIDE // 256) * 128
        rows_a, rows_b = grad_qkv_rows[:, :qkv_cut], grad_qkv_rows[:, qkv_cut:]
        qkv_got_a = give_first(one_a, rows_a, order_a)
        qkv_got_b = give_first(one_b, rows_b, order_b)
        qkv_a = keep_first(one_a, rows_a, qkv_got_a)
        qkv_b = keep_first(one_b, rows_b, qkv_got_b)
        rows_now, qkv_a, qkv_b = tie((rows_now, qkv_a, qkv_b))
        qkv_got_a = send_half(qkv_a, *order_a[1])
        qkv_got_b = send_half(qkv_b, *order_b[1])
    qkv_sums = jnp.sum(rows_now.astype(jnp.float32), axis=0)
    grad_input, gain_one_term, bias_one_term = input_grad(
        rows_now, grad_mat, spread, low_inputs, gain_one[None, :], grad_resid
    )
    if whole_rows:
        (
            grad_input,
            gain_one_term,
            bias_one_term,
            qkv_sums,
            qkv_got_a,
            qkv_got_b,
            got_a,
            got_b,
        ) = tie(
            (
                grad_input,
                gain_one_term,
                bias_one_term,
                qkv_sums,
                qkv_got_a,
                qkv_got_b,
                got_a,
                got_b,
            )
        )
        qkv_a, qkv_b = add_half(qkv_a, qkv_got_a), add_half(qkv_b, qkv_got_b)
        qkv_got_a = send_half(qkv_a, *order_a[2])
        qkv_got_b = send_half(qkv_b, *order_b[2])
        rest = jnp.concatenate([add_half(rest_a, got_a), add_half(rest_b, got_b)], axis=1)
        rest_got = send_half(rest, *order_a[3])
    small_grad = jnp.concatenate(
        [
            gain_one_term[0],
            bias_one_term[0],
            qkv_sums[:model_width],
            qkv_sums[2 * WIDE : 2 * WIDE + model_width],
            early_small,
        ]
    )
    small_grad = round_low(small_grad)
    if whole_rows:
        outputs, qkv_got_a, qkv_got_b, rest_got = tie(
            (outputs, qkv_got_a, qkv_got_b, rest_got)
        )
    result_got = trade_out(outputs)
    if whole_rows:
        qkv_a, qkv_b = add_half(qkv_a, qkv_got_a), add_half(qkv_b, qkv_got_b)
        sum_qkv = jnp.concatenate([qkv_a, qkv_b], axis=1)
        sum_got = send_half(sum_qkv, *order_a[3])
        rest = add_half(rest, rest_got)
        rest_got = send_half(rest, *order_a[4])
        small_grad = small_grad.reshape(owners, small_len)
        sum_got, result_got, small_grad, rest_got, sum_down = tie(
            (sum_got, result_got, small_grad, rest_got, sum_down)
        )
        rest = add_half(rest, rest_got)
        for step in order_a[5:]:
            rest = halve(rest, *step)
        sum_qkv = add_half(sum_qkv, sum_got)
        for step in order_a[4:]:
            sum_qkv = halve(sum_qkv, *step)
        small_parts = lax.all_to_all(small_grad, ALL, 0, 0, tiled=True)
        grad_small = jnp.sum(small_parts.astype(jnp.float32), axis=0)
        sides = [up_cut, up_cut + out_cut, FF + out_cut]
        sum_up = jnp.concatenate([rest[:, : sides[0]], rest[:, sides[1] : sides[2]]], axis=1)
        sum_out = jnp.concatenate([rest[:, sides[0] : sides[1]], rest[:, sides[2] :]], axis=1)
        grad_qkv = pick_blocks(sum_qkv, model_width)
    else:
        sum_qkv = send_sum(act_one, pick_blocks(grad_qkv_rows, model_width), small_grad)
        grad_qkv, grad_small = sum_qkv[:, :qkv_width], sum_qkv[:, qkv_width:]
    result = trade_join(outputs, result_got)
    grad_tokens = trade_join(grad_input, trade_out(grad_input))
    grad_small = grad_small.astype(jnp.float32).reshape(-1)[:small_len]
    grad_qkv, grad_out, grad_up, grad_down = [
        piece.astype(jnp.float32).reshape(-1) for piece in (grad_qkv, sum_out, sum_up, sum_down)
    ]
    return (result, grad_tokens, grad_qkv, grad_out, grad_up, grad_down, grad_small)


def solution(mesh):
    groups, owners = mesh.shape["dp"], mesh.shape["ctx"]
    fine = Mesh(mesh.devices.reshape(groups, owners // 2, 2), ("dp", "y", "core"))
    rows = P("dp", ("y", "core"), None)
    flat = P(("dp", "y", "core"))
    return jax.shard_map(
        local,
        mesh=fine,
        in_specs=(rows, P("dp", None), flat, flat, flat, flat, flat, rows),
        out_specs=(rows, rows, flat, flat, flat, flat, flat),
        check_vma=False,
    )
```
